512 devices in a mesh: gx: 32 (over x_lo, z, core), gz: 16 (over x_hi, y).
Axes of the slice: x: 4 (x_hi: 2, x_lo: 2; x = x_hi * 2 + x_lo), y: 8, z: 8, core: 2. Of those that a mesh axis runs over, the one named last changes fastest.
Arguments:
- checkpoint: float32 [26, 128, 128, 128], P(None, 'gx', 'gz'), as said below
- adjoint_end: float32 [26, 128, 128, 128], P(None, 'gx', 'gz'), may hold values from -12 to 12
- porosity: float32 [128, 128, 128], P('gx', 'gz'), may hold values from 0 to 1
- node_type: int32 [128, 128, 128], P('gx', 'gz'), may hold values from 0 to 3, as said below
- inlet_index: int32 [128, 128, 128], P('gx', 'gz'), may hold values from 0 to 1
- inlet_conc: float32 [2], replicated, may hold values from 0.5 to 2
Outputs:
- adjoint_start: float32 [26, 128, 128, 128], P(None, 'gx', 'gz')
- porosity_grad: float32 [128, 128, 128], P('gx', 'gz')
- grad_total: float32 [], replicated
The draws below stay inside these ranges and needn't reach their ends.
Inputs may be any that keep to these rules, and one draw needn't show every extreme that they name: `checkpoint`: every population is positive. `node_type`: 0 fluid, 1 solid, 2 inlet, 3 outlet.
All inputs are finite; a program needn't handle non-finite values.
Results may differ from the reference program's by a relative error of at most 0.0003.
Values sent between devices are 32-bit elements; how exact they have to be, the bound alone decides.
A program may use at most 64 MiB of HBM per device.

```python
import jax
import jax.numpy as jnp
import numpy as np
from jax import lax

CX = 4
NY = 128
NIN = 2
NX = 128
NZ = 128
N_GX = 32


def draw_tables():
    flow_vel = np.array([[0, 0, 0], [1, 0, 0], [-1, 0, 0], [0, 1, 0], [0, -1, 0], [0, 0, 1], [0, 0, -1], [1, 1, 0], [-1, -1, 0], [1, -1, 0], [-1, 1, 0], [1, 0, 1], [-1, 0, -1], [1, 0, -1], [-1, 0, 1], [0, 1, 1], [0, -1, -1], [0, 1, -1], [0, -1, 1]], dtype=np.float32)
    flow_weight = np.array([1.0 / 3.0] + [1.0 / 18.0] * 6 + [1.0 / 36.0] * 12, dtype=np.float32)
    scalar_weight = np.array([0.25] + [0.125] * 6, dtype=np.float32)
    return (flow_vel, flow_weight, scalar_weight)


def draw_checkpoint(key, part):
    key = jax.random.fold_in(key, 11)
    subkeys = jax.random.split(key, 4)
    flow_vel, flow_weight, scalar_weight = draw_tables()
    density = jax.random.uniform(subkeys[0], (NX, NZ, NY), jnp.float32, 0.8, 1.2)
    velocity = jax.random.uniform(subkeys[1], (3, NX, NZ, NY), jnp.float32, -0.08, 0.08)
    scalar_level = jnp.exp(jax.random.uniform(subkeys[2], (NX, NZ, NY), jnp.float32, np.log(0.2), np.log(2.0)))
    ripple = jax.random.uniform(subkeys[3], (26, NX, NZ, NY), jnp.float32, -0.3, 0.3)
    projected = jnp.asarray(flow_vel[:, 0]).reshape(-1, 1, 1, 1) * velocity[0] + jnp.asarray(flow_vel[:, 1]).reshape(-1, 1, 1, 1) * velocity[1] + jnp.asarray(flow_vel[:, 2]).reshape(-1, 1, 1, 1) * velocity[2]
    square = velocity[0] * velocity[0] + velocity[1] * velocity[1] + velocity[2] * velocity[2]
    flow_part = jnp.asarray(flow_weight).reshape(-1, 1, 1, 1) * density * (1.0 + 3.0 * projected + 4.5 * projected * projected - 1.5 * square) * (1.0 + ripple[:19])
    scalar_part = jnp.asarray(scalar_weight).reshape(-1, 1, 1, 1) * scalar_level * (1.0 + 4.0 * projected[:7]) * (1.0 + ripple[19:])
    return jnp.concatenate([flow_part, scalar_part], axis=0).astype(jnp.float32)


def draw_adjoint_end(key, part):
    key = jax.random.fold_in(key, 12)
    downstream = 1.0 + 2.0 * jnp.arange(NX, dtype=jnp.float32) / (NX - 1)
    signal = jnp.clip(jax.random.normal(key, (26, NX, NZ, NY), jnp.float32), -4.0, 4.0)
    return (signal * downstream.reshape(1, NX, 1, 1)).astype(jnp.float32)


def draw_node_type(key, part):
    key = jax.random.fold_in(key, 13)
    rolled_value = jax.random.randint(key, (NX, NZ, NY), 0, 20, dtype=jnp.int32)
    return jnp.where(rolled_value < 13, 0, jnp.where(rolled_value < 17, 1, jnp.where(rolled_value < 19, 2, 3))).astype(jnp.int32)


def set_ends(drawn, stream_key, smallest, top_value):
    shape = drawn.shape
    place = [jax.random.randint(jax.random.fold_in(stream_key, axis), (), 0, shape[axis]) for axis in range(len(shape))]
    drawn = drawn.at[tuple(place)].set(smallest)
    longest = shape.index(max(shape))
    place[longest] = (place[longest] + 1) % shape[longest]
    return drawn.at[tuple(place)].set(top_value)


def block_scale(key, shape, pieces, least, top_value):
    factor_of = 1.0
    for axis_at, parts in pieces:
        draws = jax.random.uniform(jax.random.fold_in(jax.random.fold_in(key, 6), axis_at), (parts,), jnp.float32, least / len(pieces), top_value / len(pieces))
        factor_of = factor_of * jnp.repeat(jnp.exp(draws), shape[axis_at] // parts).reshape((-1,) + (1,) * (len(shape) - 1 - axis_at))
    return factor_of


def setup_inputs(seed: int = 0) -> dict:
    streams_of = jax.random.split(jax.random.key(seed), 7)
    checkpoint = draw_checkpoint(jax.random.fold_in(streams_of[6], 71), 0)
    adjoint_end = draw_adjoint_end(jax.random.fold_in(streams_of[6], 71), 0)
    porosity = jnp.clip(1.0 * jax.random.uniform(streams_of[2], (NX, NZ, NY), jnp.float32) ** block_scale(streams_of[2], (NX, NZ, NY), ((0, 32), (1, 16)), -0.2, 0.2), 0.0, 1.0)
    node_type = draw_node_type(jax.random.fold_in(streams_of[6], 71), 0)
    inlet_index = set_ends(jax.random.randint(streams_of[4], (NX, NZ, NY), 0, NIN), jax.random.fold_in(streams_of[4], 1), 0, NIN - 1).astype(jnp.int32)
    inlet_conc = jnp.clip(jax.random.uniform(streams_of[5], (NIN,), jnp.float32, 0.5, 2.0), 0.5, 2.0)
    return dict(checkpoint=checkpoint, adjoint_end=adjoint_end, porosity=porosity, node_type=node_type, inlet_index=inlet_index, inlet_conc=inlet_conc)


brinkman_strength = 4.0
inlet_speed = 0.05
shear_rate = 1.25
scalar_rate = 1.0 / 0.7
velocity_list = [(0, 0, 0), (1, 0, 0), (-1, 0, 0), (0, 1, 0), (0, -1, 0), (0, 0, 1), (0, 0, -1), (1, 1, 0), (-1, -1, 0), (1, -1, 0), (-1, 1, 0), (1, 0, 1), (-1, 0, -1), (1, 0, -1), (-1, 0, 1), (0, 1, 1), (0, -1, -1), (0, 1, -1), (0, -1, 1)]

def orthogonal_relax(polys, relax_rates):
    ortho_basis = []
    for vector in polys:
        vector = [float(value) for value in vector]
        for earlier in ortho_basis:
            factor = sum((a * b for a, b in zip(vector, earlier))) / sum((b * b for b in earlier))
            vector = [a - factor * b for a, b in zip(vector, earlier)]
        ortho_basis.append(vector)
    count = len(polys)
    matrix = [[0.0] * count for index in range(count)]
    for vector, relax_rate in zip(ortho_basis, relax_rates):
        length = sum((b * b for b in vector))
        for row in range(count):
            for column in range(count):
                matrix[row][column] += relax_rate * vector[row] * vector[column] / length
    return np.array(matrix, dtype=np.float32)

def opposite_of(velocities):
    return [[other for other, second in enumerate(velocities) if all((second[k] == -first[k] for k in range(3)))][0] for first in velocities]

def flow_row(vx, vy, vz):
    sq = vx * vx + vy * vy + vz * vz
    return [1.0, sq, sq * sq, vx, vx * sq, vy, vy * sq, vz, vz * sq, 3 * vx * vx - sq, (3 * vx * vx - sq) * sq, vy * vy - vz * vz, (vy * vy - vz * vz) * sq, vx * vy, vy * vz, vx * vz, vx * (vy * vy - vz * vz), vy * (vz * vz - vx * vx), vz * (vx * vx - vy * vy)]

def scalar_row(vx, vy, vz):
    sq = vx * vx + vy * vy + vz * vz
    return [1.0, vx, vy, vz, sq, 3 * vx * vx - sq, vy * vy - vz * vz]

def lattice_tables():
    flow_vel = velocity_list
    scalar_vel = velocity_list[:7]
    flow_weight = np.array([1.0 / 3.0] + [1.0 / 18.0] * 6 + [1.0 / 36.0] * 12, dtype=np.float32)
    scalar_weight = np.array([0.25] + [0.125] * 6, dtype=np.float32)
    flow_rows = [flow_row(*velocity) for velocity in flow_vel]
    flow_polys = [[row[k] for row in flow_rows] for k in range(19)]
    flow_rates = [0.0, 1.19, 1.4, 1.0, 1.2, 1.0, 1.2, 1.0, 1.2, shear_rate, 1.4, shear_rate, 1.4, shear_rate, shear_rate, shear_rate, 1.98, 1.98, 1.98]
    scalar_rows = [scalar_row(*velocity) for velocity in scalar_vel]
    scalar_polys = [[row[k] for row in scalar_rows] for k in range(7)]
    scalar_rates = [0.0, scalar_rate, scalar_rate, scalar_rate, 1.5, 1.5, 1.5]
    lattice_vel = np.array(flow_vel + scalar_vel, dtype=np.float32)
    return (lattice_vel, flow_weight, scalar_weight, opposite_of(flow_vel), opposite_of(scalar_vel), orthogonal_relax(flow_polys, flow_rates), orthogonal_relax(scalar_polys, scalar_rates))

def spread(vector, extra_dims):
    return jnp.asarray(np.asarray(vector, dtype=np.float32)).reshape((-1,) + (1,) * extra_dims)

def equilibrium(weights, lattice_vel, density, velocity, second):
    extra_dims = density.ndim
    projected = spread(lattice_vel[:, 0], extra_dims) * velocity[0] + spread(lattice_vel[:, 1], extra_dims) * velocity[1] + spread(lattice_vel[:, 2], extra_dims) * velocity[2]
    if second:
        square = velocity[0] * velocity[0] + velocity[1] * velocity[1] + velocity[2] * velocity[2]
        return spread(weights, extra_dims) * density * (1.0 + 3.0 * projected + 4.5 * projected * projected - 1.5 * square)
    return spread(weights, extra_dims) * density * (1.0 + 4.0 * projected)

def collide(populations, porosity, node_type, inlet_level):
    lattice_vel, flow_weight, scalar_weight, flow_opp, scalar_opp, flow_relax, scalar_relax = lattice_tables()
    flow_vel = lattice_vel[:19]
    scalar_vel = lattice_vel[19:]
    extra_dims = porosity.ndim
    flow_pops = populations[:19]
    scalar_pops = populations[19:]
    density = lax.optimization_barrier(jnp.sum(flow_pops, axis=0))
    velocity = [lax.optimization_barrier(jnp.sum(spread(flow_vel[:, axis_index], extra_dims) * flow_pops, axis=0)) / density for axis_index in range(3)]
    damping = 1.0 / (1.0 + brinkman_strength * (1.0 - porosity))
    damped = [component * damping for component in velocity]
    unit_field = jnp.ones_like(porosity)
    zero_field = jnp.zeros_like(porosity)
    inflow = [inlet_speed * unit_field, zero_field, zero_field]
    offset = flow_pops - equilibrium(flow_weight, flow_vel, density, damped, True)
    fluid_flow = flow_pops - jnp.tensordot(jnp.asarray(flow_relax), offset, axes=1, precision=lax.Precision.HIGHEST)
    solid_flow = flow_pops[jnp.array(flow_opp, dtype=jnp.int32)]
    inlet_flow = equilibrium(flow_weight, flow_vel, unit_field, inflow, True)
    outlet_flow = equilibrium(flow_weight, flow_vel, density, velocity, True)
    scalar_level = lax.optimization_barrier(jnp.sum(scalar_pops, axis=0))
    scalar_offset = scalar_pops - equilibrium(scalar_weight, scalar_vel, scalar_level, damped, False)
    fluid_scalar = scalar_pops - jnp.tensordot(jnp.asarray(scalar_relax), scalar_offset, axes=1, precision=lax.Precision.HIGHEST)
    solid_scalar = scalar_pops[jnp.array(scalar_opp, dtype=jnp.int32)]
    inlet_scalar = equilibrium(scalar_weight, scalar_vel, inlet_level, inflow, False)
    outlet_scalar = equilibrium(scalar_weight, scalar_vel, scalar_level, velocity, False)
    is_solid = (node_type == 1)[None]
    is_inlet = (node_type == 2)[None]
    is_outlet = (node_type == 3)[None]
    new_flow = jnp.where(is_solid, solid_flow, jnp.where(is_inlet, inlet_flow, jnp.where(is_outlet, outlet_flow, fluid_flow)))
    new_scalar = jnp.where(is_solid, solid_scalar, jnp.where(is_inlet, inlet_scalar, jnp.where(is_outlet, outlet_scalar, fluid_scalar)))
    return jnp.concatenate([new_flow, new_scalar], axis=0)

def vjp_collide(populations, porosity, node_type, inlet_level, cotangent):

    def local_collide(pops_in, poro_in):
        return collide(pops_in, poro_in, node_type, inlet_level)
    outcome, backward = jax.vjp(local_collide, populations, porosity)
    return backward(cotangent)

def inlet_levels(inlet_index, inlet_conc):
    levels = jnp.zeros(inlet_index.shape, jnp.float32)
    for inlet_number in range(inlet_conc.shape[0]):
        levels = jnp.where(inlet_index == inlet_number, inlet_conc[inlet_number], levels)
    return levels

def stream_whole(field, heading):
    moved = []
    for channel in range(field.shape[0]):
        shift_x, shift_y, shift_z = (heading * value for value in (velocity_list + velocity_list[:7])[channel])
        moved.append(jnp.roll(field[channel], (shift_x, shift_z, shift_y), axis=(0, 1, 2)))
    return jnp.stack(moved)

def reference(checkpoint, adjoint_end, porosity, node_type, inlet_index, inlet_conc):
    levels = inlet_levels(inlet_index, inlet_conc)
    starts = jnp.arange(N_GX, dtype=jnp.int32) * CX

    def block_of(array, start, axis_dim):
        return lax.dynamic_slice_in_dim(array, start, CX, axis_dim)

    def join_pops(stacked):
        return jnp.moveaxis(stacked, 0, 1).reshape(26, NX, NZ, NY)

    def forward_block(start):
        return collide(block_of(checkpoint, start, 1), block_of(porosity, start, 0), block_of(node_type, start, 0), block_of(levels, start, 0))
    post_start = join_pops(lax.map(forward_block, starts))
    first_state = stream_whole(post_start, 1)
    carried_mid = stream_whole(adjoint_end, -1)

    def backward_maker(state, carried):

        def backward_block(start):
            return vjp_collide(block_of(state, start, 1), block_of(porosity, start, 0), block_of(node_type, start, 0), block_of(levels, start, 0), block_of(carried, start, 1))
        return backward_block
    adjoint_mid, sens_mid = lax.map(backward_maker(first_state, carried_mid), starts)
    adjoint_mid = join_pops(adjoint_mid)
    sens_mid = sens_mid.reshape(NX, NZ, NY)
    carried_start = stream_whole(adjoint_mid, -1)
    adjoint_start, sens_start = lax.map(backward_maker(checkpoint, carried_start), starts)
    adjoint_start = join_pops(adjoint_start)
    porosity_grad = sens_start.reshape(NX, NZ, NY) + sens_mid
    return (adjoint_start, porosity_grad, jnp.sum(porosity_grad))
```

```python
import jax
import jax.numpy as jnp
from jax import lax
from jax.experimental import pallas as pl
from jax.experimental.pallas import tpu as pltpu
from jax.sharding import PartitionSpec as P

MESH = pl.DeviceIdType.MESH
F32 = jnp.float32

VEL = [
    (0, 0, 0),
    (1, 0, 0),
    (-1, 0, 0),
    (0, 1, 0),
    (0, -1, 0),
    (0, 0, 1),
    (0, 0, -1),
    (1, 1, 0),
    (-1, -1, 0),
    (1, -1, 0),
    (-1, 1, 0),
    (1, 0, 1),
    (-1, 0, -1),
    (1, 0, -1),
    (-1, 0, 1),
    (0, 1, 1),
    (0, -1, -1),
    (0, 1, -1),
    (0, -1, 1),
]
VEL = VEL + VEL[:7]
CH = 26
PLANES = 4
ROWS = 8
LANES = 128

BRINKMAN = 4.0
SPEED = 0.05
RATE_H = 1.0 / 0.7
RATE_E = 1.5

E_NORM = 2394.0
FLUID_P, FLUID_Q = -0.2, -0.1
K_MEAN = 1.4 / 19.0
K_E = (1.4 - 1.19) / E_NORM
K_N = 0.15 / 18.0
K_D = 0.15 / 4.0
K_J = 0.2 / 10.0
K_Q = 0.78 / 8.0


def moments(f):
    e = [f[a] + f[a + 1] for a in range(1, 19, 2)]
    o = [f[a] - f[a + 1] for a in range(1, 19, 2)]
    sxy, txy = o[3] + o[4], o[3] - o[4]
    sxz, txz = o[5] + o[6], o[5] - o[6]
    syz, tyz = o[7] + o[8], o[7] - o[8]
    exy, dxy = e[3] + e[4], e[3] - e[4]
    exz, dxz = e[5] + e[6], e[5] - e[6]
    eyz, dyz = e[7] + e[8], e[7] - e[8]
    axis_sum = e[0] + e[1] + e[2]
    diag_sum = exy + exz + eyz
    return dict(
        e=e,
        o=o,
        f0=f[0],
        axis=axis_sum,
        diag=diag_sum,
        across=(eyz, exz, exy),
        cross=(dxy, dxz, dyz),
        j=(o[0] + sxy + sxz, o[1] + txy + syz, o[2] + txz + tyz),
        q=(sxy - sxz, syz - txy, txz - tyz),
    )


def density_velocity(m):
    r = m["f0"] + m["axis"] + m["diag"]
    inverse = 1.0 / r
    return r, inverse, [j * inverse for j in m["j"]]


def second_order(m):
    shift = m["axis"] - m["diag"]
    return [3.0 * (m["e"][a] - m["across"][a]) - shift for a in range(3)]


def assemble(even_rest, even_axis, even_diag, cross, odd_axis, odd_diag, third, pe, po, m):
    out = [even_rest]
    for a in range(3):
        even = pe * m["e"][a] + even_axis[a]
        odd = po * m["o"][a] + odd_axis[a]
        out += [even + odd, even - odd]
    x, y, z = odd_diag
    qx, qy, qz = third
    xy_x, xy_y = x + qx, y - qy
    xz_x, xz_z = x - qx, z + qz
    yz_y, yz_z = y + qy, z - qz
    odds = [xy_x + xy_y, xy_x - xy_y, xz_x + xz_z, xz_x - xz_z, yz_y + yz_z, yz_y - yz_z]
    for k in range(6):
        base = even_diag[2 - k // 2]
        base = base + cross[k // 2] if k % 2 == 0 else base - cross[k // 2]
        even = pe * m["e"][3 + k] + base
        odd = po * m["o"][3 + k] + odds[k]
        out += [even + odd, even - odd]
    return out


def cell_kinds(kind):
    return kind == 0, kind == 1, kind == 2, kind == 3


def relax_factors(kind):
    fluid, solid, _, _ = cell_kinds(kind)
    pe = jnp.where(fluid, FLUID_P, jnp.where(solid, 0.5, 0.0))
    po = jnp.where(fluid, FLUID_Q, jnp.where(solid, -0.5, 0.0))
    he = jnp.where(fluid, 0.5 - RATE_E / 2, jnp.where(solid, 0.5, 0.0))
    ho = jnp.where(fluid, 0.5 - RATE_H / 2, jnp.where(solid, -0.5, 0.0))
    return pe, po, he, ho


def damping_of(porosity):
    return 1.0 / (1.0 + BRINKMAN * (1.0 - porosity))


def dot3(a, b):
    return a[0] * b[0] + a[1] * b[1] + a[2] * b[2]


def collide(pops, porosity, kind, level):
    fluid, solid, inlet, outlet = cell_kinds(kind)
    pe, po, he, ho = relax_factors(kind)
    f, h = pops[:19], pops[19:]
    m = moments(f)
    r, _, u = density_velocity(m)
    d = damping_of(porosity)
    d_eff = jnp.where(outlet, 1.0, d)
    b = [c * d_eff for c in u]
    zero = jnp.zeros_like(r)

    def on(value):
        return jnp.where(fluid, value, 0.0)

    def pick(at_fluid, elsewhere):
        return jnp.where(fluid, at_fluid, jnp.where(solid, 0.0, elsewhere))

    re = jnp.where(inlet, 1.0, r)
    be = [
        jnp.where(inlet, SPEED, b[0]),
        jnp.where(inlet, 0.0, b[1]),
        jnp.where(inlet, 0.0, b[2]),
    ]
    rb = [re * c for c in be]
    bb = [p * c for p, c in zip(rb, be)]
    b2 = bb[0] + bb[1] + bb[2]
    crossed = (rb[0] * be[1], rb[0] * be[2], rb[1] * be[2])
    quad_rest = pick(-0.65, -0.5) * b2
    axis_all = pick(-0.09, -1.0 / 12.0) * b2
    axis_own = pick(0.325, 0.25)
    quad_axis = [axis_all + axis_own * c for c in bb]
    diag_all = pick(0.095, 1.0 / 12.0) * b2
    diag_own = pick(-0.15, -0.125)
    quad_diag = [diag_all + diag_own * c for c in bb]
    cross_own = pick(0.3125, 0.25)
    quad_cross = [cross_own * c for c in crossed]
    lin_axis_own = pick(0.18, 1.0 / 6.0)
    lin_diag_own = pick(0.08, 1.0 / 12.0)
    lin_axis = [lin_axis_own * c for c in rb]
    lin_diag = [lin_diag_own * c for c in rb]
    n = second_order(m)
    e_f = -30.0 * m["f0"] - 11.0 * m["axis"] + 8.0 * m["diag"]
    de = K_E * (e_f + 11.0 * r)
    even_rest = jnp.where(fluid, 1.4 / 3.0 * r - 30.0 * de, pick(0.0, 1.0 / 3.0) * re)
    even_axis = jnp.where(fluid, 1.4 / 18.0 * r - 11.0 * de, pick(0.0, 1.0 / 18.0) * re)
    even_diag = jnp.where(fluid, 1.4 / 36.0 * r + 8.0 * de, pick(0.0, 1.0 / 36.0) * re)
    rest_own = jnp.where(fluid, -0.4, jnp.where(solid, 1.0, 0.0))
    n_own = on(K_N)
    n = [n_own * c for c in n]
    d_own = on(K_D)
    j_own = on(K_J)
    q_own = on(-K_Q)
    jj = [j_own * c for c in m["j"]]
    new_f = assemble(
        rest_own * m["f0"] + even_rest + quad_rest,
        [even_axis + quad_axis[a] + n[a] for a in range(3)],
        [even_diag + quad_diag[a] - n[a] for a in range(3)],
        [quad_cross[k] + d_own * m["cross"][k] for k in range(3)],
        [lin_axis[a] + jj[a] for a in range(3)],
        [lin_diag[a] + jj[a] for a in range(3)],
        [q_own * c for c in m["q"]],
        pe,
        po,
        m,
    )
    kappa = on(BRINKMAN * d)
    kappa2 = kappa + kappa
    g_rest = kappa2 * quad_rest
    g_axis = [kappa2 * c for c in quad_axis]
    g_diag = [kappa2 * c for c in quad_diag]
    g_cross = [kappa2 * c for c in quad_cross]
    g_la = [kappa * c for c in lin_axis]
    g_ld = [kappa * c for c in lin_diag]
    g_f = [g_rest]
    for a in range(3):
        g_f += [g_axis[a] + g_la[a], g_axis[a] - g_la[a]]
    x, y, z = g_ld
    odds = [x + y, x - y, x + z, x - z, y + z, y - z]
    for k in range(6):
        even = g_diag[2 - k // 2]
        even = even + g_cross[k // 2] if k % 2 == 0 else even - g_cross[k // 2]
        g_f += [even + odds[k], even - odds[k]]
    he_pairs = [h[a] + h[a + 1] for a in (1, 3, 5)]
    ho_pairs = [h[a] - h[a + 1] for a in (1, 3, 5)]
    s = h[0] + he_pairs[0] + he_pairs[1] + he_pairs[2]
    se = jnp.where(inlet, level, s)
    s_even = pick(RATE_E, 1.0) * se
    s_odd = pick(0.5 * RATE_H, 0.5) * se
    new_h = [jnp.where(fluid, 1.0 - RATE_E, jnp.where(solid, 1.0, 0.0)) * h[0] + 0.25 * s_even]
    g_h = [zero]
    for a in range(3):
        even = he * he_pairs[a] + 0.125 * s_even
        push = s_odd * be[a]
        odd = ho * ho_pairs[a] + push
        new_h += [even + odd, even - odd]
        push = kappa * push
        g_h += [push, -push]
    return new_f + new_h, g_f + g_h


def weighted_factors(a, b, own):
    return (
        own[0] - a * K_MEAN + 30.0 * b * K_E,
        own[1] - a * K_MEAN + 11.0 * b * K_E,
        own[2] - a * K_MEAN - 8.0 * b * K_E,
    )


A0_F = weighted_factors(1.0, -11.0, (1.4 / 3.0, 1.4 / 18.0, 1.4 / 36.0))
A2_F = weighted_factors(1.0 / 3.0, 5.0 / 9.0, (0.0, 1.0 / 540.0, 1.4 / 36.0 - 1.0 / 540.0))


def transposed(pops, carried, porosity, kind):
    fluid, solid, inlet, outlet = cell_kinds(kind)
    pe, po, he, ho = relax_factors(kind)
    f, h = pops[:19], pops[19:]
    ms = moments(f)
    r, inverse, u = density_velocity(ms)
    s = h[0] + (h[1] + h[2]) + (h[3] + h[4]) + (h[5] + h[6])
    d = jnp.where(outlet, 1.0, damping_of(porosity))
    b = [c * d for c in u]
    ratio4 = 4.0 * s * inverse

    m = moments(carried[:19])
    mu = carried[19:]
    f0, axis, diag = m["f0"], m["axis"], m["diag"]

    def pick(at_fluid, at_outlet):
        return jnp.where(fluid, at_fluid, at_outlet)

    a0 = (
        pick(A0_F[0], 1.0 / 3.0) * f0
        + pick(A0_F[1], 1.0 / 18.0) * axis
        + pick(A0_F[2], 1.0 / 36.0) * diag
    )
    common = (
        pick(A2_F[0], 0.0) * f0 + pick(A2_F[1], 0.0) * axis + pick(A2_F[2], 1.0 / 36.0) * diag
    )
    own = pick(1.4 / 18.0 - 3.0 / 540.0, 1.0 / 18.0)
    away = pick(-1.4 / 36.0 + 3.0 / 540.0, -1.0 / 36.0)
    a2 = [own * m["e"][a] + away * m["across"][a] + common for a in range(3)]
    cross_own = pick(1.25 / 36.0, 1.0 / 36.0)
    axy, axz, ayz = [cross_own * c for c in m["cross"]]
    o_own = pick(1.0 / 30.0, 1.0 / 36.0)
    j_own = pick(0.96 / 36.0, 1.0 / 36.0)
    a1 = [o_own * m["o"][a] + j_own * m["j"][a] for a in range(3)]
    me = [mu[a] + mu[a + 1] for a in (1, 3, 5)]
    mo = [mu[a] - mu[a + 1] for a in (1, 3, 5)]
    me_sum = me[0] + me[1] + me[2]
    mean_h = (RATE_E / 7.0) * (mu[0] + me_sum)
    b0 = pick(RATE_E, 1.0) * (0.25 * mu[0] + 0.125 * me_sum) - pick(mean_h, 0.0)
    b1_own = pick(0.125 * RATE_H, 0.125)
    b1 = [b1_own * c for c in mo]

    ab = [
        a2[0] * b[0] + axy * b[1] + axz * b[2],
        axy * b[0] + a2[1] * b[1] + ayz * b[2],
        axz * b[0] + ayz * b[1] + a2[2] * b[2],
    ]
    curved = [9.0 * ab[a] - 3.0 * a0 * b[a] for a in range(3)]
    b1b = dot3(b1, b)
    total = [3.0 * a1[a] + curved[a] + ratio4 * b1[a] for a in range(3)]
    to_r = a0 - 0.5 * dot3(b, curved) - ratio4 * b1b
    to_s = b0 + 4.0 * b1b
    sens = jnp.where(fluid, BRINKMAN * d * d * dot3(ms["j"], total), 0.0)

    active = jnp.logical_or(fluid, outlet)
    d_on = jnp.where(active, d, 0.0)
    to_r = jnp.where(active, to_r, 0.0)
    to_s = jnp.where(active, to_s, 0.0)
    to_j = [d_on * c for c in total]

    def on(value):
        return jnp.where(fluid, value, 0.0)

    mean = on(K_MEAN) * (f0 + axis + diag)
    ef = on(K_E) * (-30.0 * f0 - 11.0 * axis + 8.0 * diag)
    base = to_r + mean
    n_own = on(K_N)
    n = [n_own * c for c in second_order(m)]
    d_own = on(K_D)
    jj_own = on(K_J)
    q_own = on(-K_Q)
    odd = [to_j[a] + jj_own * m["j"][a] for a in range(3)]
    rest_own = jnp.where(fluid, -0.4, jnp.where(solid, 1.0, 0.0))
    base_axis = base - 11.0 * ef
    base_diag = base + 8.0 * ef
    out_f = assemble(
        rest_own * f0 + base - 30.0 * ef,
        [base_axis + n[a] for a in range(3)],
        [base_diag - n[a] for a in range(3)],
        [d_own * c for c in m["cross"]],
        odd,
        odd,
        [q_own * c for c in m["q"]],
        pe,
        po,
        m,
    )
    to_s = to_s + on(mean_h)
    out_h = [jnp.where(fluid, 1.0 - RATE_E, jnp.where(solid, 1.0, 0.0)) * mu[0] + to_s]
    for a in range(3):
        even = he * me[a] + to_s
        odd = ho * mo[a]
        out_h += [even + odd, even - odd]
    return out_f + out_h, sens


class Stream:
    def __init__(self, heading, fields):
        self.heading = heading
        self.fields = fields
        self.vel = [tuple(heading * c for c in v) for v in VEL]
        plus = [i for i in range(CH) if self.vel[i][0] == 1]
        minus = [i for i in range(CH) if self.vel[i][0] == -1]
        still = [i for i in range(CH) if self.vel[i][0] == 0]
        order = [(k, i) for group in (plus, minus, still) for k in range(fields) for i in group]
        self.place = {key: at for at, key in enumerate(order)}
        self.face = len(plus) * fields
        self.z_place = {}
        self.edge = {}
        for sign in (1, -1):
            group = [i for i in range(CH) if self.vel[i][2] == sign]
            group.sort(key=lambda i: -abs(self.vel[i][0]))
            keys = [(k, i) for i in group for k in range(fields)]
            self.z_count = len(keys)
            for at, key in enumerate(keys):
                self.z_place[key] = (0 if sign == 1 else 1, at)
            for at, i in enumerate(group[:2]):
                self.edge[(self.vel[i][0], sign)] = at * fields

    def scratch(self):
        return [
            pltpu.VMEM((CH * self.fields, PLANES + 2, ROWS, LANES), F32),
            pltpu.VMEM((2, self.z_count, PLANES, 1, LANES), F32),
            pltpu.VMEM((2, self.z_count, PLANES + 2, 1, LANES), F32),
            pltpu.SemaphoreType.DMA((8,)),
            pltpu.SemaphoreType.DMA((8,)),
        ]

    def put(self, refs, x, field, values):
        padded, rows = refs[0], refs[1]
        for i, value in enumerate(values):
            _, vy, vz = self.vel[i]
            if vy:
                value = pltpu.roll(value, vy % LANES, 1)
            padded[self.place[(field, i)], x + 1] = value
            if vz:
                side, at = self.z_place[(field, i)]
                row = ROWS - 1 if vz == 1 else 0
                rows[side, at, x] = value[row : row + 1, :]

    def copies(self, refs, gx, gz, n_gx, n_gz):
        padded, rows, halo, send, recv = refs
        found = []
        for at, (dx, dz) in enumerate(
            ((1, 0), (-1, 0), (0, 1), (0, -1), (1, 1), (1, -1), (-1, 1), (-1, -1))
        ):
            target = (lax.rem(gx + dx + n_gx, n_gx), lax.rem(gz + dz + n_gz, n_gz))
            side = 0 if dz == 1 else 1
            if dz == 0:
                start = 0 if dx == 1 else self.face
                source = padded.at[pl.ds(start, self.face), PLANES if dx == 1 else 1]
                landing = padded.at[pl.ds(start, self.face), 0 if dx == 1 else PLANES + 1]
            elif dx == 0:
                source = rows.at[side]
                landing = halo.at[side, :, pl.ds(1, PLANES)]
            else:
                start = self.edge[(dx, dz)]
                source = rows.at[side, pl.ds(start, self.fields), PLANES - 1 if dx == 1 else 0]
                landing = halo.at[side, pl.ds(start, self.fields), 0 if dx == 1 else PLANES + 1]
            found.append(
                pltpu.make_async_remote_copy(
                    src_ref=source,
                    dst_ref=landing,
                    send_sem=send.at[at],
                    recv_sem=recv.at[at],
                    device_id=target,
                    device_id_type=MESH,
                )
            )
        return found

    def get(self, refs, x, field):
        padded, halo = refs[0], refs[2]
        row = lax.broadcasted_iota(jnp.int32, (ROWS, LANES), 0)
        values = []
        for i in range(CH):
            vx, _, vz = self.vel[i]
            value = padded[self.place[(field, i)], x + 1 - vx]
            if vz:
                side, at = self.z_place[(field, i)]
                edge = 0 if vz == 1 else ROWS - 1
                value = jnp.where(
                    row == edge, halo[side, at, x + 1 - vx], pltpu.roll(value, vz % ROWS, 0)
                )
            values.append(value)
        return values


FORWARD = Stream(1, 2)
BACKWARD = Stream(-1, 1)


def kernel(n_gx, n_gz, *refs):
    (checkpoint, adjoint_end, porosity, node_type, inlet_index, inlet_conc) = refs[:6]
    (out_ref, grad_ref, total_ref) = refs[6:9]
    (cp, ae, por, kind, feed, conc, sens, in_sem) = refs[9:17]
    forward, back_mid, back_start = refs[17:22], refs[22:27], refs[27:32]
    (mine_a, got_a, mine_b, got_b, red_send, red_recv) = refs[32:]
    gx, gz = lax.axis_index("gx"), lax.axis_index("gz")

    def gx_at(k):
        return lax.rem(gx + k, n_gx)

    def gz_at(k):
        return lax.rem(gz + k, n_gz)

    barrier = pltpu.get_barrier_semaphore()

    def greet(target):
        pl.semaphore_signal(barrier, inc=1, device_id=target, device_id_type=MESH)

    loads = [
        pltpu.make_async_copy(source, target, in_sem.at[k])
        for k, (source, target) in enumerate(
            (
                (checkpoint, cp),
                (porosity, por),
                (node_type, kind),
                (inlet_index, feed),
                (inlet_conc, conc),
                (adjoint_end, ae),
            )
        )
    ]
    for load in loads:
        load.start()

    @pl.loop(1, n_gx)
    def _(k):
        greet((gx_at(k), gz))

    @pl.loop(1, n_gz)
    def _(k):
        greet((gx, gz_at(k)))

    for dx in (1, n_gx - 1):
        for dz in (1, n_gz - 1):
            greet((gx_at(dx), gz_at(dz)))

    for load in loads[:5]:
        load.wait()

    def start_plane(x, carry):
        level = jnp.where(feed[x] == 0, conc[0], jnp.where(feed[x] == 1, conc[1], 0.0))
        post, slope = collide([cp[i, x] for i in range(CH)], por[x], kind[x], level)
        FORWARD.put(forward, x, 0, post)
        FORWARD.put(forward, x, 1, slope)
        return carry

    lax.fori_loop(0, PLANES, start_plane, 0)
    loads[5].wait()

    def end_plane(x, carry):
        BACKWARD.put(back_mid, x, 0, [ae[i, x] for i in range(CH)])
        return carry

    lax.fori_loop(0, PLANES, end_plane, 0)

    pl.semaphore_wait(barrier, n_gx + n_gz + 2)
    first = FORWARD.copies(forward, gx, gz, n_gx, n_gz)
    first += BACKWARD.copies(back_mid, gx, gz, n_gx, n_gz)
    for copy in first:
        copy.start()
    for copy in first:
        copy.wait_recv()

    def mid_plane(x, total):
        state = FORWARD.get(forward, x, 0)
        slope = FORWARD.get(forward, x, 1)
        carried = BACKWARD.get(back_mid, x, 0)
        adjoint, sens_mid = transposed(state, carried, por[x], kind[x])
        sens[x] = sens_mid
        BACKWARD.put(back_start, x, 0, adjoint)
        sums = [a * b for a, b in zip(adjoint, slope)] + [sens_mid, total]
        while len(sums) > 1:
            sums = [a + b for a, b in zip(sums[::2], sums[1::2])] + sums[len(sums) & ~1 :]
        return sums[0]

    total = lax.fori_loop(0, PLANES, mid_plane, jnp.zeros((ROWS, LANES), F32))
    second = BACKWARD.copies(back_start, gx, gz, n_gx, n_gz)
    for copy in second:
        copy.start()
    mine_a[...] = jnp.sum(total, axis=0, keepdims=True)

    def reduce_copy(stage, mine, got, slot, target):
        return pltpu.make_async_remote_copy(
            src_ref=mine,
            dst_ref=got.at[slot],
            send_sem=red_send.at[stage],
            recv_sem=red_recv.at[stage],
            device_id=target,
            device_id_type=MESH,
        )

    @pl.loop(1, n_gx)
    def _(k):
        reduce_copy(0, mine_a, got_a, gx, (gx_at(k), gz)).start()

    for copy in second:
        copy.wait_recv()

    def last_plane(x, carry):
        state = [cp[i, x] for i in range(CH)]
        carried = BACKWARD.get(back_start, x, 0)
        adjoint, sens_start = transposed(state, carried, por[x], kind[x])
        for i in range(CH):
            out_ref[i, x] = adjoint[i]
        grad_ref[x] = sens_start + sens[x]
        return carry

    def wait_stage(stage, got, count):
        pltpu.make_async_copy(
            got.at[pl.ds(0, count)], got.at[pl.ds(0, count)], red_recv.at[stage]
        ).wait()

    def wait_sent(stage, got, count):
        pltpu.make_async_copy(
            got.at[pl.ds(0, count)], got.at[pl.ds(0, count)], red_send.at[stage]
        ).wait()

    wait_stage(0, got_a, n_gx - 1)
    got_a[gx] = mine_a[...]
    mine_b[...] = jnp.sum(got_a[...], axis=0)

    @pl.loop(1, n_gz)
    def _(k):
        reduce_copy(1, mine_b, got_b, gz, (gx, gz_at(k))).start()

    lax.fori_loop(0, PLANES, last_plane, 0)

    wait_stage(1, got_b, n_gz - 1)
    got_b[gz] = mine_b[...]
    total_ref[...] = jnp.sum(jnp.sum(got_b[...], axis=0), axis=1, keepdims=True)

    wait_sent(0, got_a, n_gx - 1)
    wait_sent(1, got_b, n_gz - 1)
    for copy in first + second:
        copy.wait_send()


def solution(mesh):
    n_gx, n_gz = mesh.shape["gx"], mesh.shape["gz"]

    def on_device(*args):
        block = (PLANES, ROWS, LANES)
        any_space = pl.BlockSpec(memory_space=pl.ANY)
        in_vmem = pl.BlockSpec(memory_space=pltpu.VMEM)
        adjoint, grad, total = pl.pallas_call(
            lambda *refs: kernel(n_gx, n_gz, *refs),
            out_shape=(
                jax.ShapeDtypeStruct((CH,) + block, F32),
                jax.ShapeDtypeStruct(block, F32),
                jax.ShapeDtypeStruct((1, 1), F32),
            ),
            in_specs=[any_space] * 6,
            out_specs=(in_vmem, in_vmem, in_vmem),
            scratch_shapes=[
                pltpu.VMEM((CH,) + block, F32),
                pltpu.VMEM((CH,) + block, F32),
                pltpu.VMEM(block, F32),
                pltpu.VMEM(block, jnp.int32),
                pltpu.VMEM(block, jnp.int32),
                pltpu.SMEM((2,), F32),
                pltpu.VMEM(block, F32),
                pltpu.SemaphoreType.DMA((6,)),
            ]
            + FORWARD.scratch()
            + BACKWARD.scratch()
            + BACKWARD.scratch()
            + [
                pltpu.VMEM((1, LANES), F32),
                pltpu.VMEM((n_gx, 1, LANES), F32),
                pltpu.VMEM((1, LANES), F32),
                pltpu.VMEM((n_gz, 1, LANES), F32),
                pltpu.SemaphoreType.DMA((2,)),
                pltpu.SemaphoreType.DMA((2,)),
            ],
            compiler_params=pltpu.CompilerParams(
                collective_id=0, has_side_effects=True, vmem_limit_bytes=32 * 1024 * 1024
            ),
        )(*args)
        return adjoint, grad, total.reshape(())

    return jax.shard_map(
        on_device,
        mesh=mesh,
        in_specs=(
            P(None, "gx", "gz", None),
            P(None, "gx", "gz", None),
            P("gx", "gz", None),
            P("gx", "gz", None),
            P("gx", "gz", None),
            P(),
        ),
        out_specs=(P(None, "gx", "gz", None), P("gx", "gz", None), P()),
        check_vma=False,
    )
```

```python
import jax
import jax.numpy as jnp
from jax import lax
from jax.experimental import pallas as pl
from jax.experimental.pallas import tpu as pltpu
from jax.sharding import PartitionSpec as P

MESH = pl.DeviceIdType.MESH
F32 = jnp.float32

VEL = [
    (0, 0, 0),
    (1, 0, 0),
    (-1, 0, 0),
    (0, 1, 0),
    (0, -1, 0),
    (0, 0, 1),
    (0, 0, -1),
    (1, 1, 0),
    (-1, -1, 0),
    (1, -1, 0),
    (-1, 1, 0),
    (1, 0, 1),
    (-1, 0, -1),
    (1, 0, -1),
    (-1, 0, 1),
    (0, 1, 1),
    (0, -1, -1),
    (0, 1, -1),
    (0, -1, 1),
]
VEL = VEL + VEL[:7]
CH = 26
PLANES = 4
ROWS = 8
LANES = 128

NEIGHBOURS = ((1, 0), (-1, 0), (0, 1), (0, -1), (1, 1), (1, -1), (-1, 1), (-1, -1))

BRINKMAN = 4.0
SPEED = 0.05
RATE_H = 1.0 / 0.7
RATE_E = 1.5

E_NORM = 2394.0
FLUID_P, FLUID_Q = -0.2, -0.1
K_MEAN = 1.4 / 19.0
K_E = (1.4 - 1.19) / E_NORM
K_N = 0.15 / 18.0
K_D = 0.15 / 4.0
K_J = 0.2 / 10.0
K_Q = 0.78 / 8.0


def moments(f):
    e = [f[a] + f[a + 1] for a in range(1, 19, 2)]
    o = [f[a] - f[a + 1] for a in range(1, 19, 2)]
    sxy, txy = o[3] + o[4], o[3] - o[4]
    sxz, txz = o[5] + o[6], o[5] - o[6]
    syz, tyz = o[7] + o[8], o[7] - o[8]
    exy, dxy = e[3] + e[4], e[3] - e[4]
    exz, dxz = e[5] + e[6], e[5] - e[6]
    eyz, dyz = e[7] + e[8], e[7] - e[8]
    axis_sum = e[0] + e[1] + e[2]
    diag_sum = exy + exz + eyz
    return dict(
        e=e,
        o=o,
        f0=f[0],
        axis=axis_sum,
        diag=diag_sum,
        across=(eyz, exz, exy),
        cross=(dxy, dxz, dyz),
        j=(o[0] + sxy + sxz, o[1] + txy + syz, o[2] + txz + tyz),
        q=(sxy - sxz, syz - txy, txz - tyz),
    )


def density_velocity(m):
    r = m["f0"] + m["axis"] + m["diag"]
    inverse = 1.0 / r
    return r, inverse, [j * inverse for j in m["j"]]


def second_order(m):
    shift = m["axis"] - m["diag"]
    return [3.0 * (m["e"][a] - m["across"][a]) - shift for a in range(3)]


def assemble(even_rest, even_axis, even_diag, cross, odd_axis, odd_diag, third, pe, po, m):
    out = [even_rest]
    for a in range(3):
        even = pe * m["e"][a] + even_axis[a]
        odd = po * m["o"][a] + odd_axis[a]
        out += [even + odd, even - odd]
    x, y, z = odd_diag
    qx, qy, qz = third
    xy_x, xy_y = x + qx, y - qy
    xz_x, xz_z = x - qx, z + qz
    yz_y, yz_z = y + qy, z - qz
    odds = [xy_x + xy_y, xy_x - xy_y, xz_x + xz_z, xz_x - xz_z, yz_y + yz_z, yz_y - yz_z]
    for k in range(6):
        base = even_diag[2 - k // 2]
        base = base + cross[k // 2] if k % 2 == 0 else base - cross[k // 2]
        even = pe * m["e"][3 + k] + base
        odd = po * m["o"][3 + k] + odds[k]
        out += [even + odd, even - odd]
    return out


def cell_kinds(kind):
    return kind == 0, kind == 1, kind == 2, kind == 3


def relax_factors(kind):
    fluid, solid, _, _ = cell_kinds(kind)
    pe = jnp.where(fluid, FLUID_P, jnp.where(solid, 0.5, 0.0))
    po = jnp.where(fluid, FLUID_Q, jnp.where(solid, -0.5, 0.0))
    he = jnp.where(fluid, 0.5 - RATE_E / 2, jnp.where(solid, 0.5, 0.0))
    ho = jnp.where(fluid, 0.5 - RATE_H / 2, jnp.where(solid, -0.5, 0.0))
    return pe, po, he, ho


def damping_of(porosity):
    return 1.0 / (1.0 + BRINKMAN * (1.0 - porosity))


def dot3(a, b):
    return a[0] * b[0] + a[1] * b[1] + a[2] * b[2]


def collide(pops, porosity, kind, level):
    fluid, solid, inlet, outlet = cell_kinds(kind)
    pe, po, he, ho = relax_factors(kind)
    f, h = pops[:19], pops[19:]
    m = moments(f)
    r, _, u = density_velocity(m)
    d = damping_of(porosity)
    d_eff = jnp.where(outlet, 1.0, d)
    b = [c * d_eff for c in u]
    zero = jnp.zeros_like(r)

    def on(value):
        return jnp.where(fluid, value, 0.0)

    def pick(at_fluid, elsewhere):
        return jnp.where(fluid, at_fluid, jnp.where(solid, 0.0, elsewhere))

    re = jnp.where(inlet, 1.0, r)
    be = [
        jnp.where(inlet, SPEED, b[0]),
        jnp.where(inlet, 0.0, b[1]),
        jnp.where(inlet, 0.0, b[2]),
    ]
    rb = [re * c for c in be]
    bb = [p * c for p, c in zip(rb, be)]
    b2 = bb[0] + bb[1] + bb[2]
    crossed = (rb[0] * be[1], rb[0] * be[2], rb[1] * be[2])
    quad_rest = pick(-0.65, -0.5) * b2
    axis_all = pick(-0.09, -1.0 / 12.0) * b2
    axis_own = pick(0.325, 0.25)
    quad_axis = [axis_all + axis_own * c for c in bb]
    diag_all = pick(0.095, 1.0 / 12.0) * b2
    diag_own = pick(-0.15, -0.125)
    quad_diag = [diag_all + diag_own * c for c in bb]
    cross_own = pick(0.3125, 0.25)
    quad_cross = [cross_own * c for c in crossed]
    lin_axis_own = pick(0.18, 1.0 / 6.0)
    lin_diag_own = pick(0.08, 1.0 / 12.0)
    lin_axis = [lin_axis_own * c for c in rb]
    lin_diag = [lin_diag_own * c for c in rb]
    n = second_order(m)
    e_f = -30.0 * m["f0"] - 11.0 * m["axis"] + 8.0 * m["diag"]
    de = K_E * (e_f + 11.0 * r)
    even_rest = jnp.where(fluid, 1.4 / 3.0 * r - 30.0 * de, pick(0.0, 1.0 / 3.0) * re)
    even_axis = jnp.where(fluid, 1.4 / 18.0 * r - 11.0 * de, pick(0.0, 1.0 / 18.0) * re)
    even_diag = jnp.where(fluid, 1.4 / 36.0 * r + 8.0 * de, pick(0.0, 1.0 / 36.0) * re)
    rest_own = jnp.where(fluid, -0.4, jnp.where(solid, 1.0, 0.0))
    n_own = on(K_N)
    n = [n_own * c for c in n]
    d_own = on(K_D)
    j_own = on(K_J)
    q_own = on(-K_Q)
    jj = [j_own * c for c in m["j"]]
    new_f = assemble(
        rest_own * m["f0"] + even_rest + quad_rest,
        [even_axis + quad_axis[a] + n[a] for a in range(3)],
        [even_diag + quad_diag[a] - n[a] for a in range(3)],
        [quad_cross[k] + d_own * m["cross"][k] for k in range(3)],
        [lin_axis[a] + jj[a] for a in range(3)],
        [lin_diag[a] + jj[a] for a in range(3)],
        [q_own * c for c in m["q"]],
        pe,
        po,
        m,
    )
    kappa = on(BRINKMAN * d)
    kappa2 = kappa + kappa
    g_rest = kappa2 * quad_rest
    g_axis = [kappa2 * c for c in quad_axis]
    g_diag = [kappa2 * c for c in quad_diag]
    g_cross = [kappa2 * c for c in quad_cross]
    g_la = [kappa * c for c in lin_axis]
    g_ld = [kappa * c for c in lin_diag]
    g_f = [g_rest]
    for a in range(3):
        g_f += [g_axis[a] + g_la[a], g_axis[a] - g_la[a]]
    x, y, z = g_ld
    odds = [x + y, x - y, x + z, x - z, y + z, y - z]
    for k in range(6):
        even = g_diag[2 - k // 2]
        even = even + g_cross[k // 2] if k % 2 == 0 else even - g_cross[k // 2]
        g_f += [even + odds[k], even - odds[k]]
    he_pairs = [h[a] + h[a + 1] for a in (1, 3, 5)]
    ho_pairs = [h[a] - h[a + 1] for a in (1, 3, 5)]
    s = h[0] + he_pairs[0] + he_pairs[1] + he_pairs[2]
    se = jnp.where(inlet, level, s)
    s_even = pick(RATE_E, 1.0) * se
    s_odd = pick(0.5 * RATE_H, 0.5) * se
    new_h = [jnp.where(fluid, 1.0 - RATE_E, jnp.where(solid, 1.0, 0.0)) * h[0] + 0.25 * s_even]
    g_h = [zero]
    for a in range(3):
        even = he * he_pairs[a] + 0.125 * s_even
        push = s_odd * be[a]
        odd = ho * ho_pairs[a] + push
        new_h += [even + odd, even - odd]
        push = kappa * push
        g_h += [push, -push]
    return new_f + new_h, g_f + g_h


def weighted_factors(a, b, own):
    return (
        own[0] - a * K_MEAN + 30.0 * b * K_E,
        own[1] - a * K_MEAN + 11.0 * b * K_E,
        own[2] - a * K_MEAN - 8.0 * b * K_E,
    )


A0_F = weighted_factors(1.0, -11.0, (1.4 / 3.0, 1.4 / 18.0, 1.4 / 36.0))
A2_F = weighted_factors(1.0 / 3.0, 5.0 / 9.0, (0.0, 1.0 / 540.0, 1.4 / 36.0 - 1.0 / 540.0))


def transposed(pops, carried, porosity, kind):
    fluid, solid, inlet, outlet = cell_kinds(kind)
    pe, po, he, ho = relax_factors(kind)
    f, h = pops[:19], pops[19:]
    ms = moments(f)
    r, inverse, u = density_velocity(ms)
    s = h[0] + (h[1] + h[2]) + (h[3] + h[4]) + (h[5] + h[6])
    d = jnp.where(outlet, 1.0, damping_of(porosity))
    b = [c * d for c in u]
    ratio4 = 4.0 * s * inverse

    m = moments(carried[:19])
    mu = carried[19:]
    f0, axis, diag = m["f0"], m["axis"], m["diag"]

    def pick(at_fluid, at_outlet):
        return jnp.where(fluid, at_fluid, at_outlet)

    a0 = (
        pick(A0_F[0], 1.0 / 3.0) * f0
        + pick(A0_F[1], 1.0 / 18.0) * axis
        + pick(A0_F[2], 1.0 / 36.0) * diag
    )
    common = (
        pick(A2_F[0], 0.0) * f0 + pick(A2_F[1], 0.0) * axis + pick(A2_F[2], 1.0 / 36.0) * diag
    )
    own = pick(1.4 / 18.0 - 3.0 / 540.0, 1.0 / 18.0)
    away = pick(-1.4 / 36.0 + 3.0 / 540.0, -1.0 / 36.0)
    a2 = [own * m["e"][a] + away * m["across"][a] + common for a in range(3)]
    cross_own = pick(1.25 / 36.0, 1.0 / 36.0)
    axy, axz, ayz = [cross_own * c for c in m["cross"]]
    o_own = pick(1.0 / 30.0, 1.0 / 36.0)
    j_own = pick(0.96 / 36.0, 1.0 / 36.0)
    a1 = [o_own * m["o"][a] + j_own * m["j"][a] for a in range(3)]
    me = [mu[a] + mu[a + 1] for a in (1, 3, 5)]
    mo = [mu[a] - mu[a + 1] for a in (1, 3, 5)]
    me_sum = me[0] + me[1] + me[2]
    mean_h = (RATE_E / 7.0) * (mu[0] + me_sum)
    b0 = pick(RATE_E, 1.0) * (0.25 * mu[0] + 0.125 * me_sum) - pick(mean_h, 0.0)
    b1_own = pick(0.125 * RATE_H, 0.125)
    b1 = [b1_own * c for c in mo]

    ab = [
        a2[0] * b[0] + axy * b[1] + axz * b[2],
        axy * b[0] + a2[1] * b[1] + ayz * b[2],
        axz * b[0] + ayz * b[1] + a2[2] * b[2],
    ]
    curved = [9.0 * ab[a] - 3.0 * a0 * b[a] for a in range(3)]
    b1b = dot3(b1, b)
    total = [3.0 * a1[a] + curved[a] + ratio4 * b1[a] for a in range(3)]
    to_r = a0 - 0.5 * dot3(b, curved) - ratio4 * b1b
    to_s = b0 + 4.0 * b1b
    sens = jnp.where(fluid, BRINKMAN * d * d * dot3(ms["j"], total), 0.0)

    active = jnp.logical_or(fluid, outlet)
    d_on = jnp.where(active, d, 0.0)
    to_r = jnp.where(active, to_r, 0.0)
    to_s = jnp.where(active, to_s, 0.0)
    to_j = [d_on * c for c in total]

    def on(value):
        return jnp.where(fluid, value, 0.0)

    mean = on(K_MEAN) * (f0 + axis + diag)
    ef = on(K_E) * (-30.0 * f0 - 11.0 * axis + 8.0 * diag)
    base = to_r + mean
    n_own = on(K_N)
    n = [n_own * c for c in second_order(m)]
    d_own = on(K_D)
    jj_own = on(K_J)
    q_own = on(-K_Q)
    odd = [to_j[a] + jj_own * m["j"][a] for a in range(3)]
    rest_own = jnp.where(fluid, -0.4, jnp.where(solid, 1.0, 0.0))
    base_axis = base - 11.0 * ef
    base_diag = base + 8.0 * ef
    out_f = assemble(
        rest_own * f0 + base - 30.0 * ef,
        [base_axis + n[a] for a in range(3)],
        [base_diag - n[a] for a in range(3)],
        [d_own * c for c in m["cross"]],
        odd,
        odd,
        [q_own * c for c in m["q"]],
        pe,
        po,
        m,
    )
    to_s = to_s + on(mean_h)
    out_h = [jnp.where(fluid, 1.0 - RATE_E, jnp.where(solid, 1.0, 0.0)) * mu[0] + to_s]
    for a in range(3):
        even = he * me[a] + to_s
        odd = ho * mo[a]
        out_h += [even + odd, even - odd]
    return out_f + out_h, sens


class Stream:
    def __init__(self, heading, fields):
        self.heading = heading
        self.fields = fields
        self.vel = [tuple(heading * c for c in v) for v in VEL]
        plus = [i for i in range(CH) if self.vel[i][0] == 1]
        minus = [i for i in range(CH) if self.vel[i][0] == -1]
        still = [i for i in range(CH) if self.vel[i][0] == 0]
        order = [(k, i) for group in (plus, minus, still) for k in range(fields) for i in group]
        self.place = {key: at for at, key in enumerate(order)}
        self.face = len(plus) * fields
        self.z_place = {}
        self.edge = {}
        for sign in (1, -1):
            group = [i for i in range(CH) if self.vel[i][2] == sign]
            group.sort(key=lambda i: -abs(self.vel[i][0]))
            keys = [(k, i) for i in group for k in range(fields)]
            self.z_count = len(keys)
            for at, key in enumerate(keys):
                self.z_place[key] = (0 if sign == 1 else 1, at)
            for at, i in enumerate(group[:2]):
                self.edge[(self.vel[i][0], sign)] = at * fields

    def scratch(self):
        return [
            pltpu.VMEM((CH * self.fields, PLANES + 2, ROWS, LANES), F32),
            pltpu.VMEM((2, self.z_count, PLANES, 1, LANES), F32),
            pltpu.VMEM((2, self.z_count, PLANES + 2, 1, LANES), F32),
            pltpu.SemaphoreType.DMA((8,)),
            pltpu.SemaphoreType.DMA((8,)),
        ]

    def put(self, refs, x, field, values):
        padded, rows = refs[0], refs[1]
        for i, value in enumerate(values):
            _, vy, vz = self.vel[i]
            if vy:
                value = pltpu.roll(value, vy % LANES, 1)
            padded[self.place[(field, i)], x + 1] = value
            if vz:
                side, at = self.z_place[(field, i)]
                row = ROWS - 1 if vz == 1 else 0
                rows[side, at, x] = value[row : row + 1, :]

    def copies(self, refs, gx, gz, n_gx, n_gz):
        padded, rows, halo, send, recv = refs
        found = []
        for at, (dx, dz) in enumerate(NEIGHBOURS):
            target = (lax.rem(gx + dx + n_gx, n_gx), lax.rem(gz + dz + n_gz, n_gz))
            side = 0 if dz == 1 else 1
            if dz == 0:
                start = 0 if dx == 1 else self.face
                source = padded.at[pl.ds(start, self.face), PLANES if dx == 1 else 1]
                landing = padded.at[pl.ds(start, self.face), 0 if dx == 1 else PLANES + 1]
            elif dx == 0:
                source = rows.at[side]
                landing = halo.at[side, :, pl.ds(1, PLANES)]
            else:
                start = self.edge[(dx, dz)]
                source = rows.at[side, pl.ds(start, self.fields), PLANES - 1 if dx == 1 else 0]
                landing = halo.at[side, pl.ds(start, self.fields), 0 if dx == 1 else PLANES + 1]
            found.append(
                pltpu.make_async_remote_copy(
                    src_ref=source,
                    dst_ref=landing,
                    send_sem=send.at[at],
                    recv_sem=recv.at[at],
                    device_id=target,
                    device_id_type=MESH,
                )
            )
        return found

    def get(self, refs, x, field):
        padded, halo = refs[0], refs[2]
        row = lax.broadcasted_iota(jnp.int32, (ROWS, LANES), 0)
        values = []
        for i in range(CH):
            vx, _, vz = self.vel[i]
            value = padded[self.place[(field, i)], x + 1 - vx]
            if vz:
                side, at = self.z_place[(field, i)]
                edge = 0 if vz == 1 else ROWS - 1
                value = jnp.where(
                    row == edge, halo[side, at, x + 1 - vx], pltpu.roll(value, vz % ROWS, 0)
                )
            values.append(value)
        return values


FORWARD = Stream(1, 2)
BACKWARD = Stream(-1, 1)


def ring_distance(offset, size):
    return min(offset, size - offset)


def column_partners(n_gx):
    n_z = n_gx // 4
    found = [(z, core) for z in range(n_z) for core in range(2) if z or core]
    return sorted(found, key=lambda o: -(ring_distance(o[0], n_z) + 0.5 * o[1]))


def sheet_partners(n_gz):
    n_y = n_gz // 2
    found = [(a, b, y) for a in range(2) for b in range(2) for y in range(n_y) if a or b or y]
    return sorted(found, key=lambda o: -(ring_distance(o[2], n_y) + (0, 2, 1, 1)[2 * o[0] + o[1]]))


def kernel(n_gx, n_gz, *refs):
    (checkpoint, adjoint_end, porosity, node_type, inlet_index, inlet_conc) = refs[:6]
    (out_ref, grad_ref, sum_ref) = refs[6:9]
    (cp, ae, por, kind, feed, conc, sens, in_sem) = refs[9:17]
    forward, back_mid, back_start = refs[17:22], refs[22:27], refs[27:32]
    (mine_a, got_a, mine_b, got_b, red_send, red_recv) = refs[32:]
    gx, gz = lax.axis_index("gx"), lax.axis_index("gz")
    n_column, n_sheet = n_gx // 2, 2 * n_gz
    x_lo, column_at = gx // n_column, lax.rem(gx, n_column)
    z, core = column_at // 2, lax.rem(column_at, 2)
    x_hi, y = gz // (n_gz // 2), lax.rem(gz, n_gz // 2)

    def column_target(offset):
        dz, dcore = offset
        at = 2 * lax.rem(z + dz, n_column // 2) + lax.rem(core + dcore, 2)
        return (x_lo * n_column + at, gz)

    def sheet_target(offset):
        dlo, dhi, dy = offset
        to_gz = lax.rem(x_hi + dhi, 2) * (n_gz // 2) + lax.rem(y + dy, n_gz // 2)
        return (lax.rem(x_lo + dlo, 2) * n_column + column_at, to_gz)

    columns = [column_target(o) for o in column_partners(n_gx)]
    sheets = [sheet_target(o) for o in sheet_partners(n_gz)]

    loads = [
        pltpu.make_async_copy(source, target, in_sem.at[k])
        for k, (source, target) in enumerate(
            (
                (checkpoint, cp),
                (porosity, por),
                (node_type, kind),
                (inlet_index, feed),
                (inlet_conc, conc),
                (adjoint_end, ae),
            )
        )
    ]
    for load in loads:
        load.start()

    barrier = pltpu.get_barrier_semaphore()
    greeted = [
        (lax.rem(gx + dx + n_gx, n_gx), lax.rem(gz + dz + n_gz, n_gz)) for dx, dz in NEIGHBOURS
    ]
    greeted += columns + sheets
    for target in greeted:
        pl.semaphore_signal(barrier, inc=1, device_id=target, device_id_type=MESH)

    for load in loads[:5]:
        load.wait()

    def start_plane(x, carry):
        level = jnp.where(feed[x] == 0, conc[0], jnp.where(feed[x] == 1, conc[1], 0.0))
        post, slope = collide([cp[i, x] for i in range(CH)], por[x], kind[x], level)
        FORWARD.put(forward, x, 0, post)
        FORWARD.put(forward, x, 1, slope)
        return carry

    lax.fori_loop(0, PLANES, start_plane, 0, unroll=True)
    loads[5].wait()

    def end_plane(x, carry):
        BACKWARD.put(back_mid, x, 0, [ae[i, x] for i in range(CH)])
        return carry

    lax.fori_loop(0, PLANES, end_plane, 0, unroll=True)

    pl.semaphore_wait(barrier, len(greeted))
    first = FORWARD.copies(forward, gx, gz, n_gx, n_gz)
    first += BACKWARD.copies(back_mid, gx, gz, n_gx, n_gz)
    for copy in first:
        copy.start()
    for copy in first:
        copy.wait_recv()

    def mid_plane(x, total):
        state = FORWARD.get(forward, x, 0)
        slope = FORWARD.get(forward, x, 1)
        carried = BACKWARD.get(back_mid, x, 0)
        adjoint, sens_mid = transposed(state, carried, por[x], kind[x])
        sens[x] = sens_mid
        BACKWARD.put(back_start, x, 0, adjoint)
        sums = [a * b for a, b in zip(adjoint, slope)] + [sens_mid, total]
        while len(sums) > 1:
            sums = [a + b for a, b in zip(sums[::2], sums[1::2])] + sums[len(sums) & ~1 :]
        return sums[0]

    total = lax.fori_loop(0, PLANES, mid_plane, jnp.zeros((ROWS, LANES), F32), unroll=True)

    def reduce_copy(stage, mine, got, slot, target):
        return pltpu.make_async_remote_copy(
            src_ref=mine,
            dst_ref=got.at[slot],
            send_sem=red_send.at[stage],
            recv_sem=red_recv.at[stage],
            device_id=target,
            device_id_type=MESH,
        )

    def wait_for(semaphore, got, count):
        pltpu.make_async_copy(got.at[pl.ds(0, count)], got.at[pl.ds(0, count)], semaphore).wait()

    mine_a[...] = jnp.sum(total, axis=0, keepdims=True)
    for target in columns:
        reduce_copy(0, mine_a, got_a, column_at, target).start()
    second = BACKWARD.copies(back_start, gx, gz, n_gx, n_gz)
    for copy in second:
        copy.start()

    wait_for(red_recv.at[0], got_a, n_column - 1)
    got_a[column_at] = mine_a[...]
    mine_b[...] = jnp.sum(got_a[...], axis=0)
    sheet_at = x_lo * n_gz + gz
    for target in sheets:
        reduce_copy(1, mine_b, got_b, sheet_at, target).start()

    for copy in second:
        copy.wait_recv()

    def last_plane(x, carry):
        state = [cp[i, x] for i in range(CH)]
        carried = BACKWARD.get(back_start, x, 0)
        adjoint, sens_start = transposed(state, carried, por[x], kind[x])
        for i in range(CH):
            out_ref[i, x] = adjoint[i]
        grad_ref[x] = sens_start + sens[x]
        return carry

    lax.fori_loop(0, PLANES, last_plane, 0, unroll=True)

    for copy in first + second:
        copy.wait_send()
    wait_for(red_send.at[0], got_a, n_column - 1)
    wait_for(red_send.at[1], got_b, n_sheet - 1)
    wait_for(red_recv.at[1], got_b, n_sheet - 1)
    got_b[sheet_at] = mine_b[...]
    sum_ref[...] = jnp.sum(got_b[...], axis=0)


def finish(adjoint, grad, row, out_ref, grad_ref, total_ref, held, sems):
    copies = [
        pltpu.make_async_copy(adjoint, out_ref, sems.at[0]),
        pltpu.make_async_copy(grad, grad_ref, sems.at[1]),
        pltpu.make_async_copy(held, total_ref, sems.at[2]),
    ]
    copies[0].start()
    copies[1].start()
    held[...] = jnp.sum(row[...], axis=1, keepdims=True)
    copies[2].start()
    for copy in copies:
        copy.wait()


def solution(mesh):
    n_gx, n_gz = mesh.shape["gx"], mesh.shape["gz"]
    block = (PLANES, ROWS, LANES)
    any_space = pl.BlockSpec(memory_space=pl.ANY)
    in_vmem = pl.BlockSpec(memory_space=pltpu.VMEM)

    def on_device(*args):
        args = [pltpu.with_memory_space_constraint(a, pltpu.HBM) for a in args]
        held = pl.pallas_call(
            lambda *refs: kernel(n_gx, n_gz, *refs),
            out_shape=(
                pltpu.VMEM((CH,) + block, F32),
                pltpu.VMEM(block, F32),
                pltpu.VMEM((1, LANES), F32),
            ),
            in_specs=[any_space] * 6,
            out_specs=(in_vmem, in_vmem, in_vmem),
            scratch_shapes=[
                pltpu.VMEM((CH,) + block, F32),
                pltpu.VMEM((CH,) + block, F32),
                pltpu.VMEM(block, F32),
                pltpu.VMEM(block, jnp.int32),
                pltpu.VMEM(block, jnp.int32),
                pltpu.SMEM((2,), F32),
                pltpu.VMEM(block, F32),
                pltpu.SemaphoreType.DMA((6,)),
            ]
            + FORWARD.scratch()
            + BACKWARD.scratch()
            + BACKWARD.scratch()
            + [
                pltpu.VMEM((1, LANES), F32),
                pltpu.VMEM((n_gx // 2, 1, LANES), F32),
                pltpu.VMEM((1, LANES), F32),
                pltpu.VMEM((2 * n_gz, 1, LANES), F32),
                pltpu.SemaphoreType.DMA((2,)),
                pltpu.SemaphoreType.DMA((2,)),
            ],
            compiler_params=pltpu.CompilerParams(
                collective_id=0, has_side_effects=True, vmem_limit_bytes=32 * 1024 * 1024
            ),
        )(*args)
        held = [pltpu.with_memory_space_constraint(a, pltpu.VMEM) for a in held]
        adjoint, grad, total = pl.pallas_call(
            finish,
            out_shape=(
                jax.ShapeDtypeStruct((CH,) + block, F32),
                jax.ShapeDtypeStruct(block, F32),
                jax.ShapeDtypeStruct((1, 1), F32),
            ),
            in_specs=[in_vmem, in_vmem, in_vmem],
            out_specs=(any_space, any_space, any_space),
            scratch_shapes=[pltpu.VMEM((1, 1), F32), pltpu.SemaphoreType.DMA((3,))],
        )(*held)
        return adjoint, grad, total.reshape(())

    return jax.shard_map(
        on_device,
        mesh=mesh,
        in_specs=(
            P(None, "gx", "gz", None),
            P(None, "gx", "gz", None),
            P("gx", "gz", None),
            P("gx", "gz", None),
            P("gx", "gz", None),
            P(),
        ),
        out_specs=(P(None, "gx", "gz", None), P("gx", "gz", None), P()),
        check_vma=False,
    )
```

```python
import jax
import jax.numpy as jnp
from jax import lax
from jax.experimental import pallas as pl
from jax.experimental.pallas import tpu as pltpu
from jax.sharding import PartitionSpec as P

MESH = pl.DeviceIdType.MESH
F32 = jnp.float32

VEL = [
    (0, 0, 0),
    (1, 0, 0),
    (-1, 0, 0),
    (0, 1, 0),
    (0, -1, 0),
    (0, 0, 1),
    (0, 0, -1),
    (1, 1, 0),
    (-1, -1, 0),
    (1, -1, 0),
    (-1, 1, 0),
    (1, 0, 1),
    (-1, 0, -1),
    (1, 0, -1),
    (-1, 0, 1),
    (0, 1, 1),
    (0, -1, -1),
    (0, 1, -1),
    (0, -1, 1),
]
VEL = VEL + VEL[:7]
CH = 26
PLANES = 4
ROWS = 8
LANES = 128

NEIGHBOURS = ((1, 1), (1, -1), (-1, 1), (-1, -1), (0, 1), (0, -1), (1, 0), (-1, 0))

HUB_CORE = 1

BRINKMAN = 4.0
SPEED = 0.05
RATE_H = 1.0 / 0.7
RATE_E = 1.5

E_NORM = 2394.0
FLUID_P, FLUID_Q = -0.2, -0.1
K_MEAN = 1.4 / 19.0
K_E = (1.4 - 1.19) / E_NORM
K_N = 0.15 / 18.0
K_D = 0.15 / 4.0
K_J = 0.2 / 10.0
K_Q = 0.78 / 8.0


def moments(f):
    e = [f[a] + f[a + 1] for a in range(1, 19, 2)]
    o = [f[a] - f[a + 1] for a in range(1, 19, 2)]
    sxy, txy = o[3] + o[4], o[3] - o[4]
    sxz, txz = o[5] + o[6], o[5] - o[6]
    syz, tyz = o[7] + o[8], o[7] - o[8]
    exy, dxy = e[3] + e[4], e[3] - e[4]
    exz, dxz = e[5] + e[6], e[5] - e[6]
    eyz, dyz = e[7] + e[8], e[7] - e[8]
    axis_sum = e[0] + e[1] + e[2]
    diag_sum = exy + exz + eyz
    return dict(
        e=e,
        o=o,
        f0=f[0],
        axis=axis_sum,
        diag=diag_sum,
        across=(eyz, exz, exy),
        cross=(dxy, dxz, dyz),
        j=(o[0] + sxy + sxz, o[1] + txy + syz, o[2] + txz + tyz),
        q=(sxy - sxz, syz - txy, txz - tyz),
    )


def density_velocity(m):
    r = m["f0"] + m["axis"] + m["diag"]
    inverse = 1.0 / r
    return r, inverse, [j * inverse for j in m["j"]]


def second_order(m):
    shift = m["axis"] - m["diag"]
    return [3.0 * (m["e"][a] - m["across"][a]) - shift for a in range(3)]


def assemble(even_rest, even_axis, even_diag, cross, odd_axis, odd_diag, third, pe, po, m):
    out = [even_rest]
    for a in range(3):
        even = pe * m["e"][a] + even_axis[a]
        odd = po * m["o"][a] + odd_axis[a]
        out += [even + odd, even - odd]
    x, y, z = odd_diag
    qx, qy, qz = third
    xy_x, xy_y = x + qx, y - qy
    xz_x, xz_z = x - qx, z + qz
    yz_y, yz_z = y + qy, z - qz
    odds = [xy_x + xy_y, xy_x - xy_y, xz_x + xz_z, xz_x - xz_z, yz_y + yz_z, yz_y - yz_z]
    for k in range(6):
        base = even_diag[2 - k // 2]
        base = base + cross[k // 2] if k % 2 == 0 else base - cross[k // 2]
        even = pe * m["e"][3 + k] + base
        odd = po * m["o"][3 + k] + odds[k]
        out += [even + odd, even - odd]
    return out


def cell_kinds(kind):
    return kind == 0, kind == 1, kind == 2, kind == 3


def relax_factors(kind):
    fluid, solid, _, _ = cell_kinds(kind)
    pe = jnp.where(fluid, FLUID_P, jnp.where(solid, 0.5, 0.0))
    po = jnp.where(fluid, FLUID_Q, jnp.where(solid, -0.5, 0.0))
    he = jnp.where(fluid, 0.5 - RATE_E / 2, jnp.where(solid, 0.5, 0.0))
    ho = jnp.where(fluid, 0.5 - RATE_H / 2, jnp.where(solid, -0.5, 0.0))
    return pe, po, he, ho


def damping_of(porosity):
    return 1.0 / (1.0 + BRINKMAN * (1.0 - porosity))


def dot3(a, b):
    return a[0] * b[0] + a[1] * b[1] + a[2] * b[2]


def collide(pops, porosity, kind, level):
    fluid, solid, inlet, outlet = cell_kinds(kind)
    pe, po, he, ho = relax_factors(kind)
    f, h = pops[:19], pops[19:]
    m = moments(f)
    r, _, u = density_velocity(m)
    d = damping_of(porosity)
    d_eff = jnp.where(outlet, 1.0, d)
    b = [c * d_eff for c in u]
    zero = jnp.zeros_like(r)

    def on(value):
        return jnp.where(fluid, value, 0.0)

    def pick(at_fluid, elsewhere):
        return jnp.where(fluid, at_fluid, jnp.where(solid, 0.0, elsewhere))

    re = jnp.where(inlet, 1.0, r)
    be = [
        jnp.where(inlet, SPEED, b[0]),
        jnp.where(inlet, 0.0, b[1]),
        jnp.where(inlet, 0.0, b[2]),
    ]
    rb = [re * c for c in be]
    bb = [p * c for p, c in zip(rb, be)]
    b2 = bb[0] + bb[1] + bb[2]
    crossed = (rb[0] * be[1], rb[0] * be[2], rb[1] * be[2])
    quad_rest = pick(-0.65, -0.5) * b2
    axis_all = pick(-0.09, -1.0 / 12.0) * b2
    axis_own = pick(0.325, 0.25)
    quad_axis = [axis_all + axis_own * c for c in bb]
    diag_all = pick(0.095, 1.0 / 12.0) * b2
    diag_own = pick(-0.15, -0.125)
    quad_diag = [diag_all + diag_own * c for c in bb]
    cross_own = pick(0.3125, 0.25)
    quad_cross = [cross_own * c for c in crossed]
    lin_axis_own = pick(0.18, 1.0 / 6.0)
    lin_diag_own = pick(0.08, 1.0 / 12.0)
    lin_axis = [lin_axis_own * c for c in rb]
    lin_diag = [lin_diag_own * c for c in rb]
    n = second_order(m)
    e_f = -30.0 * m["f0"] - 11.0 * m["axis"] + 8.0 * m["diag"]
    de = K_E * (e_f + 11.0 * r)
    even_rest = jnp.where(fluid, 1.4 / 3.0 * r - 30.0 * de, pick(0.0, 1.0 / 3.0) * re)
    even_axis = jnp.where(fluid, 1.4 / 18.0 * r - 11.0 * de, pick(0.0, 1.0 / 18.0) * re)
    even_diag = jnp.where(fluid, 1.4 / 36.0 * r + 8.0 * de, pick(0.0, 1.0 / 36.0) * re)
    rest_own = jnp.where(fluid, -0.4, jnp.where(solid, 1.0, 0.0))
    n_own = on(K_N)
    n = [n_own * c for c in n]
    d_own = on(K_D)
    j_own = on(K_J)
    q_own = on(-K_Q)
    jj = [j_own * c for c in m["j"]]
    new_f = assemble(
        rest_own * m["f0"] + even_rest + quad_rest,
        [even_axis + quad_axis[a] + n[a] for a in range(3)],
        [even_diag + quad_diag[a] - n[a] for a in range(3)],
        [quad_cross[k] + d_own * m["cross"][k] for k in range(3)],
        [lin_axis[a] + jj[a] for a in range(3)],
        [lin_diag[a] + jj[a] for a in range(3)],
        [q_own * c for c in m["q"]],
        pe,
        po,
        m,
    )
    kappa = on(BRINKMAN * d)
    kappa2 = kappa + kappa
    g_rest = kappa2 * quad_rest
    g_axis = [kappa2 * c for c in quad_axis]
    g_diag = [kappa2 * c for c in quad_diag]
    g_cross = [kappa2 * c for c in quad_cross]
    g_la = [kappa * c for c in lin_axis]
    g_ld = [kappa * c for c in lin_diag]
    g_f = [g_rest]
    for a in range(3):
        g_f += [g_axis[a] + g_la[a], g_axis[a] - g_la[a]]
    x, y, z = g_ld
    odds = [x + y, x - y, x + z, x - z, y + z, y - z]
    for k in range(6):
        even = g_diag[2 - k // 2]
        even = even + g_cross[k // 2] if k % 2 == 0 else even - g_cross[k // 2]
        g_f += [even + odds[k], even - odds[k]]
    he_pairs = [h[a] + h[a + 1] for a in (1, 3, 5)]
    ho_pairs = [h[a] - h[a + 1] for a in (1, 3, 5)]
    s = h[0] + he_pairs[0] + he_pairs[1] + he_pairs[2]
    se = jnp.where(inlet, level, s)
    s_even = pick(RATE_E, 1.0) * se
    s_odd = pick(0.5 * RATE_H, 0.5) * se
    new_h = [jnp.where(fluid, 1.0 - RATE_E, jnp.where(solid, 1.0, 0.0)) * h[0] + 0.25 * s_even]
    g_h = [zero]
    for a in range(3):
        even = he * he_pairs[a] + 0.125 * s_even
        push = s_odd * be[a]
        odd = ho * ho_pairs[a] + push
        new_h += [even + odd, even - odd]
        push = kappa * push
        g_h += [push, -push]
    return new_f + new_h, g_f + g_h


def weighted_factors(a, b, own):
    return (
        own[0] - a * K_MEAN + 30.0 * b * K_E,
        own[1] - a * K_MEAN + 11.0 * b * K_E,
        own[2] - a * K_MEAN - 8.0 * b * K_E,
    )


A0_F = weighted_factors(1.0, -11.0, (1.4 / 3.0, 1.4 / 18.0, 1.4 / 36.0))
A2_F = weighted_factors(1.0 / 3.0, 5.0 / 9.0, (0.0, 1.0 / 540.0, 1.4 / 36.0 - 1.0 / 540.0))


def transposed(pops, carried, porosity, kind):
    fluid, solid, inlet, outlet = cell_kinds(kind)
    pe, po, he, ho = relax_factors(kind)
    f, h = pops[:19], pops[19:]
    ms = moments(f)
    r, inverse, u = density_velocity(ms)
    s = h[0] + (h[1] + h[2]) + (h[3] + h[4]) + (h[5] + h[6])
    d = jnp.where(outlet, 1.0, damping_of(porosity))
    b = [c * d for c in u]
    ratio4 = 4.0 * s * inverse

    m = moments(carried[:19])
    mu = carried[19:]
    f0, axis, diag = m["f0"], m["axis"], m["diag"]

    def pick(at_fluid, at_outlet):
        return jnp.where(fluid, at_fluid, at_outlet)

    a0 = (
        pick(A0_F[0], 1.0 / 3.0) * f0
        + pick(A0_F[1], 1.0 / 18.0) * axis
        + pick(A0_F[2], 1.0 / 36.0) * diag
    )
    common = (
        pick(A2_F[0], 0.0) * f0 + pick(A2_F[1], 0.0) * axis + pick(A2_F[2], 1.0 / 36.0) * diag
    )
    own = pick(1.4 / 18.0 - 3.0 / 540.0, 1.0 / 18.0)
    away = pick(-1.4 / 36.0 + 3.0 / 540.0, -1.0 / 36.0)
    a2 = [own * m["e"][a] + away * m["across"][a] + common for a in range(3)]
    cross_own = pick(1.25 / 36.0, 1.0 / 36.0)
    axy, axz, ayz = [cross_own * c for c in m["cross"]]
    o_own = pick(1.0 / 30.0, 1.0 / 36.0)
    j_own = pick(0.96 / 36.0, 1.0 / 36.0)
    a1 = [o_own * m["o"][a] + j_own * m["j"][a] for a in range(3)]
    me = [mu[a] + mu[a + 1] for a in (1, 3, 5)]
    mo = [mu[a] - mu[a + 1] for a in (1, 3, 5)]
    me_sum = me[0] + me[1] + me[2]
    mean_h = (RATE_E / 7.0) * (mu[0] + me_sum)
    b0 = pick(RATE_E, 1.0) * (0.25 * mu[0] + 0.125 * me_sum) - pick(mean_h, 0.0)
    b1_own = pick(0.125 * RATE_H, 0.125)
    b1 = [b1_own * c for c in mo]

    ab = [
        a2[0] * b[0] + axy * b[1] + axz * b[2],
        axy * b[0] + a2[1] * b[1] + ayz * b[2],
        axz * b[0] + ayz * b[1] + a2[2] * b[2],
    ]
    curved = [9.0 * ab[a] - 3.0 * a0 * b[a] for a in range(3)]
    b1b = dot3(b1, b)
    total = [3.0 * a1[a] + curved[a] + ratio4 * b1[a] for a in range(3)]
    to_r = a0 - 0.5 * dot3(b, curved) - ratio4 * b1b
    to_s = b0 + 4.0 * b1b
    sens = jnp.where(fluid, BRINKMAN * d * d * dot3(ms["j"], total), 0.0)

    active = jnp.logical_or(fluid, outlet)
    d_on = jnp.where(active, d, 0.0)
    to_r = jnp.where(active, to_r, 0.0)
    to_s = jnp.where(active, to_s, 0.0)
    to_j = [d_on * c for c in total]

    def on(value):
        return jnp.where(fluid, value, 0.0)

    mean = on(K_MEAN) * (f0 + axis + diag)
    ef = on(K_E) * (-30.0 * f0 - 11.0 * axis + 8.0 * diag)
    base = to_r + mean
    n_own = on(K_N)
    n = [n_own * c for c in second_order(m)]
    d_own = on(K_D)
    jj_own = on(K_J)
    q_own = on(-K_Q)
    odd = [to_j[a] + jj_own * m["j"][a] for a in range(3)]
    rest_own = jnp.where(fluid, -0.4, jnp.where(solid, 1.0, 0.0))
    base_axis = base - 11.0 * ef
    base_diag = base + 8.0 * ef
    out_f = assemble(
        rest_own * f0 + base - 30.0 * ef,
        [base_axis + n[a] for a in range(3)],
        [base_diag - n[a] for a in range(3)],
        [d_own * c for c in m["cross"]],
        odd,
        odd,
        [q_own * c for c in m["q"]],
        pe,
        po,
        m,
    )
    to_s = to_s + on(mean_h)
    out_h = [jnp.where(fluid, 1.0 - RATE_E, jnp.where(solid, 1.0, 0.0)) * mu[0] + to_s]
    for a in range(3):
        even = he * me[a] + to_s
        odd = ho * mo[a]
        out_h += [even + odd, even - odd]
    return out_f + out_h, sens


class Stream:
    def __init__(self, heading, fields):
        self.heading = heading
        self.fields = fields
        self.vel = [tuple(heading * c for c in v) for v in VEL]
        plus = [i for i in range(CH) if self.vel[i][0] == 1]
        minus = [i for i in range(CH) if self.vel[i][0] == -1]
        still = [i for i in range(CH) if self.vel[i][0] == 0]
        order = [(k, i) for group in (plus, minus, still) for k in range(fields) for i in group]
        self.place = {key: at for at, key in enumerate(order)}
        self.face = len(plus) * fields
        self.z_place = {}
        self.edge = {}
        for sign in (1, -1):
            group = [i for i in range(CH) if self.vel[i][2] == sign]
            group.sort(key=lambda i: -abs(self.vel[i][0]))
            keys = [(k, i) for i in group for k in range(fields)]
            self.z_count = len(keys)
            for at, key in enumerate(keys):
                self.z_place[key] = (0 if sign == 1 else 1, at)
            for at, i in enumerate(group[:2]):
                self.edge[(self.vel[i][0], sign)] = at * fields

    def scratch(self):
        return [
            pltpu.VMEM((CH * self.fields, PLANES + 2, ROWS, LANES), F32),
            pltpu.VMEM((2, self.z_count, PLANES, 1, LANES), F32),
            pltpu.VMEM((2, self.z_count, PLANES + 2, 1, LANES), F32),
            pltpu.SemaphoreType.DMA((8,)),
            pltpu.SemaphoreType.DMA((8,)),
        ]

    def put(self, refs, x, field, values):
        padded, rows = refs[0], refs[1]
        for i, value in enumerate(values):
            _, vy, vz = self.vel[i]
            if vy:
                value = pltpu.roll(value, vy % LANES, 1)
            padded[self.place[(field, i)], x + 1] = value
            if vz:
                side, at = self.z_place[(field, i)]
                row = ROWS - 1 if vz == 1 else 0
                rows[side, at, x] = value[row : row + 1, :]

    def copies(self, refs, gx, gz, n_gx, n_gz):
        padded, rows, halo, send, recv = refs
        found = []
        for at, (dx, dz) in enumerate(NEIGHBOURS):
            target = (lax.rem(gx + dx + n_gx, n_gx), lax.rem(gz + dz + n_gz, n_gz))
            side = 0 if dz == 1 else 1
            if dz == 0:
                start = 0 if dx == 1 else self.face
                source = padded.at[pl.ds(start, self.face), PLANES if dx == 1 else 1]
                landing = padded.at[pl.ds(start, self.face), 0 if dx == 1 else PLANES + 1]
            elif dx == 0:
                source = rows.at[side]
                landing = halo.at[side, :, pl.ds(1, PLANES)]
            else:
                start = self.edge[(dx, dz)]
                source = rows.at[side, pl.ds(start, self.fields), PLANES - 1 if dx == 1 else 0]
                landing = halo.at[side, pl.ds(start, self.fields), 0 if dx == 1 else PLANES + 1]
            found.append(
                pltpu.make_async_remote_copy(
                    src_ref=source,
                    dst_ref=landing,
                    send_sem=send.at[at],
                    recv_sem=recv.at[at],
                    device_id=target,
                    device_id_type=MESH,
                )
            )
        return found

    def get(self, refs, x, field):
        padded, halo = refs[0], refs[2]
        row = lax.broadcasted_iota(jnp.int32, (ROWS, LANES), 0)
        values = []
        for i in range(CH):
            vx, _, vz = self.vel[i]
            value = padded[self.place[(field, i)], x + 1 - vx]
            if vz:
                side, at = self.z_place[(field, i)]
                edge = 0 if vz == 1 else ROWS - 1
                value = jnp.where(
                    row == edge, halo[side, at, x + 1 - vx], pltpu.roll(value, vz % ROWS, 0)
                )
            values.append(value)
        return values


OPPOSITE = [VEL.index(tuple(-c for c in v)) for v in VEL[:19]]
OPPOSITE += [19 + k for k in OPPOSITE[:7]]
FORWARD = Stream(1, 3)
BACKWARD = Stream(-1, 1)


def kernel(n_gx, n_gz, *refs):
    (checkpoint, adjoint_end, porosity, node_type, inlet_index, inlet_conc) = refs[:6]
    (out_ref, grad_ref, sum_ref) = refs[6:9]
    (cp, ae, por, kind, feed, conc, sens, in_sem) = refs[9:17]
    forward, back = refs[17:22], refs[22:27]
    (mine_a, got_a, mine_b, got_b, total_row, got_c, red_send, red_recv) = refs[27:]
    gx, gz = lax.axis_index("gx"), lax.axis_index("gz")
    n_column, n_sheet = n_gx // 2, 2 * n_gz
    x_lo, column_at = gx // n_column, lax.rem(gx, n_column)
    z, core = column_at // 2, lax.rem(column_at, 2)
    x_hi, y = gz // (n_gz // 2), lax.rem(gz, n_gz // 2)

    n_z = n_column // 2
    lower = z < n_z // 2
    upper = jnp.logical_not(lower)
    hub = jnp.logical_and(lower, core == HUB_CORE)
    lower_only = jnp.logical_and(lower, core != HUB_CORE)
    first_hub = jnp.logical_and(hub, z == 0)
    last_hub = jnp.logical_and(hub, z == n_z // 2 - 1)

    def column(at_z, at_core):
        return (x_lo * n_column + 2 * at_z + at_core, gz)

    n_y = n_gz // 2

    def sheet(lo, hi, at_y, at_core):
        to_gz = lax.rem(x_hi + hi, 2) * n_y + at_y
        return (lax.rem(x_lo + lo, 2) * n_column + 2 * z + at_core, to_gz)

    rows = [*reversed(range(n_y // 2)), *reversed(range(n_y // 2, n_y))]
    around = [(lo, hi, k, c) for k in rows for hi in (1, 0) for lo in (1, 0) for c in (1 - HUB_CORE, HUB_CORE)]

    def each_of(offsets, act):
        for lo, hi, k, c in offsets:
            if lo or hi or c != HUB_CORE:
                act(sheet(lo, hi, k, c))
            else:

                @pl.when(y != k)
                def _():
                    act(sheet(lo, hi, k, c))

    to_hubs = [o for o in around if o[3] == HUB_CORE]
    column_hubs = [(k, HUB_CORE) for k in range(n_z // 2)]
    fourth = [(k, c) for k in range(3 * n_z // 4, n_z) for c in range(2)]
    third = [(k, c) for k in range(n_z // 2, 3 * n_z // 4) for c in range(2)]

    barrier = pltpu.get_barrier_semaphore()

    def greet(target):
        pl.semaphore_signal(barrier, inc=1, device_id=target, device_id_type=MESH)

    def neighbour(dx, dz):
        return (lax.rem(gx + dx + n_gx, n_gx), lax.rem(gz + dz + n_gz, n_gz))

    for dx, dz in NEIGHBOURS:
        greet(neighbour(dx, dz))

    loads = [
        pltpu.make_async_copy(source, target, in_sem.at[k])
        for k, (source, target) in enumerate(
            (
                (checkpoint, cp),
                (porosity, por),
                (node_type, kind),
                (inlet_index, feed),
                (inlet_conc, conc),
                (adjoint_end, ae),
            )
        )
    ]
    for load in loads:
        load.start()

    @pl.when(upper)
    def _():
        greet(column(jnp.where(z < 3 * n_z // 4, n_z // 2 - 1, 0), HUB_CORE))

    @pl.when(lower_only)
    def _():
        for offset in to_hubs:
            greet(sheet(*offset))

    @pl.when(hub)
    def _():
        each_of(to_hubs, greet)
        greet(column(z, 1 - HUB_CORE))
        for k in range(1, n_z):
            for c in range(2):
                greet(column(lax.rem(z + k, n_z), c))

    for load in loads[:5]:
        load.wait()

    def start_plane(x, carry):
        level = jnp.where(feed[x] == 0, conc[0], jnp.where(feed[x] == 1, conc[1], 0.0))
        post, slope = collide([cp[i, x] for i in range(CH)], por[x], kind[x], level)
        FORWARD.put(forward, x, 0, post)
        FORWARD.put(forward, x, 1, slope)
        return carry

    lax.fori_loop(0, PLANES, start_plane, 0, unroll=True)
    loads[5].wait()

    def end_plane(x, carry):
        FORWARD.put(forward, x, 2, [ae[i, x] for i in OPPOSITE])
        return carry

    lax.fori_loop(0, PLANES, end_plane, 0, unroll=True)

    hub_sends = len(column_hubs) - 1 + len(around) - 1
    awaited = len(NEIGHBOURS) + jnp.where(hub, hub_sends, len(column_hubs))
    awaited += jnp.where(first_hub, len(fourth), 0) + jnp.where(last_hub, len(third), 0)
    pl.semaphore_wait(barrier, awaited)
    first = FORWARD.copies(forward, gx, gz, n_gx, n_gz)
    for copy in first:
        copy.start()
    for copy in first:
        copy.wait_recv()

    def mid_plane(x, total):
        state = FORWARD.get(forward, x, 0)
        slope = FORWARD.get(forward, x, 1)
        mirrored = FORWARD.get(forward, x, 2)
        carried = [mirrored[i] for i in OPPOSITE]
        adjoint, sens_mid = transposed(state, carried, por[x], kind[x])
        sens[x] = sens_mid
        BACKWARD.put(back, x, 0, adjoint)
        sums = [a * b for a, b in zip(adjoint, slope)] + [sens_mid, total]
        while len(sums) > 1:
            sums = [a + b for a, b in zip(sums[::2], sums[1::2])] + sums[len(sums) & ~1 :]
        return sums[0]

    total = lax.fori_loop(0, PLANES, mid_plane, jnp.zeros((ROWS, LANES), F32), unroll=True)

    def reduce_copy(stage, mine, got, slot, target):
        return pltpu.make_async_remote_copy(
            src_ref=mine,
            dst_ref=got.at[slot],
            send_sem=red_send.at[stage],
            recv_sem=red_recv.at[stage],
            device_id=target,
            device_id_type=MESH,
        )

    def wait_for(semaphore, got, count):
        pltpu.make_async_copy(got.at[pl.ds(0, count)], got.at[pl.ds(0, count)], semaphore).wait()

    mine_a[...] = jnp.sum(total, axis=0, keepdims=True)
    for k, c in column_hubs:

        @pl.when(jnp.logical_not(jnp.logical_and(hub, z == k)))
        def _():
            reduce_copy(0, mine_a, got_a, column_at, column(k, c)).start()

    second = BACKWARD.copies(back, gx, gz, n_gx, n_gz)
    for copy in second:
        copy.start()

    sheet_at = x_lo * n_gz + gz

    @pl.when(hub)
    def _():
        wait_for(red_recv.at[0], got_a, n_column - 1)
        got_a[column_at] = mine_a[...]
        mine_b[...] = jnp.sum(got_a[...], axis=0)
        each_of(
            around, lambda target: reduce_copy(1, mine_b, got_b, sheet_at, target).start()
        )
        got_b[sheet_at] = mine_b[...]

    for copy in second:
        copy.wait_recv()

    def last_plane(x, carry):
        state = [cp[i, x] for i in range(CH)]
        carried = BACKWARD.get(back, x, 0)
        adjoint, sens_start = transposed(state, carried, por[x], kind[x])
        for i in range(CH):
            out_ref[i, x] = adjoint[i]
        grad_ref[x] = sens_start + sens[x]
        return carry

    lax.fori_loop(0, PLANES, last_plane, 0, unroll=True)

    for copy in first + second:
        copy.wait_send()

    @pl.when(hub)
    def _():
        wait_for(red_recv.at[1], got_b, n_sheet - 1)

    @pl.when(lower_only)
    def _():
        wait_for(red_recv.at[1], got_b, n_sheet)

    @pl.when(lower)
    def _():
        total_row[...] = jnp.sum(got_b[...], axis=0)
        sum_ref[...] = total_row[...]

    for is_hub, targets in ((first_hub, fourth), (last_hub, third)):

        @pl.when(is_hub)
        def _():
            for k, c in targets:
                reduce_copy(2, total_row, got_c, 0, column(k, c)).start()
            wait_for(red_send.at[2], got_b, len(targets))

    @pl.when(upper)
    def _():
        wait_for(red_recv.at[2], got_c, 1)
        sum_ref[...] = got_c[0]

    @pl.when(hub)
    def _():
        wait_for(red_send.at[0], got_a, len(column_hubs) - 1)
        wait_for(red_send.at[1], got_b, n_sheet - 1)
        wait_for(red_send.at[1], got_b, n_sheet)

    @pl.when(jnp.logical_not(hub))
    def _():
        wait_for(red_send.at[0], got_a, len(column_hubs))


def finish(adjoint, grad, row, out_ref, grad_ref, total_ref, held, sems):
    copies = [
        pltpu.make_async_copy(adjoint, out_ref, sems.at[0]),
        pltpu.make_async_copy(grad, grad_ref, sems.at[1]),
        pltpu.make_async_copy(held, total_ref, sems.at[2]),
    ]
    copies[0].start()
    copies[1].start()
    held[...] = jnp.sum(row[...], axis=1, keepdims=True)
    copies[2].start()
    for copy in copies:
        copy.wait()


def solution(mesh):
    n_gx, n_gz = mesh.shape["gx"], mesh.shape["gz"]
    block = (PLANES, ROWS, LANES)
    any_space = pl.BlockSpec(memory_space=pl.ANY)
    in_vmem = pl.BlockSpec(memory_space=pltpu.VMEM)

    def on_device(*args):
        args = [pltpu.with_memory_space_constraint(a, pltpu.HBM) for a in args]
        held = pl.pallas_call(
            lambda *refs: kernel(n_gx, n_gz, *refs),
            out_shape=(
                pltpu.VMEM((CH,) + block, F32),
                pltpu.VMEM(block, F32),
                pltpu.VMEM((1, LANES), F32),
            ),
            in_specs=[any_space] * 6,
            out_specs=(in_vmem, in_vmem, in_vmem),
            scratch_shapes=[
                pltpu.VMEM((CH,) + block, F32),
                pltpu.VMEM((CH,) + block, F32),
                pltpu.VMEM(block, F32),
                pltpu.VMEM(block, jnp.int32),
                pltpu.VMEM(block, jnp.int32),
                pltpu.SMEM((2,), F32),
                pltpu.VMEM(block, F32),
                pltpu.SemaphoreType.DMA((6,)),
            ]
            + FORWARD.scratch()
            + BACKWARD.scratch()
            + [
                pltpu.VMEM((1, LANES), F32),
                pltpu.VMEM((n_gx // 2, 1, LANES), F32),
                pltpu.VMEM((1, LANES), F32),
                pltpu.VMEM((2 * n_gz, 1, LANES), F32),
                pltpu.VMEM((1, LANES), F32),
                pltpu.VMEM((1, 1, LANES), F32),
                pltpu.SemaphoreType.DMA((3,)),
                pltpu.SemaphoreType.DMA((3,)),
            ],
            compiler_params=pltpu.CompilerParams(
                collective_id=0, has_side_effects=True, vmem_limit_bytes=32 * 1024 * 1024
            ),
        )(*args)
        held = [pltpu.with_memory_space_constraint(a, pltpu.VMEM) for a in held]
        adjoint, grad, total = pl.pallas_call(
            finish,
            out_shape=(
                jax.ShapeDtypeStruct((CH,) + block, F32),
                jax.ShapeDtypeStruct(block, F32),
                jax.ShapeDtypeStruct((1, 1), F32),
            ),
            in_specs=[in_vmem, in_vmem, in_vmem],
            out_specs=(any_space, any_space, any_space),
            scratch_shapes=[pltpu.VMEM((1, 1), F32), pltpu.SemaphoreType.DMA((3,))],
        )(*held)
        return adjoint, grad, total.reshape(())

    return jax.shard_map(
        on_device,
        mesh=mesh,
        in_specs=(
            P(None, "gx", "gz", None),
            P(None, "gx", "gz", None),
            P("gx", "gz", None),
            P("gx", "gz", None),
            P("gx", "gz", None),
            P(),
        ),
        out_specs=(P(None, "gx", "gz", None), P("gx", "gz", None), P()),
        check_vma=False,
    )
```

```python
import jax
import jax.numpy as jnp
from jax import lax
from jax.experimental import pallas as pl
from jax.experimental.pallas import tpu as pltpu
from jax.sharding import PartitionSpec as P

MESH = pl.DeviceIdType.MESH
F32 = jnp.float32

VEL = [
    (0, 0, 0),
    (1, 0, 0),
    (-1, 0, 0),
    (0, 1, 0),
    (0, -1, 0),
    (0, 0, 1),
    (0, 0, -1),
    (1, 1, 0),
    (-1, -1, 0),
    (1, -1, 0),
    (-1, 1, 0),
    (1, 0, 1),
    (-1, 0, -1),
    (1, 0, -1),
    (-1, 0, 1),
    (0, 1, 1),
    (0, -1, -1),
    (0, 1, -1),
    (0, -1, 1),
]
VEL = VEL + VEL[:7]
CH = 26
PLANES = 4
ROWS = 8
LANES = 128

NEIGHBOURS = ((1, 1), (1, -1), (-1, 1), (-1, -1), (0, 1), (0, -1), (1, 0), (-1, 0))

HUB_CORE = 1

BRINKMAN = 4.0
SPEED = 0.05
RATE_H = 1.0 / 0.7
RATE_E = 1.5

E_NORM = 2394.0
FLUID_P, FLUID_Q = -0.2, -0.1
K_MEAN = 1.4 / 19.0
K_E = (1.4 - 1.19) / E_NORM
K_N = 0.15 / 18.0
K_D = 0.15 / 4.0
K_J = 0.2 / 10.0
K_Q = 0.78 / 8.0


def moments(f):
    e = [f[a] + f[a + 1] for a in range(1, 19, 2)]
    o = [f[a] - f[a + 1] for a in range(1, 19, 2)]
    sxy, txy = o[3] + o[4], o[3] - o[4]
    sxz, txz = o[5] + o[6], o[5] - o[6]
    syz, tyz = o[7] + o[8], o[7] - o[8]
    exy, dxy = e[3] + e[4], e[3] - e[4]
    exz, dxz = e[5] + e[6], e[5] - e[6]
    eyz, dyz = e[7] + e[8], e[7] - e[8]
    axis_sum = e[0] + e[1] + e[2]
    diag_sum = exy + exz + eyz
    return dict(
        e=e,
        o=o,
        f0=f[0],
        axis=axis_sum,
        diag=diag_sum,
        across=(eyz, exz, exy),
        cross=(dxy, dxz, dyz),
        j=(o[0] + sxy + sxz, o[1] + txy + syz, o[2] + txz + tyz),
        q=(sxy - sxz, syz - txy, txz - tyz),
    )


def density_velocity(m):
    r = m["f0"] + m["axis"] + m["diag"]
    inverse = 1.0 / r
    return r, inverse, [j * inverse for j in m["j"]]


def second_order(m):
    shift = m["axis"] - m["diag"]
    return [3.0 * (m["e"][a] - m["across"][a]) - shift for a in range(3)]


def assemble(even_rest, even_axis, even_diag, cross, odd_axis, odd_diag, third, pe, po, m):
    out = [even_rest]
    for a in range(3):
        even = pe * m["e"][a] + even_axis[a]
        odd = po * m["o"][a] + odd_axis[a]
        out += [even + odd, even - odd]
    x, y, z = odd_diag
    qx, qy, qz = third
    xy_x, xy_y = x + qx, y - qy
    xz_x, xz_z = x - qx, z + qz
    yz_y, yz_z = y + qy, z - qz
    odds = [xy_x + xy_y, xy_x - xy_y, xz_x + xz_z, xz_x - xz_z, yz_y + yz_z, yz_y - yz_z]
    for k in range(6):
        base = even_diag[2 - k // 2]
        base = base + cross[k // 2] if k % 2 == 0 else base - cross[k // 2]
        even = pe * m["e"][3 + k] + base
        odd = po * m["o"][3 + k] + odds[k]
        out += [even + odd, even - odd]
    return out


def cell_kinds(kind):
    return kind == 0, kind == 1, kind == 2, kind == 3


def relax_factors(kind):
    fluid, solid, _, _ = cell_kinds(kind)
    pe = jnp.where(fluid, FLUID_P, jnp.where(solid, 0.5, 0.0))
    po = jnp.where(fluid, FLUID_Q, jnp.where(solid, -0.5, 0.0))
    he = jnp.where(fluid, 0.5 - RATE_E / 2, jnp.where(solid, 0.5, 0.0))
    ho = jnp.where(fluid, 0.5 - RATE_H / 2, jnp.where(solid, -0.5, 0.0))
    return pe, po, he, ho


def damping_of(porosity):
    return 1.0 / (1.0 + BRINKMAN * (1.0 - porosity))


def dot3(a, b):
    return a[0] * b[0] + a[1] * b[1] + a[2] * b[2]


def collide(pops, porosity, kind, level):
    fluid, solid, inlet, outlet = cell_kinds(kind)
    pe, po, he, ho = relax_factors(kind)
    f, h = pops[:19], pops[19:]
    m = moments(f)
    r, _, u = density_velocity(m)
    d = damping_of(porosity)
    d_eff = jnp.where(outlet, 1.0, d)
    b = [c * d_eff for c in u]
    zero = jnp.zeros_like(r)

    def on(value):
        return jnp.where(fluid, value, 0.0)

    def pick(at_fluid, elsewhere):
        return jnp.where(fluid, at_fluid, jnp.where(solid, 0.0, elsewhere))

    re = jnp.where(inlet, 1.0, r)
    be = [
        jnp.where(inlet, SPEED, b[0]),
        jnp.where(inlet, 0.0, b[1]),
        jnp.where(inlet, 0.0, b[2]),
    ]
    rb = [re * c for c in be]
    bb = [p * c for p, c in zip(rb, be)]
    b2 = bb[0] + bb[1] + bb[2]
    crossed = (rb[0] * be[1], rb[0] * be[2], rb[1] * be[2])
    quad_rest = pick(-0.65, -0.5) * b2
    axis_all = pick(-0.09, -1.0 / 12.0) * b2
    axis_own = pick(0.325, 0.25)
    quad_axis = [axis_all + axis_own * c for c in bb]
    diag_all = pick(0.095, 1.0 / 12.0) * b2
    diag_own = pick(-0.15, -0.125)
    quad_diag = [diag_all + diag_own * c for c in bb]
    cross_own = pick(0.3125, 0.25)
    quad_cross = [cross_own * c for c in crossed]
    lin_axis_own = pick(0.18, 1.0 / 6.0)
    lin_diag_own = pick(0.08, 1.0 / 12.0)
    lin_axis = [lin_axis_own * c for c in rb]
    lin_diag = [lin_diag_own * c for c in rb]
    n = second_order(m)
    e_f = -30.0 * m["f0"] - 11.0 * m["axis"] + 8.0 * m["diag"]
    de = K_E * (e_f + 11.0 * r)
    even_rest = jnp.where(fluid, 1.4 / 3.0 * r - 30.0 * de, pick(0.0, 1.0 / 3.0) * re)
    even_axis = jnp.where(fluid, 1.4 / 18.0 * r - 11.0 * de, pick(0.0, 1.0 / 18.0) * re)
    even_diag = jnp.where(fluid, 1.4 / 36.0 * r + 8.0 * de, pick(0.0, 1.0 / 36.0) * re)
    rest_own = jnp.where(fluid, -0.4, jnp.where(solid, 1.0, 0.0))
    n_own = on(K_N)
    n = [n_own * c for c in n]
    d_own = on(K_D)
    j_own = on(K_J)
    q_own = on(-K_Q)
    jj = [j_own * c for c in m["j"]]
    new_f = assemble(
        rest_own * m["f0"] + even_rest + quad_rest,
        [even_axis + quad_axis[a] + n[a] for a in range(3)],
        [even_diag + quad_diag[a] - n[a] for a in range(3)],
        [quad_cross[k] + d_own * m["cross"][k] for k in range(3)],
        [lin_axis[a] + jj[a] for a in range(3)],
        [lin_diag[a] + jj[a] for a in range(3)],
        [q_own * c for c in m["q"]],
        pe,
        po,
        m,
    )
    kappa = on(BRINKMAN * d)
    kappa2 = kappa + kappa
    g_rest = kappa2 * quad_rest
    g_axis = [kappa2 * c for c in quad_axis]
    g_diag = [kappa2 * c for c in quad_diag]
    g_cross = [kappa2 * c for c in quad_cross]
    g_la = [kappa * c for c in lin_axis]
    g_ld = [kappa * c for c in lin_diag]
    g_f = [g_rest]
    for a in range(3):
        g_f += [g_axis[a] + g_la[a], g_axis[a] - g_la[a]]
    x, y, z = g_ld
    odds = [x + y, x - y, x + z, x - z, y + z, y - z]
    for k in range(6):
        even = g_diag[2 - k // 2]
        even = even + g_cross[k // 2] if k % 2 == 0 else even - g_cross[k // 2]
        g_f += [even + odds[k], even - odds[k]]
    he_pairs = [h[a] + h[a + 1] for a in (1, 3, 5)]
    ho_pairs = [h[a] - h[a + 1] for a in (1, 3, 5)]
    s = h[0] + he_pairs[0] + he_pairs[1] + he_pairs[2]
    se = jnp.where(inlet, level, s)
    s_even = pick(RATE_E, 1.0) * se
    s_odd = pick(0.5 * RATE_H, 0.5) * se
    new_h = [jnp.where(fluid, 1.0 - RATE_E, jnp.where(solid, 1.0, 0.0)) * h[0] + 0.25 * s_even]
    g_h = [zero]
    for a in range(3):
        even = he * he_pairs[a] + 0.125 * s_even
        push = s_odd * be[a]
        odd = ho * ho_pairs[a] + push
        new_h += [even + odd, even - odd]
        push = kappa * push
        g_h += [push, -push]
    return new_f + new_h, g_f + g_h


def weighted_factors(a, b, own):
    return (
        own[0] - a * K_MEAN + 30.0 * b * K_E,
        own[1] - a * K_MEAN + 11.0 * b * K_E,
        own[2] - a * K_MEAN - 8.0 * b * K_E,
    )


A0_F = weighted_factors(1.0, -11.0, (1.4 / 3.0, 1.4 / 18.0, 1.4 / 36.0))
A2_F = weighted_factors(1.0 / 3.0, 5.0 / 9.0, (0.0, 1.0 / 540.0, 1.4 / 36.0 - 1.0 / 540.0))


def transposed(pops, carried, porosity, kind):
    fluid, solid, inlet, outlet = cell_kinds(kind)
    pe, po, he, ho = relax_factors(kind)
    f, h = pops[:19], pops[19:]
    ms = moments(f)
    r, inverse, u = density_velocity(ms)
    s = h[0] + (h[1] + h[2]) + (h[3] + h[4]) + (h[5] + h[6])
    d = jnp.where(outlet, 1.0, damping_of(porosity))
    b = [c * d for c in u]
    ratio4 = 4.0 * s * inverse

    m = moments(carried[:19])
    mu = carried[19:]
    f0, axis, diag = m["f0"], m["axis"], m["diag"]

    def pick(at_fluid, at_outlet):
        return jnp.where(fluid, at_fluid, at_outlet)

    a0 = (
        pick(A0_F[0], 1.0 / 3.0) * f0
        + pick(A0_F[1], 1.0 / 18.0) * axis
        + pick(A0_F[2], 1.0 / 36.0) * diag
    )
    common = (
        pick(A2_F[0], 0.0) * f0 + pick(A2_F[1], 0.0) * axis + pick(A2_F[2], 1.0 / 36.0) * diag
    )
    own = pick(1.4 / 18.0 - 3.0 / 540.0, 1.0 / 18.0)
    away = pick(-1.4 / 36.0 + 3.0 / 540.0, -1.0 / 36.0)
    a2 = [own * m["e"][a] + away * m["across"][a] + common for a in range(3)]
    cross_own = pick(1.25 / 36.0, 1.0 / 36.0)
    axy, axz, ayz = [cross_own * c for c in m["cross"]]
    o_own = pick(1.0 / 30.0, 1.0 / 36.0)
    j_own = pick(0.96 / 36.0, 1.0 / 36.0)
    a1 = [o_own * m["o"][a] + j_own * m["j"][a] for a in range(3)]
    me = [mu[a] + mu[a + 1] for a in (1, 3, 5)]
    mo = [mu[a] - mu[a + 1] for a in (1, 3, 5)]
    me_sum = me[0] + me[1] + me[2]
    mean_h = (RATE_E / 7.0) * (mu[0] + me_sum)
    b0 = pick(RATE_E, 1.0) * (0.25 * mu[0] + 0.125 * me_sum) - pick(mean_h, 0.0)
    b1_own = pick(0.125 * RATE_H, 0.125)
    b1 = [b1_own * c for c in mo]

    ab = [
        a2[0] * b[0] + axy * b[1] + axz * b[2],
        axy * b[0] + a2[1] * b[1] + ayz * b[2],
        axz * b[0] + ayz * b[1] + a2[2] * b[2],
    ]
    curved = [9.0 * ab[a] - 3.0 * a0 * b[a] for a in range(3)]
    b1b = dot3(b1, b)
    total = [3.0 * a1[a] + curved[a] + ratio4 * b1[a] for a in range(3)]
    to_r = a0 - 0.5 * dot3(b, curved) - ratio4 * b1b
    to_s = b0 + 4.0 * b1b
    sens = jnp.where(fluid, BRINKMAN * d * d * dot3(ms["j"], total), 0.0)

    active = jnp.logical_or(fluid, outlet)
    d_on = jnp.where(active, d, 0.0)
    to_r = jnp.where(active, to_r, 0.0)
    to_s = jnp.where(active, to_s, 0.0)
    to_j = [d_on * c for c in total]

    def on(value):
        return jnp.where(fluid, value, 0.0)

    mean = on(K_MEAN) * (f0 + axis + diag)
    ef = on(K_E) * (-30.0 * f0 - 11.0 * axis + 8.0 * diag)
    base = to_r + mean
    n_own = on(K_N)
    n = [n_own * c for c in second_order(m)]
    d_own = on(K_D)
    jj_own = on(K_J)
    q_own = on(-K_Q)
    odd = [to_j[a] + jj_own * m["j"][a] for a in range(3)]
    rest_own = jnp.where(fluid, -0.4, jnp.where(solid, 1.0, 0.0))
    base_axis = base - 11.0 * ef
    base_diag = base + 8.0 * ef
    out_f = assemble(
        rest_own * f0 + base - 30.0 * ef,
        [base_axis + n[a] for a in range(3)],
        [base_diag - n[a] for a in range(3)],
        [d_own * c for c in m["cross"]],
        odd,
        odd,
        [q_own * c for c in m["q"]],
        pe,
        po,
        m,
    )
    to_s = to_s + on(mean_h)
    out_h = [jnp.where(fluid, 1.0 - RATE_E, jnp.where(solid, 1.0, 0.0)) * mu[0] + to_s]
    for a in range(3):
        even = he * me[a] + to_s
        odd = ho * mo[a]
        out_h += [even + odd, even - odd]
    return out_f + out_h, sens


class Stream:
    def __init__(self, heading, fields):
        self.heading = heading
        self.fields = fields
        self.vel = [tuple(heading * c for c in v) for v in VEL]
        plus = [i for i in range(CH) if self.vel[i][0] == 1]
        minus = [i for i in range(CH) if self.vel[i][0] == -1]
        still = [i for i in range(CH) if self.vel[i][0] == 0]
        order = [(k, i) for group in (plus, minus, still) for k in range(fields) for i in group]
        self.place = {key: at for at, key in enumerate(order)}
        self.face = len(plus) * fields
        self.z_place = {}
        self.edge = {}
        for sign in (1, -1):
            group = [i for i in range(CH) if self.vel[i][2] == sign]
            group.sort(key=lambda i: -abs(self.vel[i][0]))
            keys = [(k, i) for i in group for k in range(fields)]
            self.z_count = len(keys)
            for at, key in enumerate(keys):
                self.z_place[key] = (0 if sign == 1 else 1, at)
            for at, i in enumerate(group[:2]):
                self.edge[(self.vel[i][0], sign)] = at * fields

    def scratch(self):
        return [
            pltpu.VMEM((CH * self.fields, PLANES + 2, ROWS, LANES), F32),
            pltpu.VMEM((2, self.z_count, PLANES, 1, LANES), F32),
            pltpu.VMEM((2, self.z_count, PLANES + 2, 1, LANES), F32),
            pltpu.SemaphoreType.DMA((8,)),
            pltpu.SemaphoreType.DMA((8,)),
        ]

    def put(self, refs, x, field, values):
        padded, rows = refs[0], refs[1]
        for i, value in enumerate(values):
            _, vy, vz = self.vel[i]
            if vy:
                value = pltpu.roll(value, vy % LANES, 1)
            padded[self.place[(field, i)], x + 1] = value
            if vz:
                side, at = self.z_place[(field, i)]
                row = ROWS - 1 if vz == 1 else 0
                rows[side, at, x] = value[row : row + 1, :]

    def copies(self, refs, gx, gz, n_gx, n_gz):
        padded, rows, halo, send, recv = refs
        found = []
        for at, (dx, dz) in enumerate(NEIGHBOURS):
            target = (lax.rem(gx + dx + n_gx, n_gx), lax.rem(gz + dz + n_gz, n_gz))
            side = 0 if dz == 1 else 1
            if dz == 0:
                start = 0 if dx == 1 else self.face
                source = padded.at[pl.ds(start, self.face), PLANES if dx == 1 else 1]
                landing = padded.at[pl.ds(start, self.face), 0 if dx == 1 else PLANES + 1]
            elif dx == 0:
                source = rows.at[side]
                landing = halo.at[side, :, pl.ds(1, PLANES)]
            else:
                start = self.edge[(dx, dz)]
                source = rows.at[side, pl.ds(start, self.fields), PLANES - 1 if dx == 1 else 0]
                landing = halo.at[side, pl.ds(start, self.fields), 0 if dx == 1 else PLANES + 1]
            found.append(
                pltpu.make_async_remote_copy(
                    src_ref=source,
                    dst_ref=landing,
                    send_sem=send.at[at],
                    recv_sem=recv.at[at],
                    device_id=target,
                    device_id_type=MESH,
                )
            )
        return found

    def get(self, refs, x, field):
        padded, halo = refs[0], refs[2]
        row = lax.broadcasted_iota(jnp.int32, (ROWS, LANES), 0)
        values = []
        for i in range(CH):
            vx, _, vz = self.vel[i]
            value = padded[self.place[(field, i)], x + 1 - vx]
            if vz:
                side, at = self.z_place[(field, i)]
                edge = 0 if vz == 1 else ROWS - 1
                value = jnp.where(
                    row == edge, halo[side, at, x + 1 - vx], pltpu.roll(value, vz % ROWS, 0)
                )
            values.append(value)
        return values


OPPOSITE = [VEL.index(tuple(-c for c in v)) for v in VEL[:19]]
OPPOSITE += [19 + k for k in OPPOSITE[:7]]
FORWARD = Stream(1, 3)
BACKWARD = Stream(-1, 1)


def kernel(n_gx, n_gz, *refs):
    (checkpoint, adjoint_end, porosity, node_type, inlet_index, inlet_conc) = refs[:6]
    (out_ref, grad_ref, sum_ref) = refs[6:9]
    (cp, ae, por, kind, feed, conc, sens, in_sem) = refs[9:17]
    forward, back = refs[17:22], refs[22:27]
    (mine_a, got_a, mine_b, got_b, total_row, got_c, got_r, red_send, red_recv) = refs[27:]
    gx, gz = lax.axis_index("gx"), lax.axis_index("gz")
    n_column, n_sheet = n_gx // 2, 2 * n_gz
    x_lo, column_at = gx // n_column, lax.rem(gx, n_column)
    z, core = column_at // 2, lax.rem(column_at, 2)
    x_hi, y = gz // (n_gz // 2), lax.rem(gz, n_gz // 2)

    n_z = n_column // 2
    lower = z < n_z // 2
    upper = jnp.logical_not(lower)
    hub = jnp.logical_and(lower, core == HUB_CORE)
    lower_only = jnp.logical_and(lower, core != HUB_CORE)
    last_hub = jnp.logical_and(hub, z == n_z // 2 - 1)
    next_hub = jnp.logical_and(hub, z == n_z // 2 - 2)

    root = jnp.logical_and(gx == HUB_CORE, gz == 0)
    not_root = jnp.logical_not(root)
    root_at = (HUB_CORE, 0)

    def column(at_z, at_core):
        return (x_lo * n_column + 2 * at_z + at_core, gz)

    n_y = n_gz // 2

    def sheet(lo, hi, at_y, at_core):
        to_gz = lax.rem(x_hi + hi, 2) * n_y + at_y
        return (lax.rem(x_lo + lo, 2) * n_column + 2 * z + at_core, to_gz)

    rows = [*reversed(range(n_y // 2)), *reversed(range(n_y // 2, n_y))]
    around = [(lo, hi, k, c) for k in rows for hi in (1, 0) for lo in (1, 0) for c in (1 - HUB_CORE, HUB_CORE)]

    def each_of(offsets, act):
        for lo, hi, k, c in offsets:
            if lo or hi or c != HUB_CORE:
                act(sheet(lo, hi, k, c))
            else:

                @pl.when(y != k)
                def _():
                    act(sheet(lo, hi, k, c))

    to_hubs = [o for o in around if o[3] == HUB_CORE]
    column_hubs = [(k, HUB_CORE) for k in range(n_z // 2)]
    fourth = [(k, c) for k in range(3 * n_z // 4, n_z) for c in range(2)]
    third = [(k, c) for k in range(n_z // 2, 3 * n_z // 4) for c in range(2)]

    barrier = pltpu.get_barrier_semaphore()

    def greet(target):
        pl.semaphore_signal(barrier, inc=1, device_id=target, device_id_type=MESH)

    def neighbour(dx, dz):
        return (lax.rem(gx + dx + n_gx, n_gx), lax.rem(gz + dz + n_gz, n_gz))

    for dx, dz in NEIGHBOURS:
        greet(neighbour(dx, dz))

    loads = [
        pltpu.make_async_copy(source, target, in_sem.at[k])
        for k, (source, target) in enumerate(
            (
                (checkpoint, cp),
                (porosity, por),
                (node_type, kind),
                (inlet_index, feed),
                (inlet_conc, conc),
                (adjoint_end, ae),
            )
        )
    ]
    for load in loads:
        load.start()

    @pl.when(upper)
    def _():
        greet(column(n_z // 2 - jnp.where(z < 3 * n_z // 4, 1, 2), HUB_CORE))

    @pl.when(lower_only)
    def _():
        for offset in to_hubs:
            greet(sheet(*offset))

    @pl.when(jnp.logical_and(hub, not_root))
    def _():
        each_of(to_hubs, greet)

    @pl.when(hub)
    def _():
        greet(column(z, 1 - HUB_CORE))
        for k in range(1, n_z):
            for c in range(2):
                greet(column(lax.rem(z + k, n_z), c))

    @pl.when(root)
    def _():
        @pl.loop(0, n_gx)
        def _(k):
            to_gx = lax.rem(k, 2) * n_column + n_column - 1 - k // 2
            for to_gz in range(n_gz):
                if to_gz:
                    greet((to_gx, to_gz))
                else:

                    @pl.when(to_gx != HUB_CORE)
                    def _():
                        greet((to_gx, to_gz))

    for load in loads[:5]:
        load.wait()

    def start_plane(x, carry):
        level = jnp.where(feed[x] == 0, conc[0], jnp.where(feed[x] == 1, conc[1], 0.0))
        post, slope = collide([cp[i, x] for i in range(CH)], por[x], kind[x], level)
        FORWARD.put(forward, x, 0, post)
        FORWARD.put(forward, x, 1, slope)
        return carry

    lax.fori_loop(0, PLANES, start_plane, 0, unroll=True)
    loads[5].wait()

    def end_plane(x, carry):
        FORWARD.put(forward, x, 2, [ae[i, x] for i in OPPOSITE])
        return carry

    lax.fori_loop(0, PLANES, end_plane, 0, unroll=True)

    hub_sends = len(column_hubs) - 1 + len(around) - 1
    awaited = len(NEIGHBOURS) + jnp.where(hub, hub_sends, len(column_hubs))
    awaited += jnp.where(root, 0, 1) - jnp.where(jnp.logical_and(jnp.logical_and(hub, z == 0), not_root), 1, 0)
    awaited += jnp.where(next_hub, len(fourth), 0) + jnp.where(last_hub, len(third), 0)
    pl.semaphore_wait(barrier, awaited)
    first = FORWARD.copies(forward, gx, gz, n_gx, n_gz)
    for copy in first:
        copy.start()
    for copy in first:
        copy.wait_recv()

    def mid_plane(x, total):
        state = FORWARD.get(forward, x, 0)
        slope = FORWARD.get(forward, x, 1)
        mirrored = FORWARD.get(forward, x, 2)
        carried = [mirrored[i] for i in OPPOSITE]
        adjoint, sens_mid = transposed(state, carried, por[x], kind[x])
        sens[x] = sens_mid
        BACKWARD.put(back, x, 0, adjoint)
        sums = [a * b for a, b in zip(adjoint, slope)] + [sens_mid, total]
        while len(sums) > 1:
            sums = [a + b for a, b in zip(sums[::2], sums[1::2])] + sums[len(sums) & ~1 :]
        return sums[0]

    total = lax.fori_loop(0, PLANES, mid_plane, jnp.zeros((ROWS, LANES), F32), unroll=True)

    def reduce_copy(stage, mine, got, slot, target):
        return pltpu.make_async_remote_copy(
            src_ref=mine,
            dst_ref=got.at[slot],
            send_sem=red_send.at[stage],
            recv_sem=red_recv.at[stage],
            device_id=target,
            device_id_type=MESH,
        )

    def wait_for(semaphore, got, count):
        pltpu.make_async_copy(got.at[pl.ds(0, count)], got.at[pl.ds(0, count)], semaphore).wait()

    mine_a[...] = jnp.sum(total, axis=0, keepdims=True)
    @pl.when(not_root)
    def _():
        reduce_copy(3, mine_a, got_r, pl.ds(gx * n_gz + gz, 1), root_at).start()

    for k, c in column_hubs:

        @pl.when(jnp.logical_not(jnp.logical_and(hub, z == k)))
        def _():
            reduce_copy(0, mine_a, got_a, column_at, column(k, c)).start()

    second = BACKWARD.copies(back, gx, gz, n_gx, n_gz)
    for copy in second:
        copy.start()

    sheet_at = x_lo * n_gz + gz

    def send_sheet(target):
        copy = reduce_copy(1, mine_b, got_b, sheet_at, target)

        @pl.when(jnp.logical_or(target[0] != HUB_CORE, target[1] != 0))
        def _():
            copy.start()

    @pl.when(hub)
    def _():
        wait_for(red_recv.at[0], got_a, n_column - 1)
        got_a[column_at] = mine_a[...]
        mine_b[...] = jnp.sum(got_a[...], axis=0)
        each_of(around, send_sheet)
        got_b[sheet_at] = mine_b[...]

    for copy in second:
        copy.wait_recv()

    def last_plane(x, carry):
        state = [cp[i, x] for i in range(CH)]
        carried = BACKWARD.get(back, x, 0)
        adjoint, sens_start = transposed(state, carried, por[x], kind[x])
        for i in range(CH):
            out_ref[i, x] = adjoint[i]
        grad_ref[x] = sens_start + sens[x]
        return carry

    lax.fori_loop(0, PLANES, last_plane, 0, unroll=True)

    for copy in first + second:
        copy.wait_send()

    @pl.when(jnp.logical_and(hub, not_root))
    def _():
        wait_for(red_recv.at[1], got_b, n_sheet - 1)

    @pl.when(lower_only)
    def _():
        wait_for(red_recv.at[1], got_b, n_sheet)

    @pl.when(jnp.logical_and(lower, not_root))
    def _():
        total_row[...] = jnp.sum(got_b[...], axis=0)
        sum_ref[...] = total_row[...]

    @pl.when(root)
    def _():
        wait_for(red_recv.at[3], got_r, n_gx * n_gz - 1)
        got_r[pl.ds(HUB_CORE * n_gz, 1), :] = mine_a[...]
        total_row[...] = jnp.sum(got_r[...], axis=0, keepdims=True)
        sum_ref[...] = total_row[...]

    for is_hub, targets in ((next_hub, fourth), (last_hub, third)):

        @pl.when(is_hub)
        def _():
            for k, c in targets:
                reduce_copy(2, total_row, got_c, 0, column(k, c)).start()
            wait_for(red_send.at[2], got_b, len(targets))

    @pl.when(upper)
    def _():
        wait_for(red_recv.at[2], got_c, 1)
        sum_ref[...] = got_c[0]

    @pl.when(hub)
    def _():
        wait_for(red_send.at[0], got_a, len(column_hubs) - 1)
        wait_for(red_send.at[1], got_b, n_sheet - 2)
        wait_for(red_send.at[1], got_b, n_sheet)

    @pl.when(jnp.logical_and(hub, jnp.logical_or(root, z != 0)))
    def _():
        wait_for(red_send.at[1], got_b, 1)

    @pl.when(not_root)
    def _():
        wait_for(red_send.at[3], got_r, 1)

    @pl.when(jnp.logical_not(hub))
    def _():
        wait_for(red_send.at[0], got_a, len(column_hubs))


def finish(adjoint, grad, row, out_ref, grad_ref, total_ref, held, sems):
    copies = [
        pltpu.make_async_copy(adjoint, out_ref, sems.at[0]),
        pltpu.make_async_copy(grad, grad_ref, sems.at[1]),
        pltpu.make_async_copy(held, total_ref, sems.at[2]),
    ]
    copies[0].start()
    copies[1].start()
    held[...] = jnp.sum(row[...], axis=1, keepdims=True)
    copies[2].start()
    for copy in copies:
        copy.wait()


def solution(mesh):
    n_gx, n_gz = mesh.shape["gx"], mesh.shape["gz"]
    block = (PLANES, ROWS, LANES)
    any_space = pl.BlockSpec(memory_space=pl.ANY)
    in_vmem = pl.BlockSpec(memory_space=pltpu.VMEM)

    def on_device(*args):
        args = [pltpu.with_memory_space_constraint(a, pltpu.HBM) for a in args]
        held = pl.pallas_call(
            lambda *refs: kernel(n_gx, n_gz, *refs),
            out_shape=(
                pltpu.VMEM((CH,) + block, F32),
                pltpu.VMEM(block, F32),
                pltpu.VMEM((1, LANES), F32),
            ),
            in_specs=[any_space] * 6,
            out_specs=(in_vmem, in_vmem, in_vmem),
            scratch_shapes=[
                pltpu.VMEM((CH,) + block, F32),
                pltpu.VMEM((CH,) + block, F32),
                pltpu.VMEM(block, F32),
                pltpu.VMEM(block, jnp.int32),
                pltpu.VMEM(block, jnp.int32),
                pltpu.SMEM((2,), F32),
                pltpu.VMEM(block, F32),
                pltpu.SemaphoreType.DMA((6,)),
            ]
            + FORWARD.scratch()
            + BACKWARD.scratch()
            + [
                pltpu.VMEM((1, LANES), F32),
                pltpu.VMEM((n_gx // 2, 1, LANES), F32),
                pltpu.VMEM((1, LANES), F32),
                pltpu.VMEM((2 * n_gz, 1, LANES), F32),
                pltpu.VMEM((1, LANES), F32),
                pltpu.VMEM((1, 1, LANES), F32),
                pltpu.VMEM((n_gx * n_gz, LANES), F32),
                pltpu.SemaphoreType.DMA((4,)),
                pltpu.SemaphoreType.DMA((4,)),
            ],
            compiler_params=pltpu.CompilerParams(
                collective_id=0, has_side_effects=True, vmem_limit_bytes=32 * 1024 * 1024
            ),
        )(*args)
        held = [pltpu.with_memory_space_constraint(a, pltpu.VMEM) for a in held]
        adjoint, grad, total = pl.pallas_call(
            finish,
            out_shape=(
                jax.ShapeDtypeStruct((CH,) + block, F32),
                jax.ShapeDtypeStruct(block, F32),
                jax.ShapeDtypeStruct((1, 1), F32),
            ),
            in_specs=[in_vmem, in_vmem, in_vmem],
            out_specs=(any_space, any_space, any_space),
            scratch_shapes=[pltpu.VMEM((1, 1), F32), pltpu.SemaphoreType.DMA((3,))],
        )(*held)
        return adjoint, grad, total.reshape(())

    return jax.shard_map(
        on_device,
        mesh=mesh,
        in_specs=(
            P(None, "gx", "gz", None),
            P(None, "gx", "gz", None),
            P("gx", "gz", None),
            P("gx", "gz", None),
            P("gx", "gz", None),
            P(),
        ),
        out_specs=(P(None, "gx", "gz", None), P("gx", "gz", None), P()),
        check_vma=False,
    )
```

```python
import jax
import jax.numpy as jnp
from jax import lax
from jax.experimental import pallas as pl
from jax.experimental.pallas import tpu as pltpu
from jax.sharding import PartitionSpec as P

MESH = pl.DeviceIdType.MESH
F32 = jnp.float32

VEL = [
    (0, 0, 0),
    (1, 0, 0),
    (-1, 0, 0),
    (0, 1, 0),
    (0, -1, 0),
    (0, 0, 1),
    (0, 0, -1),
    (1, 1, 0),
    (-1, -1, 0),
    (1, -1, 0),
    (-1, 1, 0),
    (1, 0, 1),
    (-1, 0, -1),
    (1, 0, -1),
    (-1, 0, 1),
    (0, 1, 1),
    (0, -1, -1),
    (0, 1, -1),
    (0, -1, 1),
]
VEL = VEL + VEL[:7]
CH = 26
PLANES = 4
ROWS = 8
LANES = 128

NEIGHBOURS = ((1, 0), (-1, 0), (1, 1), (1, -1), (-1, 1), (-1, -1), (0, 1), (0, -1))

HUB_CORE = 1

BRINKMAN = 4.0
SPEED = 0.05
RATE_H = 1.0 / 0.7
RATE_E = 1.5

E_NORM = 2394.0
FLUID_P, FLUID_Q = -0.2, -0.1
K_MEAN = 1.4 / 19.0
K_E = (1.4 - 1.19) / E_NORM
K_N = 0.15 / 18.0
K_D = 0.15 / 4.0
K_J = 0.2 / 10.0
K_Q = 0.78 / 8.0


def moments(f):
    e = [f[a] + f[a + 1] for a in range(1, 19, 2)]
    o = [f[a] - f[a + 1] for a in range(1, 19, 2)]
    sxy, txy = o[3] + o[4], o[3] - o[4]
    sxz, txz = o[5] + o[6], o[5] - o[6]
    syz, tyz = o[7] + o[8], o[7] - o[8]
    exy, dxy = e[3] + e[4], e[3] - e[4]
    exz, dxz = e[5] + e[6], e[5] - e[6]
    eyz, dyz = e[7] + e[8], e[7] - e[8]
    axis_sum = e[0] + e[1] + e[2]
    diag_sum = exy + exz + eyz
    return dict(
        e=e,
        o=o,
        f0=f[0],
        axis=axis_sum,
        diag=diag_sum,
        across=(eyz, exz, exy),
        cross=(dxy, dxz, dyz),
        j=(o[0] + sxy + sxz, o[1] + txy + syz, o[2] + txz + tyz),
        q=(sxy - sxz, syz - txy, txz - tyz),
    )


def density_velocity(m):
    r = m["f0"] + m["axis"] + m["diag"]
    inverse = 1.0 / r
    return r, inverse, [j * inverse for j in m["j"]]


def second_order(m):
    shift = m["axis"] - m["diag"]
    return [3.0 * (m["e"][a] - m["across"][a]) - shift for a in range(3)]


def assemble(even_rest, even_axis, even_diag, cross, odd_axis, odd_diag, third, pe, po, m):
    out = [even_rest]
    for a in range(3):
        even = pe * m["e"][a] + even_axis[a]
        odd = po * m["o"][a] + odd_axis[a]
        out += [even + odd, even - odd]
    x, y, z = odd_diag
    qx, qy, qz = third
    xy_x, xy_y = x + qx, y - qy
    xz_x, xz_z = x - qx, z + qz
    yz_y, yz_z = y + qy, z - qz
    odds = [xy_x + xy_y, xy_x - xy_y, xz_x + xz_z, xz_x - xz_z, yz_y + yz_z, yz_y - yz_z]
    for k in range(6):
        base = even_diag[2 - k // 2]
        base = base + cross[k // 2] if k % 2 == 0 else base - cross[k // 2]
        even = pe * m["e"][3 + k] + base
        odd = po * m["o"][3 + k] + odds[k]
        out += [even + odd, even - odd]
    return out


def cell_kinds(kind):
    return kind == 0, kind == 1, kind == 2, kind == 3


def relax_factors(kind):
    fluid, solid, _, _ = cell_kinds(kind)
    pe = jnp.where(fluid, FLUID_P, jnp.where(solid, 0.5, 0.0))
    po = jnp.where(fluid, FLUID_Q, jnp.where(solid, -0.5, 0.0))
    he = jnp.where(fluid, 0.5 - RATE_E / 2, jnp.where(solid, 0.5, 0.0))
    ho = jnp.where(fluid, 0.5 - RATE_H / 2, jnp.where(solid, -0.5, 0.0))
    return pe, po, he, ho


def damping_of(porosity):
    return 1.0 / (1.0 + BRINKMAN * (1.0 - porosity))


def dot3(a, b):
    return a[0] * b[0] + a[1] * b[1] + a[2] * b[2]


def collide(pops, porosity, kind, level):
    fluid, solid, inlet, outlet = cell_kinds(kind)
    pe, po, he, ho = relax_factors(kind)
    f, h = pops[:19], pops[19:]
    m = moments(f)
    r, _, u = density_velocity(m)
    d = damping_of(porosity)
    d_eff = jnp.where(outlet, 1.0, d)
    b = [c * d_eff for c in u]
    zero = jnp.zeros_like(r)

    def on(value):
        return jnp.where(fluid, value, 0.0)

    def pick(at_fluid, elsewhere):
        return jnp.where(fluid, at_fluid, jnp.where(solid, 0.0, elsewhere))

    re = jnp.where(inlet, 1.0, r)
    be = [
        jnp.where(inlet, SPEED, b[0]),
        jnp.where(inlet, 0.0, b[1]),
        jnp.where(inlet, 0.0, b[2]),
    ]
    rb = [re * c for c in be]
    bb = [p * c for p, c in zip(rb, be)]
    b2 = bb[0] + bb[1] + bb[2]
    crossed = (rb[0] * be[1], rb[0] * be[2], rb[1] * be[2])
    quad_rest = pick(-0.65, -0.5) * b2
    axis_all = pick(-0.09, -1.0 / 12.0) * b2
    axis_own = pick(0.325, 0.25)
    quad_axis = [axis_all + axis_own * c for c in bb]
    diag_all = pick(0.095, 1.0 / 12.0) * b2
    diag_own = pick(-0.15, -0.125)
    quad_diag = [diag_all + diag_own * c for c in bb]
    cross_own = pick(0.3125, 0.25)
    quad_cross = [cross_own * c for c in crossed]
    lin_axis_own = pick(0.18, 1.0 / 6.0)
    lin_diag_own = pick(0.08, 1.0 / 12.0)
    lin_axis = [lin_axis_own * c for c in rb]
    lin_diag = [lin_diag_own * c for c in rb]
    n = second_order(m)
    e_f = -30.0 * m["f0"] - 11.0 * m["axis"] + 8.0 * m["diag"]
    de = K_E * (e_f + 11.0 * r)
    even_rest = jnp.where(fluid, 1.4 / 3.0 * r - 30.0 * de, pick(0.0, 1.0 / 3.0) * re)
    even_axis = jnp.where(fluid, 1.4 / 18.0 * r - 11.0 * de, pick(0.0, 1.0 / 18.0) * re)
    even_diag = jnp.where(fluid, 1.4 / 36.0 * r + 8.0 * de, pick(0.0, 1.0 / 36.0) * re)
    rest_own = jnp.where(fluid, -0.4, jnp.where(solid, 1.0, 0.0))
    n_own = on(K_N)
    n = [n_own * c for c in n]
    d_own = on(K_D)
    j_own = on(K_J)
    q_own = on(-K_Q)
    jj = [j_own * c for c in m["j"]]
    new_f = assemble(
        rest_own * m["f0"] + even_rest + quad_rest,
        [even_axis + quad_axis[a] + n[a] for a in range(3)],
        [even_diag + quad_diag[a] - n[a] for a in range(3)],
        [quad_cross[k] + d_own * m["cross"][k] for k in range(3)],
        [lin_axis[a] + jj[a] for a in range(3)],
        [lin_diag[a] + jj[a] for a in range(3)],
        [q_own * c for c in m["q"]],
        pe,
        po,
        m,
    )
    kappa = on(BRINKMAN * d)
    kappa2 = kappa + kappa
    g_rest = kappa2 * quad_rest
    g_axis = [kappa2 * c for c in quad_axis]
    g_diag = [kappa2 * c for c in quad_diag]
    g_cross = [kappa2 * c for c in quad_cross]
    g_la = [kappa * c for c in lin_axis]
    g_ld = [kappa * c for c in lin_diag]
    g_f = [g_rest]
    for a in range(3):
        g_f += [g_axis[a] + g_la[a], g_axis[a] - g_la[a]]
    x, y, z = g_ld
    odds = [x + y, x - y, x + z, x - z, y + z, y - z]
    for k in range(6):
        even = g_diag[2 - k // 2]
        even = even + g_cross[k // 2] if k % 2 == 0 else even - g_cross[k // 2]
        g_f += [even + odds[k], even - odds[k]]
    he_pairs = [h[a] + h[a + 1] for a in (1, 3, 5)]
    ho_pairs = [h[a] - h[a + 1] for a in (1, 3, 5)]
    s = h[0] + he_pairs[0] + he_pairs[1] + he_pairs[2]
    se = jnp.where(inlet, level, s)
    s_even = pick(RATE_E, 1.0) * se
    s_odd = pick(0.5 * RATE_H, 0.5) * se
    new_h = [jnp.where(fluid, 1.0 - RATE_E, jnp.where(solid, 1.0, 0.0)) * h[0] + 0.25 * s_even]
    g_h = [zero]
    for a in range(3):
        even = he * he_pairs[a] + 0.125 * s_even
        push = s_odd * be[a]
        odd = ho * ho_pairs[a] + push
        new_h += [even + odd, even - odd]
        push = kappa * push
        g_h += [push, -push]
    return new_f + new_h, g_f + g_h


def weighted_factors(a, b, own):
    return (
        own[0] - a * K_MEAN + 30.0 * b * K_E,
        own[1] - a * K_MEAN + 11.0 * b * K_E,
        own[2] - a * K_MEAN - 8.0 * b * K_E,
    )


A0_F = weighted_factors(1.0, -11.0, (1.4 / 3.0, 1.4 / 18.0, 1.4 / 36.0))
A2_F = weighted_factors(1.0 / 3.0, 5.0 / 9.0, (0.0, 1.0 / 540.0, 1.4 / 36.0 - 1.0 / 540.0))


def transposed(pops, carried, porosity, kind):
    fluid, solid, inlet, outlet = cell_kinds(kind)
    pe, po, he, ho = relax_factors(kind)
    f, h = pops[:19], pops[19:]
    ms = moments(f)
    r, inverse, u = density_velocity(ms)
    s = h[0] + (h[1] + h[2]) + (h[3] + h[4]) + (h[5] + h[6])
    d = jnp.where(outlet, 1.0, damping_of(porosity))
    b = [c * d for c in u]
    ratio4 = 4.0 * s * inverse

    m = moments(carried[:19])
    mu = carried[19:]
    f0, axis, diag = m["f0"], m["axis"], m["diag"]

    def pick(at_fluid, at_outlet):
        return jnp.where(fluid, at_fluid, at_outlet)

    a0 = (
        pick(A0_F[0], 1.0 / 3.0) * f0
        + pick(A0_F[1], 1.0 / 18.0) * axis
        + pick(A0_F[2], 1.0 / 36.0) * diag
    )
    common = (
        pick(A2_F[0], 0.0) * f0 + pick(A2_F[1], 0.0) * axis + pick(A2_F[2], 1.0 / 36.0) * diag
    )
    own = pick(1.4 / 18.0 - 3.0 / 540.0, 1.0 / 18.0)
    away = pick(-1.4 / 36.0 + 3.0 / 540.0, -1.0 / 36.0)
    a2 = [own * m["e"][a] + away * m["across"][a] + common for a in range(3)]
    cross_own = pick(1.25 / 36.0, 1.0 / 36.0)
    axy, axz, ayz = [cross_own * c for c in m["cross"]]
    o_own = pick(1.0 / 30.0, 1.0 / 36.0)
    j_own = pick(0.96 / 36.0, 1.0 / 36.0)
    a1 = [o_own * m["o"][a] + j_own * m["j"][a] for a in range(3)]
    me = [mu[a] + mu[a + 1] for a in (1, 3, 5)]
    mo = [mu[a] - mu[a + 1] for a in (1, 3, 5)]
    me_sum = me[0] + me[1] + me[2]
    mean_h = (RATE_E / 7.0) * (mu[0] + me_sum)
    b0 = pick(RATE_E, 1.0) * (0.25 * mu[0] + 0.125 * me_sum) - pick(mean_h, 0.0)
    b1_own = pick(0.125 * RATE_H, 0.125)
    b1 = [b1_own * c for c in mo]

    ab = [
        a2[0] * b[0] + axy * b[1] + axz * b[2],
        axy * b[0] + a2[1] * b[1] + ayz * b[2],
        axz * b[0] + ayz * b[1] + a2[2] * b[2],
    ]
    curved = [9.0 * ab[a] - 3.0 * a0 * b[a] for a in range(3)]
    b1b = dot3(b1, b)
    total = [3.0 * a1[a] + curved[a] + ratio4 * b1[a] for a in range(3)]
    to_r = a0 - 0.5 * dot3(b, curved) - ratio4 * b1b
    to_s = b0 + 4.0 * b1b
    sens = jnp.where(fluid, BRINKMAN * d * d * dot3(ms["j"], total), 0.0)

    active = jnp.logical_or(fluid, outlet)
    d_on = jnp.where(active, d, 0.0)
    to_r = jnp.where(active, to_r, 0.0)
    to_s = jnp.where(active, to_s, 0.0)
    to_j = [d_on * c for c in total]

    def on(value):
        return jnp.where(fluid, value, 0.0)

    mean = on(K_MEAN) * (f0 + axis + diag)
    ef = on(K_E) * (-30.0 * f0 - 11.0 * axis + 8.0 * diag)
    base = to_r + mean
    n_own = on(K_N)
    n = [n_own * c for c in second_order(m)]
    d_own = on(K_D)
    jj_own = on(K_J)
    q_own = on(-K_Q)
    odd = [to_j[a] + jj_own * m["j"][a] for a in range(3)]
    rest_own = jnp.where(fluid, -0.4, jnp.where(solid, 1.0, 0.0))
    base_axis = base - 11.0 * ef
    base_diag = base + 8.0 * ef
    out_f = assemble(
        rest_own * f0 + base - 30.0 * ef,
        [base_axis + n[a] for a in range(3)],
        [base_diag - n[a] for a in range(3)],
        [d_own * c for c in m["cross"]],
        odd,
        odd,
        [q_own * c for c in m["q"]],
        pe,
        po,
        m,
    )
    to_s = to_s + on(mean_h)
    out_h = [jnp.where(fluid, 1.0 - RATE_E, jnp.where(solid, 1.0, 0.0)) * mu[0] + to_s]
    for a in range(3):
        even = he * me[a] + to_s
        odd = ho * mo[a]
        out_h += [even + odd, even - odd]
    return out_f + out_h, sens


class Stream:
    def __init__(self, heading, fields):
        self.heading = heading
        self.fields = fields
        self.vel = [tuple(heading * c for c in v) for v in VEL]
        plus = [i for i in range(CH) if self.vel[i][0] == 1]
        minus = [i for i in range(CH) if self.vel[i][0] == -1]
        still = [i for i in range(CH) if self.vel[i][0] == 0]
        order = [(k, i) for group in (plus, minus, still) for k in range(fields) for i in group]
        self.place = {key: at for at, key in enumerate(order)}
        self.face = len(plus) * fields
        self.z_place = {}
        self.edge = {}
        for sign in (1, -1):
            group = [i for i in range(CH) if self.vel[i][2] == sign]
            group.sort(key=lambda i: -abs(self.vel[i][0]))
            keys = [(k, i) for i in group for k in range(fields)]
            self.z_count = len(keys)
            for at, key in enumerate(keys):
                self.z_place[key] = (0 if sign == 1 else 1, at)
            for at, i in enumerate(group[:2]):
                self.edge[(self.vel[i][0], sign)] = at * fields

    def scratch(self):
        return [
            pltpu.VMEM((CH * self.fields, PLANES + 2, ROWS, LANES), F32),
            pltpu.VMEM((2, self.z_count, PLANES, 1, LANES), F32),
            pltpu.VMEM((2, self.z_count, PLANES + 2, 1, LANES), F32),
            pltpu.SemaphoreType.DMA((8,)),
            pltpu.SemaphoreType.DMA((8,)),
        ]

    def put(self, refs, x, field, values):
        padded, rows = refs[0], refs[1]
        for i, value in enumerate(values):
            _, vy, vz = self.vel[i]
            if vy:
                value = pltpu.roll(value, vy % LANES, 1)
            padded[self.place[(field, i)], x + 1] = value
            if vz:
                side, at = self.z_place[(field, i)]
                row = ROWS - 1 if vz == 1 else 0
                rows[side, at, x] = value[row : row + 1, :]

    def copies(self, refs, gx, gz, n_gx, n_gz):
        padded, rows, halo, send, recv = refs
        found = []
        for at, (dx, dz) in enumerate(NEIGHBOURS):
            target = (lax.rem(gx + dx + n_gx, n_gx), lax.rem(gz + dz + n_gz, n_gz))
            side = 0 if dz == 1 else 1
            if dz == 0:
                start = 0 if dx == 1 else self.face
                source = padded.at[pl.ds(start, self.face), PLANES if dx == 1 else 1]
                landing = padded.at[pl.ds(start, self.face), 0 if dx == 1 else PLANES + 1]
            elif dx == 0:
                source = rows.at[side]
                landing = halo.at[side, :, pl.ds(1, PLANES)]
            else:
                start = self.edge[(dx, dz)]
                source = rows.at[side, pl.ds(start, self.fields), PLANES - 1 if dx == 1 else 0]
                landing = halo.at[side, pl.ds(start, self.fields), 0 if dx == 1 else PLANES + 1]
            found.append(
                pltpu.make_async_remote_copy(
                    src_ref=source,
                    dst_ref=landing,
                    send_sem=send.at[at],
                    recv_sem=recv.at[at],
                    device_id=target,
                    device_id_type=MESH,
                )
            )
        return found

    def get(self, refs, x, field):
        padded, halo = refs[0], refs[2]
        row = lax.broadcasted_iota(jnp.int32, (ROWS, LANES), 0)
        values = []
        for i in range(CH):
            vx, _, vz = self.vel[i]
            value = padded[self.place[(field, i)], x + 1 - vx]
            if vz:
                side, at = self.z_place[(field, i)]
                edge = 0 if vz == 1 else ROWS - 1
                value = jnp.where(
                    row == edge, halo[side, at, x + 1 - vx], pltpu.roll(value, vz % ROWS, 0)
                )
            values.append(value)
        return values


OPPOSITE = [VEL.index(tuple(-c for c in v)) for v in VEL[:19]]
OPPOSITE += [19 + k for k in OPPOSITE[:7]]
FORWARD = Stream(1, 3)
BACKWARD = Stream(-1, 1)


def kernel(n_gx, n_gz, *refs):
    (checkpoint, adjoint_end, porosity, node_type, inlet_index, inlet_conc) = refs[:6]
    (out_ref, grad_ref, sum_ref) = refs[6:9]
    (cp, ae, por, kind, feed, conc, sens, in_sem) = refs[9:17]
    forward, back = refs[17:22], refs[22:27]
    (mine_a, got_a, mine_b, got_b, total_row, got_c, got_r, red_send, red_recv) = refs[27:]
    gx, gz = lax.axis_index("gx"), lax.axis_index("gz")
    n_column, n_sheet = n_gx // 2, 2 * n_gz
    x_lo, column_at = gx // n_column, lax.rem(gx, n_column)
    z, core = column_at // 2, lax.rem(column_at, 2)
    x_hi, y = gz // (n_gz // 2), lax.rem(gz, n_gz // 2)

    n_z = n_column // 2
    lower = z < n_z // 2
    upper = jnp.logical_not(lower)
    hub = jnp.logical_and(lower, core == HUB_CORE)
    lower_only = jnp.logical_and(lower, core != HUB_CORE)
    last_hub = jnp.logical_and(hub, z == n_z // 2 - 1)
    next_hub = jnp.logical_and(hub, z == n_z // 2 - 2)

    root = jnp.logical_and(gx == HUB_CORE, gz == 0)
    not_root = jnp.logical_not(root)
    root_at = (HUB_CORE, 0)

    def column(at_z, at_core):
        return (x_lo * n_column + 2 * at_z + at_core, gz)

    n_y = n_gz // 2

    def sheet(lo, hi, at_y, at_core):
        to_gz = lax.rem(x_hi + hi, 2) * n_y + at_y
        return (lax.rem(x_lo + lo, 2) * n_column + 2 * z + at_core, to_gz)

    rows = [*reversed(range(n_y // 2)), *reversed(range(n_y // 2, n_y))]
    around = [(lo, hi, k, c) for k in rows for hi in (1, 0) for lo in (1, 0) for c in (1 - HUB_CORE, HUB_CORE)]

    def each_of(offsets, act):
        for lo, hi, k, c in offsets:
            if lo or hi or c != HUB_CORE:
                act(sheet(lo, hi, k, c))
            else:

                @pl.when(y != k)
                def _():
                    act(sheet(lo, hi, k, c))

    to_hubs = [o for o in around if o[3] == HUB_CORE]
    column_hubs = [(k, HUB_CORE) for k in range(n_z // 2)]
    fourth = [(k, c) for k in range(3 * n_z // 4, n_z) for c in range(2)]
    third = [(k, c) for k in range(n_z // 2, 3 * n_z // 4) for c in range(2)]

    barrier = pltpu.get_barrier_semaphore()

    def greet(target):
        pl.semaphore_signal(barrier, inc=1, device_id=target, device_id_type=MESH)

    def neighbour(dx, dz):
        return (lax.rem(gx + dx + n_gx, n_gx), lax.rem(gz + dz + n_gz, n_gz))

    for dx, dz in NEIGHBOURS:
        greet(neighbour(dx, dz))

    loads = [
        pltpu.make_async_copy(source, target, in_sem.at[k])
        for k, (source, target) in enumerate(
            (
                (checkpoint, cp),
                (porosity, por),
                (node_type, kind),
                (inlet_index, feed),
                (inlet_conc, conc),
                (adjoint_end, ae),
            )
        )
    ]
    for load in loads:
        load.start()

    @pl.when(upper)
    def _():
        greet(column(n_z // 2 - jnp.where(z < 3 * n_z // 4, 1, 2), HUB_CORE))

    @pl.when(lower_only)
    def _():
        for offset in to_hubs:
            greet(sheet(*offset))

    @pl.when(jnp.logical_and(hub, not_root))
    def _():
        each_of(to_hubs, greet)

    @pl.when(hub)
    def _():
        greet(column(z, 1 - HUB_CORE))
        for k in range(1, n_z):
            for c in range(2):
                greet(column(lax.rem(z + k, n_z), c))

    @pl.when(root)
    def _():
        @pl.loop(0, n_gx)
        def _(k):
            to_gx = lax.rem(k, 2) * n_column + n_column - 1 - k // 2
            for to_gz in range(n_gz):
                if to_gz:
                    greet((to_gx, to_gz))
                else:

                    @pl.when(to_gx != HUB_CORE)
                    def _():
                        greet((to_gx, to_gz))

    for load in loads[:5]:
        load.wait()

    def start_plane(x, carry):
        level = jnp.where(feed[x] == 0, conc[0], jnp.where(feed[x] == 1, conc[1], 0.0))
        post, slope = collide([cp[i, x] for i in range(CH)], por[x], kind[x], level)
        FORWARD.put(forward, x, 0, post)
        FORWARD.put(forward, x, 1, slope)
        return carry

    lax.fori_loop(0, PLANES, start_plane, 0, unroll=True)
    loads[5].wait()

    def end_plane(x, carry):
        FORWARD.put(forward, x, 2, [ae[i, x] for i in OPPOSITE])
        return carry

    lax.fori_loop(0, PLANES, end_plane, 0, unroll=True)

    hub_sends = len(column_hubs) - 1 + len(around) - 1
    awaited = len(NEIGHBOURS) + jnp.where(hub, hub_sends, len(column_hubs))
    awaited += jnp.where(root, 0, 1) - jnp.where(jnp.logical_and(jnp.logical_and(hub, z == 0), not_root), 1, 0)
    awaited += jnp.where(next_hub, len(fourth), 0) + jnp.where(last_hub, len(third), 0)
    pl.semaphore_wait(barrier, awaited)
    first = FORWARD.copies(forward, gx, gz, n_gx, n_gz)
    for copy in first:
        copy.start()
    def mid_plane(x, total):
        state = FORWARD.get(forward, x, 0)
        slope = FORWARD.get(forward, x, 1)
        mirrored = FORWARD.get(forward, x, 2)
        carried = [mirrored[i] for i in OPPOSITE]
        adjoint, sens_mid = transposed(state, carried, por[x], kind[x])
        sens[x] = sens_mid
        BACKWARD.put(back, x, 0, adjoint)
        sums = [a * b for a, b in zip(adjoint, slope)] + [sens_mid, total]
        while len(sums) > 1:
            sums = [a + b for a, b in zip(sums[::2], sums[1::2])] + sums[len(sums) & ~1 :]
        return sums[0]

    over_z = [copy for copy, (dx, dz) in zip(first, NEIGHBOURS) if dx == 0]
    over_x = [copy for copy, (dx, dz) in zip(first, NEIGHBOURS) if dx != 0]
    for copy in over_z:
        copy.wait_recv()
    total = jnp.zeros((ROWS, LANES), F32)
    total = lax.fori_loop(0, PLANES - 2, lambda k, t: mid_plane(k + 1, t), total, unroll=True)
    for copy in over_x:
        copy.wait_recv()
    total = lax.fori_loop(0, 2, lambda k, t: mid_plane(k * (PLANES - 1), t), total, unroll=True)

    def reduce_copy(stage, mine, got, slot, target):
        return pltpu.make_async_remote_copy(
            src_ref=mine,
            dst_ref=got.at[slot],
            send_sem=red_send.at[stage],
            recv_sem=red_recv.at[stage],
            device_id=target,
            device_id_type=MESH,
        )

    def wait_for(semaphore, got, count):
        pltpu.make_async_copy(got.at[pl.ds(0, count)], got.at[pl.ds(0, count)], semaphore).wait()

    def in_order(terms):
        sum_of = terms[0]
        for term in terms[1:]:
            sum_of = sum_of + term
        return sum_of

    mine_a[...] = jnp.sum(total, axis=0, keepdims=True)
    sheet_at = x_lo * n_gz + gz

    @pl.when(not_root)
    def _():
        reduce_copy(3, mine_a, got_r, pl.ds(column_at * n_sheet + sheet_at, 1), root_at).start()

    for k, c in column_hubs:

        @pl.when(jnp.logical_not(jnp.logical_and(hub, z == k)))
        def _():
            reduce_copy(0, mine_a, got_a, column_at, column(k, c)).start()

    second = BACKWARD.copies(back, gx, gz, n_gx, n_gz)
    for copy in second:
        copy.start()

    def send_sheet(target):
        reduce_copy(1, mine_b, got_b, pl.ds(sheet_at, 1), target).start()

    def send_unless_root(target):
        @pl.when(jnp.logical_or(target[0] != HUB_CORE, target[1] != 0))
        def _():
            send_sheet(target)

    @pl.when(hub)
    def _():
        wait_for(red_recv.at[0], got_a, n_column - 1)
        got_a[column_at] = mine_a[...]
        mine_b[...] = in_order([got_a[k] for k in range(n_column)])
        may_be_root = [o for o in around if o[2] == 0 and o[3] == HUB_CORE]
        each_of([o for o in around if o not in may_be_root], send_sheet)
        each_of(may_be_root, send_unless_root)
        got_b[pl.ds(sheet_at, 1), :] = mine_b[...]

    for copy in second:
        copy.wait_recv()

    def last_plane(x, carry):
        state = [cp[i, x] for i in range(CH)]
        carried = BACKWARD.get(back, x, 0)
        adjoint, sens_start = transposed(state, carried, por[x], kind[x])
        for i in range(CH):
            out_ref[i, x] = adjoint[i]
        grad_ref[x] = sens_start + sens[x]
        return carry

    lax.fori_loop(0, PLANES, last_plane, 0, unroll=True)

    for copy in first + second:
        copy.wait_send()

    @pl.when(jnp.logical_and(hub, not_root))
    def _():
        wait_for(red_recv.at[1], got_b, n_sheet - 1)

    @pl.when(lower_only)
    def _():
        wait_for(red_recv.at[1], got_b, n_sheet)

    @pl.when(jnp.logical_and(lower, not_root))
    def _():
        total_row[...] = jnp.sum(got_b[...], axis=0, keepdims=True)
        sum_ref[...] = total_row[...]

    @pl.when(root)
    def _():
        wait_for(red_recv.at[3], got_r, n_column * n_sheet - 1)
        got_r[pl.ds(HUB_CORE * n_sheet, 1), :] = mine_a[...]
        sheet_sums = in_order([got_r[pl.ds(k * n_sheet, n_sheet), :] for k in range(n_column)])
        total_row[...] = jnp.sum(sheet_sums, axis=0, keepdims=True)
        sum_ref[...] = total_row[...]

    for is_hub, targets in ((next_hub, fourth), (last_hub, third)):

        @pl.when(is_hub)
        def _():
            for k, c in targets:
                reduce_copy(2, total_row, got_c, 0, column(k, c)).start()
            wait_for(red_send.at[2], got_b, len(targets))

    @pl.when(upper)
    def _():
        wait_for(red_recv.at[2], got_c, 1)
        sum_ref[...] = got_c[0]

    @pl.when(hub)
    def _():
        wait_for(red_send.at[0], got_a, len(column_hubs) - 1)
        wait_for(red_send.at[1], got_b, n_sheet - 2)
        wait_for(red_send.at[1], got_b, n_sheet)

    @pl.when(jnp.logical_and(hub, jnp.logical_or(root, z != 0)))
    def _():
        wait_for(red_send.at[1], got_b, 1)

    @pl.when(not_root)
    def _():
        wait_for(red_send.at[3], got_b, 1)

    @pl.when(jnp.logical_not(hub))
    def _():
        wait_for(red_send.at[0], got_a, len(column_hubs))


def finish(adjoint, grad, row, out_ref, grad_ref, total_ref, held, sems):
    copies = [
        pltpu.make_async_copy(adjoint, out_ref, sems.at[0]),
        pltpu.make_async_copy(grad, grad_ref, sems.at[1]),
        pltpu.make_async_copy(held, total_ref, sems.at[2]),
    ]
    copies[0].start()
    copies[1].start()
    held[...] = jnp.sum(row[...], axis=1, keepdims=True)
    copies[2].start()
    for copy in copies:
        copy.wait()


def solution(mesh):
    n_gx, n_gz = mesh.shape["gx"], mesh.shape["gz"]
    block = (PLANES, ROWS, LANES)
    any_space = pl.BlockSpec(memory_space=pl.ANY)
    in_vmem = pl.BlockSpec(memory_space=pltpu.VMEM)

    def on_device(*args):
        args = [pltpu.with_memory_space_constraint(a, pltpu.HBM) for a in args]
        held = pl.pallas_call(
            lambda *refs: kernel(n_gx, n_gz, *refs),
            out_shape=(
                pltpu.VMEM((CH,) + block, F32),
                pltpu.VMEM(block, F32),
                pltpu.VMEM((1, LANES), F32),
            ),
            in_specs=[any_space] * 6,
            out_specs=(in_vmem, in_vmem, in_vmem),
            scratch_shapes=[
                pltpu.VMEM((CH,) + block, F32),
                pltpu.VMEM((CH,) + block, F32),
                pltpu.VMEM(block, F32),
                pltpu.VMEM(block, jnp.int32),
                pltpu.VMEM(block, jnp.int32),
                pltpu.SMEM((2,), F32),
                pltpu.VMEM(block, F32),
                pltpu.SemaphoreType.DMA((6,)),
            ]
            + FORWARD.scratch()
            + BACKWARD.scratch()
            + [
                pltpu.VMEM((1, LANES), F32),
                pltpu.VMEM((n_gx // 2, 1, LANES), F32),
                pltpu.VMEM((1, LANES), F32),
                pltpu.VMEM((2 * n_gz, LANES), F32),
                pltpu.VMEM((1, LANES), F32),
                pltpu.VMEM((1, 1, LANES), F32),
                pltpu.VMEM((n_gx * n_gz, LANES), F32),
                pltpu.SemaphoreType.DMA((4,)),
                pltpu.SemaphoreType.DMA((4,)),
            ],
            compiler_params=pltpu.CompilerParams(
                collective_id=0, has_side_effects=True, vmem_limit_bytes=32 * 1024 * 1024
            ),
        )(*args)
        held = [pltpu.with_memory_space_constraint(a, pltpu.VMEM) for a in held]
        adjoint, grad, total = pl.pallas_call(
            finish,
            out_shape=(
                jax.ShapeDtypeStruct((CH,) + block, F32),
                jax.ShapeDtypeStruct(block, F32),
                jax.ShapeDtypeStruct((1, 1), F32),
            ),
            in_specs=[in_vmem, in_vmem, in_vmem],
            out_specs=(any_space, any_space, any_space),
            scratch_shapes=[pltpu.VMEM((1, 1), F32), pltpu.SemaphoreType.DMA((3,))],
        )(*held)
        return adjoint, grad, total.reshape(())

    return jax.shard_map(
        on_device,
        mesh=mesh,
        in_specs=(
            P(None, "gx", "gz", None),
            P(None, "gx", "gz", None),
            P("gx", "gz", None),
            P("gx", "gz", None),
            P("gx", "gz", None),
            P(),
        ),
        out_specs=(P(None, "gx", "gz", None), P("gx", "gz", None), P()),
        check_vma=False,
    )
```

```python
import jax
import jax.numpy as jnp
from jax import lax
from jax.experimental import pallas as pl
from jax.experimental.pallas import tpu as pltpu
from jax.sharding import PartitionSpec as P

MESH = pl.DeviceIdType.MESH
F32 = jnp.float32

VEL = [
    (0, 0, 0),
    (1, 0, 0),
    (-1, 0, 0),
    (0, 1, 0),
    (0, -1, 0),
    (0, 0, 1),
    (0, 0, -1),
    (1, 1, 0),
    (-1, -1, 0),
    (1, -1, 0),
    (-1, 1, 0),
    (1, 0, 1),
    (-1, 0, -1),
    (1, 0, -1),
    (-1, 0, 1),
    (0, 1, 1),
    (0, -1, -1),
    (0, 1, -1),
    (0, -1, 1),
]
VEL = VEL + VEL[:7]
CH = 26
PLANES = 4
ROWS = 8
LANES = 128

NEIGHBOURS = ((1, 0), (-1, 0), (1, 1), (1, -1), (-1, 1), (-1, -1), (0, 1), (0, -1))

HUB_CORE = 1

BRINKMAN = 4.0
SPEED = 0.05
RATE_H = 1.0 / 0.7
RATE_E = 1.5

E_NORM = 2394.0
FLUID_P, FLUID_Q = -0.2, -0.1
K_MEAN = 1.4 / 19.0
K_E = (1.4 - 1.19) / E_NORM
K_N = 0.15 / 18.0
K_D = 0.15 / 4.0
K_J = 0.2 / 10.0
K_Q = 0.78 / 8.0


def moments(f):
    e = [f[a] + f[a + 1] for a in range(1, 19, 2)]
    o = [f[a] - f[a + 1] for a in range(1, 19, 2)]
    sxy, txy = o[3] + o[4], o[3] - o[4]
    sxz, txz = o[5] + o[6], o[5] - o[6]
    syz, tyz = o[7] + o[8], o[7] - o[8]
    exy, dxy = e[3] + e[4], e[3] - e[4]
    exz, dxz = e[5] + e[6], e[5] - e[6]
    eyz, dyz = e[7] + e[8], e[7] - e[8]
    axis_sum = e[0] + e[1] + e[2]
    diag_sum = exy + exz + eyz
    return dict(
        e=e,
        o=o,
        f0=f[0],
        axis=axis_sum,
        diag=diag_sum,
        across=(eyz, exz, exy),
        cross=(dxy, dxz, dyz),
        j=(o[0] + sxy + sxz, o[1] + txy + syz, o[2] + txz + tyz),
        q=(sxy - sxz, syz - txy, txz - tyz),
    )


def density_velocity(m):
    r = m["f0"] + m["axis"] + m["diag"]
    inverse = 1.0 / r
    return r, inverse, [j * inverse for j in m["j"]]


def second_order(m):
    shift = m["axis"] - m["diag"]
    return [3.0 * (m["e"][a] - m["across"][a]) - shift for a in range(3)]


def assemble(even_rest, even_axis, even_diag, cross, odd_axis, odd_diag, third, pe, po, m):
    out = [even_rest]
    for a in range(3):
        even = pe * m["e"][a] + even_axis[a]
        odd = po * m["o"][a] + odd_axis[a]
        out += [even + odd, even - odd]
    x, y, z = odd_diag
    qx, qy, qz = third
    xy_x, xy_y = x + qx, y - qy
    xz_x, xz_z = x - qx, z + qz
    yz_y, yz_z = y + qy, z - qz
    odds = [xy_x + xy_y, xy_x - xy_y, xz_x + xz_z, xz_x - xz_z, yz_y + yz_z, yz_y - yz_z]
    for k in range(6):
        base = even_diag[2 - k // 2]
        base = base + cross[k // 2] if k % 2 == 0 else base - cross[k // 2]
        even = pe * m["e"][3 + k] + base
        odd = po * m["o"][3 + k] + odds[k]
        out += [even + odd, even - odd]
    return out


def cell_kinds(kind):
    return kind == 0, kind == 1, kind == 2, kind == 3


def relax_factors(kind):
    fluid, solid, _, _ = cell_kinds(kind)
    pe = jnp.where(fluid, FLUID_P, jnp.where(solid, 0.5, 0.0))
    po = jnp.where(fluid, FLUID_Q, jnp.where(solid, -0.5, 0.0))
    he = jnp.where(fluid, 0.5 - RATE_E / 2, jnp.where(solid, 0.5, 0.0))
    ho = jnp.where(fluid, 0.5 - RATE_H / 2, jnp.where(solid, -0.5, 0.0))
    return pe, po, he, ho


def damping_of(porosity):
    return 1.0 / (1.0 + BRINKMAN * (1.0 - porosity))


def dot3(a, b):
    return a[0] * b[0] + a[1] * b[1] + a[2] * b[2]


def collide(pops, porosity, kind, level):
    fluid, solid, inlet, outlet = cell_kinds(kind)
    pe, po, he, ho = relax_factors(kind)
    f, h = pops[:19], pops[19:]
    m = moments(f)
    r, _, u = density_velocity(m)
    d = damping_of(porosity)
    d_eff = jnp.where(outlet, 1.0, d)
    b = [c * d_eff for c in u]
    zero = jnp.zeros_like(r)

    def on(value):
        return jnp.where(fluid, value, 0.0)

    def pick(at_fluid, elsewhere):
        return jnp.where(fluid, at_fluid, jnp.where(solid, 0.0, elsewhere))

    re = jnp.where(inlet, 1.0, r)
    be = [
        jnp.where(inlet, SPEED, b[0]),
        jnp.where(inlet, 0.0, b[1]),
        jnp.where(inlet, 0.0, b[2]),
    ]
    rb = [re * c for c in be]
    bb = [p * c for p, c in zip(rb, be)]
    b2 = bb[0] + bb[1] + bb[2]
    crossed = (rb[0] * be[1], rb[0] * be[2], rb[1] * be[2])
    quad_rest = pick(-0.65, -0.5) * b2
    axis_all = pick(-0.09, -1.0 / 12.0) * b2
    axis_own = pick(0.325, 0.25)
    quad_axis = [axis_all + axis_own * c for c in bb]
    diag_all = pick(0.095, 1.0 / 12.0) * b2
    diag_own = pick(-0.15, -0.125)
    quad_diag = [diag_all + diag_own * c for c in bb]
    cross_own = pick(0.3125, 0.25)
    quad_cross = [cross_own * c for c in crossed]
    lin_axis_own = pick(0.18, 1.0 / 6.0)
    lin_diag_own = pick(0.08, 1.0 / 12.0)
    lin_axis = [lin_axis_own * c for c in rb]
    lin_diag = [lin_diag_own * c for c in rb]
    n = second_order(m)
    e_f = -30.0 * m["f0"] - 11.0 * m["axis"] + 8.0 * m["diag"]
    de = K_E * (e_f + 11.0 * r)
    even_rest = jnp.where(fluid, 1.4 / 3.0 * r - 30.0 * de, pick(0.0, 1.0 / 3.0) * re)
    even_axis = jnp.where(fluid, 1.4 / 18.0 * r - 11.0 * de, pick(0.0, 1.0 / 18.0) * re)
    even_diag = jnp.where(fluid, 1.4 / 36.0 * r + 8.0 * de, pick(0.0, 1.0 / 36.0) * re)
    rest_own = jnp.where(fluid, -0.4, jnp.where(solid, 1.0, 0.0))
    n_own = on(K_N)
    n = [n_own * c for c in n]
    d_own = on(K_D)
    j_own = on(K_J)
    q_own = on(-K_Q)
    jj = [j_own * c for c in m["j"]]
    new_f = assemble(
        rest_own * m["f0"] + even_rest + quad_rest,
        [even_axis + quad_axis[a] + n[a] for a in range(3)],
        [even_diag + quad_diag[a] - n[a] for a in range(3)],
        [quad_cross[k] + d_own * m["cross"][k] for k in range(3)],
        [lin_axis[a] + jj[a] for a in range(3)],
        [lin_diag[a] + jj[a] for a in range(3)],
        [q_own * c for c in m["q"]],
        pe,
        po,
        m,
    )
    kappa = on(BRINKMAN * d)
    kappa2 = kappa + kappa
    g_rest = kappa2 * quad_rest
    g_axis = [kappa2 * c for c in quad_axis]
    g_diag = [kappa2 * c for c in quad_diag]
    g_cross = [kappa2 * c for c in quad_cross]
    g_la = [kappa * c for c in lin_axis]
    g_ld = [kappa * c for c in lin_diag]
    g_f = [g_rest]
    for a in range(3):
        g_f += [g_axis[a] + g_la[a], g_axis[a] - g_la[a]]
    x, y, z = g_ld
    odds = [x + y, x - y, x + z, x - z, y + z, y - z]
    for k in range(6):
        even = g_diag[2 - k // 2]
        even = even + g_cross[k // 2] if k % 2 == 0 else even - g_cross[k // 2]
        g_f += [even + odds[k], even - odds[k]]
    he_pairs = [h[a] + h[a + 1] for a in (1, 3, 5)]
    ho_pairs = [h[a] - h[a + 1] for a in (1, 3, 5)]
    s = h[0] + he_pairs[0] + he_pairs[1] + he_pairs[2]
    se = jnp.where(inlet, level, s)
    s_even = pick(RATE_E, 1.0) * se
    s_odd = pick(0.5 * RATE_H, 0.5) * se
    new_h = [jnp.where(fluid, 1.0 - RATE_E, jnp.where(solid, 1.0, 0.0)) * h[0] + 0.25 * s_even]
    g_h = [zero]
    for a in range(3):
        even = he * he_pairs[a] + 0.125 * s_even
        push = s_odd * be[a]
        odd = ho * ho_pairs[a] + push
        new_h += [even + odd, even - odd]
        push = kappa * push
        g_h += [push, -push]
    return new_f + new_h, g_f + g_h


def weighted_factors(a, b, own):
    return (
        own[0] - a * K_MEAN + 30.0 * b * K_E,
        own[1] - a * K_MEAN + 11.0 * b * K_E,
        own[2] - a * K_MEAN - 8.0 * b * K_E,
    )


A0_F = weighted_factors(1.0, -11.0, (1.4 / 3.0, 1.4 / 18.0, 1.4 / 36.0))
A2_F = weighted_factors(1.0 / 3.0, 5.0 / 9.0, (0.0, 1.0 / 540.0, 1.4 / 36.0 - 1.0 / 540.0))


def transposed(pops, carried, porosity, kind):
    fluid, solid, inlet, outlet = cell_kinds(kind)
    pe, po, he, ho = relax_factors(kind)
    f, h = pops[:19], pops[19:]
    ms = moments(f)
    r, inverse, u = density_velocity(ms)
    s = h[0] + (h[1] + h[2]) + (h[3] + h[4]) + (h[5] + h[6])
    d = jnp.where(outlet, 1.0, damping_of(porosity))
    b = [c * d for c in u]
    ratio4 = 4.0 * s * inverse

    m = moments(carried[:19])
    mu = carried[19:]
    f0, axis, diag = m["f0"], m["axis"], m["diag"]

    def pick(at_fluid, at_outlet):
        return jnp.where(fluid, at_fluid, at_outlet)

    a0 = (
        pick(A0_F[0], 1.0 / 3.0) * f0
        + pick(A0_F[1], 1.0 / 18.0) * axis
        + pick(A0_F[2], 1.0 / 36.0) * diag
    )
    common = (
        pick(A2_F[0], 0.0) * f0 + pick(A2_F[1], 0.0) * axis + pick(A2_F[2], 1.0 / 36.0) * diag
    )
    own = pick(1.4 / 18.0 - 3.0 / 540.0, 1.0 / 18.0)
    away = pick(-1.4 / 36.0 + 3.0 / 540.0, -1.0 / 36.0)
    a2 = [own * m["e"][a] + away * m["across"][a] + common for a in range(3)]
    cross_own = pick(1.25 / 36.0, 1.0 / 36.0)
    axy, axz, ayz = [cross_own * c for c in m["cross"]]
    o_own = pick(1.0 / 30.0, 1.0 / 36.0)
    j_own = pick(0.96 / 36.0, 1.0 / 36.0)
    a1 = [o_own * m["o"][a] + j_own * m["j"][a] for a in range(3)]
    me = [mu[a] + mu[a + 1] for a in (1, 3, 5)]
    mo = [mu[a] - mu[a + 1] for a in (1, 3, 5)]
    me_sum = me[0] + me[1] + me[2]
    mean_h = (RATE_E / 7.0) * (mu[0] + me_sum)
    b0 = pick(RATE_E, 1.0) * (0.25 * mu[0] + 0.125 * me_sum) - pick(mean_h, 0.0)
    b1_own = pick(0.125 * RATE_H, 0.125)
    b1 = [b1_own * c for c in mo]

    ab = [
        a2[0] * b[0] + axy * b[1] + axz * b[2],
        axy * b[0] + a2[1] * b[1] + ayz * b[2],
        axz * b[0] + ayz * b[1] + a2[2] * b[2],
    ]
    curved = [9.0 * ab[a] - 3.0 * a0 * b[a] for a in range(3)]
    b1b = dot3(b1, b)
    total = [3.0 * a1[a] + curved[a] + ratio4 * b1[a] for a in range(3)]
    to_r = a0 - 0.5 * dot3(b, curved) - ratio4 * b1b
    to_s = b0 + 4.0 * b1b
    sens = jnp.where(fluid, BRINKMAN * d * d * dot3(ms["j"], total), 0.0)

    active = jnp.logical_or(fluid, outlet)
    d_on = jnp.where(active, d, 0.0)
    to_r = jnp.where(active, to_r, 0.0)
    to_s = jnp.where(active, to_s, 0.0)
    to_j = [d_on * c for c in total]

    def on(value):
        return jnp.where(fluid, value, 0.0)

    mean = on(K_MEAN) * (f0 + axis + diag)
    ef = on(K_E) * (-30.0 * f0 - 11.0 * axis + 8.0 * diag)
    base = to_r + mean
    n_own = on(K_N)
    n = [n_own * c for c in second_order(m)]
    d_own = on(K_D)
    jj_own = on(K_J)
    q_own = on(-K_Q)
    odd = [to_j[a] + jj_own * m["j"][a] for a in range(3)]
    rest_own = jnp.where(fluid, -0.4, jnp.where(solid, 1.0, 0.0))
    base_axis = base - 11.0 * ef
    base_diag = base + 8.0 * ef
    out_f = assemble(
        rest_own * f0 + base - 30.0 * ef,
        [base_axis + n[a] for a in range(3)],
        [base_diag - n[a] for a in range(3)],
        [d_own * c for c in m["cross"]],
        odd,
        odd,
        [q_own * c for c in m["q"]],
        pe,
        po,
        m,
    )
    to_s = to_s + on(mean_h)
    out_h = [jnp.where(fluid, 1.0 - RATE_E, jnp.where(solid, 1.0, 0.0)) * mu[0] + to_s]
    for a in range(3):
        even = he * me[a] + to_s
        odd = ho * mo[a]
        out_h += [even + odd, even - odd]
    return out_f + out_h, sens


class Stream:
    def __init__(self, heading, fields):
        self.heading = heading
        self.fields = fields
        self.vel = [tuple(heading * c for c in v) for v in VEL]
        plus = [i for i in range(CH) if self.vel[i][0] == 1]
        minus = [i for i in range(CH) if self.vel[i][0] == -1]
        still = [i for i in range(CH) if self.vel[i][0] == 0]
        order = [(k, i) for group in (plus, minus, still) for k in range(fields) for i in group]
        self.place = {key: at for at, key in enumerate(order)}
        self.face = len(plus) * fields
        self.z_place = {}
        self.edge = {}
        for sign in (1, -1):
            group = [i for i in range(CH) if self.vel[i][2] == sign]
            group.sort(key=lambda i: -abs(self.vel[i][0]))
            keys = [(k, i) for i in group for k in range(fields)]
            self.z_count = len(keys)
            self.rows_over_z = 2 * self.z_count * PLANES
            self.rows_over_x = 2 * self.face * ROWS + 4 * fields
            for at, key in enumerate(keys):
                self.z_place[key] = (0 if sign == 1 else 1, at)
            for at, i in enumerate(group[:2]):
                self.edge[(self.vel[i][0], sign)] = at * fields

    def scratch(self):
        return [
            pltpu.VMEM((CH * self.fields, PLANES + 2, ROWS, LANES), F32),
            pltpu.VMEM((2, self.z_count, PLANES, 1, LANES), F32),
            pltpu.VMEM((2, self.z_count, PLANES + 2, 1, LANES), F32),
            pltpu.SemaphoreType.DMA((1,)),
            pltpu.SemaphoreType.DMA((2,)),
        ]

    def put(self, refs, x, field, values):
        padded, rows = refs[0], refs[1]
        for i, value in enumerate(values):
            _, vy, vz = self.vel[i]
            if vy:
                value = pltpu.roll(value, vy % LANES, 1)
            padded[self.place[(field, i)], x + 1] = value
            if vz:
                side, at = self.z_place[(field, i)]
                row = ROWS - 1 if vz == 1 else 0
                rows[side, at, x] = value[row : row + 1, :]

    def copies(self, refs, gx, gz, n_gx, n_gz):
        padded, rows, halo, send, recv = refs
        found = []
        for dx, dz in NEIGHBOURS:
            target = (lax.rem(gx + dx + n_gx, n_gx), lax.rem(gz + dz + n_gz, n_gz))
            side = 0 if dz == 1 else 1
            if dz == 0:
                start = 0 if dx == 1 else self.face
                source = padded.at[pl.ds(start, self.face), PLANES if dx == 1 else 1]
                landing = padded.at[pl.ds(start, self.face), 0 if dx == 1 else PLANES + 1]
            elif dx == 0:
                source = rows.at[side]
                landing = halo.at[side, :, pl.ds(1, PLANES)]
            else:
                start = self.edge[(dx, dz)]
                source = rows.at[side, pl.ds(start, self.fields), PLANES - 1 if dx == 1 else 0]
                landing = halo.at[side, pl.ds(start, self.fields), 0 if dx == 1 else PLANES + 1]
            found.append(
                pltpu.make_async_remote_copy(
                    src_ref=source,
                    dst_ref=landing,
                    send_sem=send.at[0],
                    recv_sem=recv.at[0 if dx == 0 else 1],
                    device_id=target,
                    device_id_type=MESH,
                )
            )
        return found

    def get(self, refs, x, field):
        padded, halo = refs[0], refs[2]
        row = lax.broadcasted_iota(jnp.int32, (ROWS, LANES), 0)
        values = []
        for i in range(CH):
            vx, _, vz = self.vel[i]
            value = padded[self.place[(field, i)], x + 1 - vx]
            if vz:
                side, at = self.z_place[(field, i)]
                edge = 0 if vz == 1 else ROWS - 1
                value = jnp.where(
                    row == edge, halo[side, at, x + 1 - vx], pltpu.roll(value, vz % ROWS, 0)
                )
            values.append(value)
        return values


OPPOSITE = [VEL.index(tuple(-c for c in v)) for v in VEL[:19]]
OPPOSITE += [19 + k for k in OPPOSITE[:7]]
FORWARD = Stream(1, 3)
BACKWARD = Stream(-1, 1)


def kernel(n_gx, n_gz, *refs):
    (checkpoint, adjoint_end, porosity, node_type, inlet_index, inlet_conc) = refs[:6]
    (out_ref, grad_ref, sum_ref) = refs[6:9]
    (cp, ae, por, kind, feed, conc, sens, in_sem) = refs[9:17]
    forward, back = refs[17:22], refs[22:27]
    (mine_a, got_a, mine_b, got_b, total_row, got_c, got_r, red_send, red_recv) = refs[27:]
    gx, gz = lax.axis_index("gx"), lax.axis_index("gz")
    n_column, n_sheet = n_gx // 2, 2 * n_gz
    x_lo, column_at = gx // n_column, lax.rem(gx, n_column)
    z, core = column_at // 2, lax.rem(column_at, 2)
    x_hi, y = gz // (n_gz // 2), lax.rem(gz, n_gz // 2)

    n_z = n_column // 2
    lower = z < n_z // 2
    upper = jnp.logical_not(lower)
    hub = jnp.logical_and(lower, core == HUB_CORE)
    lower_only = jnp.logical_and(lower, core != HUB_CORE)
    last_hub = jnp.logical_and(hub, z == n_z // 2 - 1)
    next_hub = jnp.logical_and(hub, z == n_z // 2 - 2)

    root = jnp.logical_and(gx == HUB_CORE, gz == 0)
    not_root = jnp.logical_not(root)
    root_at = (HUB_CORE, 0)

    def column(at_z, at_core):
        return (x_lo * n_column + 2 * at_z + at_core, gz)

    n_y = n_gz // 2

    def sheet(lo, hi, at_y, at_core):
        to_gz = lax.rem(x_hi + hi, 2) * n_y + at_y
        return (lax.rem(x_lo + lo, 2) * n_column + 2 * z + at_core, to_gz)

    rows = [*reversed(range(n_y // 2)), *reversed(range(n_y // 2, n_y))]
    around = [(lo, hi, k, c) for k in rows for hi in (1, 0) for lo in (1, 0) for c in (1 - HUB_CORE, HUB_CORE)]

    def each_of(offsets, act):
        for lo, hi, k, c in offsets:
            if lo or hi or c != HUB_CORE:
                act(sheet(lo, hi, k, c))
            else:

                @pl.when(y != k)
                def _():
                    act(sheet(lo, hi, k, c))

    to_hubs = [o for o in around if o[3] == HUB_CORE]
    column_hubs = [(k, HUB_CORE) for k in range(n_z // 2)]
    fourth = [(k, c) for k in range(3 * n_z // 4, n_z) for c in range(2)]
    third = [(k, c) for k in range(n_z // 2, 3 * n_z // 4) for c in range(2)]

    barrier = pltpu.get_barrier_semaphore()

    def greet(target):
        pl.semaphore_signal(barrier, inc=1, device_id=target, device_id_type=MESH)

    def neighbour(dx, dz):
        return (lax.rem(gx + dx + n_gx, n_gx), lax.rem(gz + dz + n_gz, n_gz))

    for dx, dz in NEIGHBOURS:
        greet(neighbour(dx, dz))

    loads = [
        pltpu.make_async_copy(source, target, in_sem.at[k])
        for source, target, k in (
            (checkpoint, cp, 0),
            (porosity, por, 0),
            (node_type, kind, 0),
            (inlet_index, feed, 0),
            (inlet_conc, conc, 1),
            (adjoint_end, ae, 2),
        )
    ]
    for load in loads:
        load.start()

    @pl.when(upper)
    def _():
        greet(column(n_z // 2 - jnp.where(z < 3 * n_z // 4, 1, 2), HUB_CORE))

    @pl.when(lower_only)
    def _():
        for offset in to_hubs:
            greet(sheet(*offset))

    @pl.when(jnp.logical_and(hub, not_root))
    def _():
        each_of(to_hubs, greet)

    @pl.when(hub)
    def _():
        greet(column(z, 1 - HUB_CORE))
        for k in range(1, n_z):
            for c in range(2):
                greet(column(lax.rem(z + k, n_z), c))

    @pl.when(root)
    def _():
        @pl.loop(0, n_gx)
        def _(k):
            to_gx = lax.rem(k, 2) * n_column + n_column - 1 - k // 2
            for to_gz in range(n_gz):
                if to_gz:
                    greet((to_gx, to_gz))
                else:

                    @pl.when(to_gx != HUB_CORE)
                    def _():
                        greet((to_gx, to_gz))

    loaded = forward[0].at[pl.ds(0, CH + 3), pl.ds(0, PLANES)]
    pltpu.make_async_copy(loaded, loaded, in_sem.at[0]).wait()
    loads[4].wait()

    def start_plane(x, carry):
        level = jnp.where(feed[x] == 0, conc[0], jnp.where(feed[x] == 1, conc[1], 0.0))
        post, slope = collide([cp[i, x] for i in range(CH)], por[x], kind[x], level)
        FORWARD.put(forward, x, 0, post)
        FORWARD.put(forward, x, 1, slope)
        return carry

    lax.fori_loop(0, PLANES, start_plane, 0, unroll=True)
    loads[5].wait()

    def end_plane(x, carry):
        FORWARD.put(forward, x, 2, [ae[i, x] for i in OPPOSITE])
        return carry

    lax.fori_loop(0, PLANES, end_plane, 0, unroll=True)

    hub_sends = len(column_hubs) - 1 + len(around) - 1
    awaited = len(NEIGHBOURS) + jnp.where(hub, hub_sends, len(column_hubs))
    awaited += jnp.where(root, 0, 1) - jnp.where(jnp.logical_and(jnp.logical_and(hub, z == 0), not_root), 1, 0)
    awaited += jnp.where(next_hub, len(fourth), 0) + jnp.where(last_hub, len(third), 0)
    pl.semaphore_wait(barrier, awaited)
    for copy in FORWARD.copies(forward, gx, gz, n_gx, n_gz):
        copy.start()
    def mid_plane(x, total):
        state = FORWARD.get(forward, x, 0)
        slope = FORWARD.get(forward, x, 1)
        mirrored = FORWARD.get(forward, x, 2)
        carried = [mirrored[i] for i in OPPOSITE]
        adjoint, sens_mid = transposed(state, carried, por[x], kind[x])
        sens[x] = sens_mid
        BACKWARD.put(back, x, 0, adjoint)
        sums = [a * b for a, b in zip(adjoint, slope)] + [sens_mid, total]
        while len(sums) > 1:
            sums = [a + b for a, b in zip(sums[::2], sums[1::2])] + sums[len(sums) & ~1 :]
        return sums[0]

    def wait_for(semaphore, got, count):
        pltpu.make_async_copy(got.at[pl.ds(0, count)], got.at[pl.ds(0, count)], semaphore).wait()

    wait_for(forward[4].at[0], got_r, FORWARD.rows_over_z)
    total = jnp.zeros((ROWS, LANES), F32)
    total = lax.fori_loop(0, PLANES - 2, lambda k, t: mid_plane(k + 1, t), total, unroll=True)
    wait_for(forward[4].at[1], got_r, FORWARD.rows_over_x)
    total = lax.fori_loop(0, 2, lambda k, t: mid_plane(k * (PLANES - 1), t), total, unroll=True)

    def reduce_copy(stage, mine, got, slot, target):
        return pltpu.make_async_remote_copy(
            src_ref=mine,
            dst_ref=got.at[slot],
            send_sem=red_send.at[0],
            recv_sem=red_recv.at[min(stage, 1)],
            device_id=target,
            device_id_type=MESH,
        )

    def in_order(terms):
        sum_of = terms[0]
        for term in terms[1:]:
            sum_of = sum_of + term
        return sum_of

    mine_a[...] = jnp.sum(total, axis=0, keepdims=True)
    sheet_at = x_lo * n_gz + gz

    @pl.when(not_root)
    def _():
        reduce_copy(3, mine_a, got_r, pl.ds(column_at * n_sheet + sheet_at, 1), root_at).start()

    for k, c in column_hubs:

        @pl.when(jnp.logical_not(jnp.logical_and(hub, z == k)))
        def _():
            reduce_copy(0, mine_a, got_a, column_at, column(k, c)).start()

    for copy in BACKWARD.copies(back, gx, gz, n_gx, n_gz):
        copy.start()

    def send_sheet(target):
        reduce_copy(1, mine_b, got_b, pl.ds(sheet_at, 1), target).start()

    def send_unless_root(target):
        @pl.when(jnp.logical_or(target[0] != HUB_CORE, target[1] != 0))
        def _():
            send_sheet(target)

    @pl.when(hub)
    def _():
        wait_for(red_recv.at[0], got_a, n_column - 1)
        got_a[column_at] = mine_a[...]
        mine_b[...] = in_order([got_a[k] for k in range(n_column)])
        may_be_root = [o for o in around if o[2] == 0 and o[3] == HUB_CORE]
        each_of([o for o in around if o not in may_be_root], send_sheet)
        each_of(may_be_root, send_unless_root)
        got_b[pl.ds(sheet_at, 1), :] = mine_b[...]

    wait_for(back[4].at[0], got_r, BACKWARD.rows_over_z)
    wait_for(back[4].at[1], got_r, BACKWARD.rows_over_x)

    def last_plane(x, carry):
        state = [cp[i, x] for i in range(CH)]
        carried = BACKWARD.get(back, x, 0)
        adjoint, sens_start = transposed(state, carried, por[x], kind[x])
        for i in range(CH):
            out_ref[i, x] = adjoint[i]
        grad_ref[x] = sens_start + sens[x]
        return carry

    lax.fori_loop(0, PLANES, last_plane, 0, unroll=True)

    wait_for(forward[3].at[0], got_r, FORWARD.rows_over_z + FORWARD.rows_over_x)
    wait_for(back[3].at[0], got_r, BACKWARD.rows_over_z + BACKWARD.rows_over_x)

    @pl.when(jnp.logical_and(hub, not_root))
    def _():
        wait_for(red_recv.at[1], got_b, n_sheet - 1)

    @pl.when(lower_only)
    def _():
        wait_for(red_recv.at[1], got_b, n_sheet)

    @pl.when(jnp.logical_and(lower, not_root))
    def _():
        total_row[...] = jnp.sum(got_b[...], axis=0, keepdims=True)
        sum_ref[...] = total_row[...]

    @pl.when(root)
    def _():
        wait_for(red_recv.at[1], got_r, n_column * n_sheet - 1)
        got_r[pl.ds(HUB_CORE * n_sheet, 1), :] = mine_a[...]
        sheet_sums = in_order([got_r[pl.ds(k * n_sheet, n_sheet), :] for k in range(n_column)])
        total_row[...] = jnp.sum(sheet_sums, axis=0, keepdims=True)
        sum_ref[...] = total_row[...]

    for is_hub, targets in ((next_hub, fourth), (last_hub, third)):

        @pl.when(is_hub)
        def _():
            for k, c in targets:
                reduce_copy(2, total_row, got_c, 0, column(k, c)).start()

    @pl.when(upper)
    def _():
        wait_for(red_recv.at[1], got_c, 1)
        sum_ref[...] = got_c[0]

    hub_rows = len(column_hubs) - 1 + len(around) - 1
    for kind_of, rows_sent in (
        (jnp.logical_not(hub), len(column_hubs) + 1),
        (jnp.logical_and(hub, z == 0), hub_rows),
        (next_hub, hub_rows + 1 + len(fourth)),
        (last_hub, hub_rows + 1 + len(third)),
        (jnp.logical_and(hub, jnp.logical_and(z > 0, z < n_z // 2 - 2)), hub_rows + 1),
    ):

        @pl.when(kind_of)
        def _():
            wait_for(red_send.at[0], got_r, rows_sent)


def finish(adjoint, grad, row, out_ref, grad_ref, total_ref, held, sems):
    copies = [
        pltpu.make_async_copy(adjoint, out_ref, sems.at[0]),
        pltpu.make_async_copy(grad, grad_ref, sems.at[1]),
        pltpu.make_async_copy(held, total_ref, sems.at[2]),
    ]
    copies[0].start()
    copies[1].start()
    held[...] = jnp.sum(row[...], axis=1, keepdims=True)
    copies[2].start()
    for copy in copies:
        copy.wait()


def solution(mesh):
    n_gx, n_gz = mesh.shape["gx"], mesh.shape["gz"]
    block = (PLANES, ROWS, LANES)
    any_space = pl.BlockSpec(memory_space=pl.ANY)
    in_vmem = pl.BlockSpec(memory_space=pltpu.VMEM)

    def on_device(*args):
        args = [pltpu.with_memory_space_constraint(a, pltpu.HBM) for a in args]
        held = pl.pallas_call(
            lambda *refs: kernel(n_gx, n_gz, *refs),
            out_shape=(
                pltpu.VMEM((CH,) + block, F32),
                pltpu.VMEM(block, F32),
                pltpu.VMEM((1, LANES), F32),
            ),
            in_specs=[any_space] * 6,
            out_specs=(in_vmem, in_vmem, in_vmem),
            scratch_shapes=[
                pltpu.VMEM((CH,) + block, F32),
                pltpu.VMEM((CH,) + block, F32),
                pltpu.VMEM(block, F32),
                pltpu.VMEM(block, jnp.int32),
                pltpu.VMEM(block, jnp.int32),
                pltpu.SMEM((2,), F32),
                pltpu.VMEM(block, F32),
                pltpu.SemaphoreType.DMA((3,)),
            ]
            + FORWARD.scratch()
            + BACKWARD.scratch()
            + [
                pltpu.VMEM((1, LANES), F32),
                pltpu.VMEM((n_gx // 2, 1, LANES), F32),
                pltpu.VMEM((1, LANES), F32),
                pltpu.VMEM((2 * n_gz, LANES), F32),
                pltpu.VMEM((1, LANES), F32),
                pltpu.VMEM((1, 1, LANES), F32),
                pltpu.VMEM((n_gx * n_gz, LANES), F32),
                pltpu.SemaphoreType.DMA((1,)),
                pltpu.SemaphoreType.DMA((2,)),
            ],
            compiler_params=pltpu.CompilerParams(
                collective_id=0, has_side_effects=True, vmem_limit_bytes=32 * 1024 * 1024
            ),
        )(*args)
        held = [pltpu.with_memory_space_constraint(a, pltpu.VMEM) for a in held]
        adjoint, grad, total = pl.pallas_call(
            finish,
            out_shape=(
                jax.ShapeDtypeStruct((CH,) + block, F32),
                jax.ShapeDtypeStruct(block, F32),
                jax.ShapeDtypeStruct((1, 1), F32),
            ),
            in_specs=[in_vmem, in_vmem, in_vmem],
            out_specs=(any_space, any_space, any_space),
            scratch_shapes=[pltpu.VMEM((1, 1), F32), pltpu.SemaphoreType.DMA((3,))],
        )(*held)
        return adjoint, grad, total.reshape(())

    return jax.shard_map(
        on_device,
        mesh=mesh,
        in_specs=(
            P(None, "gx", "gz", None),
            P(None, "gx", "gz", None),
            P("gx", "gz", None),
            P("gx", "gz", None),
            P("gx", "gz", None),
            P(),
        ),
        out_specs=(P(None, "gx", "gz", None), P("gx", "gz", None), P()),
        check_vma=False,
    )
```

```python
import jax
import jax.numpy as jnp
from jax import lax
from jax.experimental import pallas as pl
from jax.experimental.pallas import tpu as pltpu
from jax.sharding import PartitionSpec as P

MESH = pl.DeviceIdType.MESH
F32 = jnp.float32

VEL = [
    (0, 0, 0),
    (1, 0, 0),
    (-1, 0, 0),
    (0, 1, 0),
    (0, -1, 0),
    (0, 0, 1),
    (0, 0, -1),
    (1, 1, 0),
    (-1, -1, 0),
    (1, -1, 0),
    (-1, 1, 0),
    (1, 0, 1),
    (-1, 0, -1),
    (1, 0, -1),
    (-1, 0, 1),
    (0, 1, 1),
    (0, -1, -1),
    (0, 1, -1),
    (0, -1, 1),
]
VEL = VEL + VEL[:7]
CH = 26
PLANES = 4
ROWS = 8
LANES = 128

NEIGHBOURS = ((1, 0), (-1, 0), (1, 1), (1, -1), (-1, 1), (-1, -1), (0, 1), (0, -1))

HUB_CORE = 1

BRINKMAN = 4.0
SPEED = 0.05
RATE_H = 1.0 / 0.7
RATE_E = 1.5

E_NORM = 2394.0
FLUID_P, FLUID_Q = -0.2, -0.1
K_MEAN = 1.4 / 19.0
K_E = (1.4 - 1.19) / E_NORM
K_N = 0.15 / 18.0
K_D = 0.15 / 4.0
K_J = 0.2 / 10.0
K_Q = 0.78 / 8.0


def moments(f):
    e = [f[a] + f[a + 1] for a in range(1, 19, 2)]
    o = [f[a] - f[a + 1] for a in range(1, 19, 2)]
    sxy, txy = o[3] + o[4], o[3] - o[4]
    sxz, txz = o[5] + o[6], o[5] - o[6]
    syz, tyz = o[7] + o[8], o[7] - o[8]
    exy, dxy = e[3] + e[4], e[3] - e[4]
    exz, dxz = e[5] + e[6], e[5] - e[6]
    eyz, dyz = e[7] + e[8], e[7] - e[8]
    axis_sum = e[0] + e[1] + e[2]
    diag_sum = exy + exz + eyz
    return dict(
        e=e,
        o=o,
        f0=f[0],
        axis=axis_sum,
        diag=diag_sum,
        across=(eyz, exz, exy),
        cross=(dxy, dxz, dyz),
        j=(o[0] + sxy + sxz, o[1] + txy + syz, o[2] + txz + tyz),
        q=(sxy - sxz, syz - txy, txz - tyz),
    )


def density_velocity(m):
    r = m["f0"] + m["axis"] + m["diag"]
    inverse = 1.0 / r
    return r, inverse, [j * inverse for j in m["j"]]


def second_order(m):
    shift = m["axis"] - m["diag"]
    return [3.0 * (m["e"][a] - m["across"][a]) - shift for a in range(3)]


def assemble(even_rest, even_axis, even_diag, cross, odd_axis, odd_diag, third, pe, po, m):
    out = [even_rest]
    for a in range(3):
        even = pe * m["e"][a] + even_axis[a]
        odd = po * m["o"][a] + odd_axis[a]
        out += [even + odd, even - odd]
    x, y, z = odd_diag
    qx, qy, qz = third
    xy_x, xy_y = x + qx, y - qy
    xz_x, xz_z = x - qx, z + qz
    yz_y, yz_z = y + qy, z - qz
    odds = [xy_x + xy_y, xy_x - xy_y, xz_x + xz_z, xz_x - xz_z, yz_y + yz_z, yz_y - yz_z]
    for k in range(6):
        base = even_diag[2 - k // 2]
        base = base + cross[k // 2] if k % 2 == 0 else base - cross[k // 2]
        even = pe * m["e"][3 + k] + base
        odd = po * m["o"][3 + k] + odds[k]
        out += [even + odd, even - odd]
    return out


def cell_kinds(kind):
    return kind == 0, kind == 1, kind == 2, kind == 3


def relax_factors(kind):
    fluid, solid, _, _ = cell_kinds(kind)
    pe = jnp.where(fluid, FLUID_P, jnp.where(solid, 0.5, 0.0))
    po = jnp.where(fluid, FLUID_Q, jnp.where(solid, -0.5, 0.0))
    he = jnp.where(fluid, 0.5 - RATE_E / 2, jnp.where(solid, 0.5, 0.0))
    ho = jnp.where(fluid, 0.5 - RATE_H / 2, jnp.where(solid, -0.5, 0.0))
    return pe, po, he, ho


def damping_of(porosity):
    return 1.0 / (1.0 + BRINKMAN * (1.0 - porosity))


def dot3(a, b):
    return a[0] * b[0] + a[1] * b[1] + a[2] * b[2]


def collide(pops, porosity, kind, level):
    fluid, solid, inlet, outlet = cell_kinds(kind)
    pe, po, he, ho = relax_factors(kind)
    f, h = pops[:19], pops[19:]
    m = moments(f)
    r, _, u = density_velocity(m)
    d = damping_of(porosity)
    d_eff = jnp.where(outlet, 1.0, d)
    b = [c * d_eff for c in u]
    zero = jnp.zeros_like(r)

    def on(value):
        return jnp.where(fluid, value, 0.0)

    def pick(at_fluid, elsewhere):
        return jnp.where(fluid, at_fluid, jnp.where(solid, 0.0, elsewhere))

    re = jnp.where(inlet, 1.0, r)
    be = [
        jnp.where(inlet, SPEED, b[0]),
        jnp.where(inlet, 0.0, b[1]),
        jnp.where(inlet, 0.0, b[2]),
    ]
    rb = [re * c for c in be]
    bb = [p * c for p, c in zip(rb, be)]
    b2 = bb[0] + bb[1] + bb[2]
    crossed = (rb[0] * be[1], rb[0] * be[2], rb[1] * be[2])
    quad_rest = pick(-0.65, -0.5) * b2
    axis_all = pick(-0.09, -1.0 / 12.0) * b2
    axis_own = pick(0.325, 0.25)
    quad_axis = [axis_all + axis_own * c for c in bb]
    diag_all = pick(0.095, 1.0 / 12.0) * b2
    diag_own = pick(-0.15, -0.125)
    quad_diag = [diag_all + diag_own * c for c in bb]
    cross_own = pick(0.3125, 0.25)
    quad_cross = [cross_own * c for c in crossed]
    lin_axis_own = pick(0.18, 1.0 / 6.0)
    lin_diag_own = pick(0.08, 1.0 / 12.0)
    lin_axis = [lin_axis_own * c for c in rb]
    lin_diag = [lin_diag_own * c for c in rb]
    n = second_order(m)
    e_f = -30.0 * m["f0"] - 11.0 * m["axis"] + 8.0 * m["diag"]
    de = K_E * (e_f + 11.0 * r)
    even_rest = jnp.where(fluid, 1.4 / 3.0 * r - 30.0 * de, pick(0.0, 1.0 / 3.0) * re)
    even_axis = jnp.where(fluid, 1.4 / 18.0 * r - 11.0 * de, pick(0.0, 1.0 / 18.0) * re)
    even_diag = jnp.where(fluid, 1.4 / 36.0 * r + 8.0 * de, pick(0.0, 1.0 / 36.0) * re)
    rest_own = jnp.where(fluid, -0.4, jnp.where(solid, 1.0, 0.0))
    n_own = on(K_N)
    n = [n_own * c for c in n]
    d_own = on(K_D)
    j_own = on(K_J)
    q_own = on(-K_Q)
    jj = [j_own * c for c in m["j"]]
    new_f = assemble(
        rest_own * m["f0"] + even_rest + quad_rest,
        [even_axis + quad_axis[a] + n[a] for a in range(3)],
        [even_diag + quad_diag[a] - n[a] for a in range(3)],
        [quad_cross[k] + d_own * m["cross"][k] for k in range(3)],
        [lin_axis[a] + jj[a] for a in range(3)],
        [lin_diag[a] + jj[a] for a in range(3)],
        [q_own * c for c in m["q"]],
        pe,
        po,
        m,
    )
    kappa = on(BRINKMAN * d)
    kappa2 = kappa + kappa
    g_rest = kappa2 * quad_rest
    g_axis = [kappa2 * c for c in quad_axis]
    g_diag = [kappa2 * c for c in quad_diag]
    g_cross = [kappa2 * c for c in quad_cross]
    g_la = [kappa * c for c in lin_axis]
    g_ld = [kappa * c for c in lin_diag]
    g_f = [g_rest]
    for a in range(3):
        g_f += [g_axis[a] + g_la[a], g_axis[a] - g_la[a]]
    x, y, z = g_ld
    odds = [x + y, x - y, x + z, x - z, y + z, y - z]
    for k in range(6):
        even = g_diag[2 - k // 2]
        even = even + g_cross[k // 2] if k % 2 == 0 else even - g_cross[k // 2]
        g_f += [even + odds[k], even - odds[k]]
    he_pairs = [h[a] + h[a + 1] for a in (1, 3, 5)]
    ho_pairs = [h[a] - h[a + 1] for a in (1, 3, 5)]
    s = h[0] + he_pairs[0] + he_pairs[1] + he_pairs[2]
    se = jnp.where(inlet, level, s)
    s_even = pick(RATE_E, 1.0) * se
    s_odd = pick(0.5 * RATE_H, 0.5) * se
    new_h = [jnp.where(fluid, 1.0 - RATE_E, jnp.where(solid, 1.0, 0.0)) * h[0] + 0.25 * s_even]
    g_h = [zero]
    for a in range(3):
        even = he * he_pairs[a] + 0.125 * s_even
        push = s_odd * be[a]
        odd = ho * ho_pairs[a] + push
        new_h += [even + odd, even - odd]
        push = kappa * push
        g_h += [push, -push]
    return new_f + new_h, g_f + g_h


def weighted_factors(a, b, own):
    return (
        own[0] - a * K_MEAN + 30.0 * b * K_E,
        own[1] - a * K_MEAN + 11.0 * b * K_E,
        own[2] - a * K_MEAN - 8.0 * b * K_E,
    )


A0_F = weighted_factors(1.0, -11.0, (1.4 / 3.0, 1.4 / 18.0, 1.4 / 36.0))
A2_F = weighted_factors(1.0 / 3.0, 5.0 / 9.0, (0.0, 1.0 / 540.0, 1.4 / 36.0 - 1.0 / 540.0))


def transposed(pops, carried, porosity, kind):
    fluid, solid, inlet, outlet = cell_kinds(kind)
    pe, po, he, ho = relax_factors(kind)
    f, h = pops[:19], pops[19:]
    ms = moments(f)
    r, inverse, u = density_velocity(ms)
    s = h[0] + (h[1] + h[2]) + (h[3] + h[4]) + (h[5] + h[6])
    d = jnp.where(outlet, 1.0, damping_of(porosity))
    b = [c * d for c in u]
    ratio4 = 4.0 * s * inverse

    m = moments(carried[:19])
    mu = carried[19:]
    f0, axis, diag = m["f0"], m["axis"], m["diag"]

    def pick(at_fluid, at_outlet):
        return jnp.where(fluid, at_fluid, at_outlet)

    a0 = (
        pick(A0_F[0], 1.0 / 3.0) * f0
        + pick(A0_F[1], 1.0 / 18.0) * axis
        + pick(A0_F[2], 1.0 / 36.0) * diag
    )
    common = (
        pick(A2_F[0], 0.0) * f0 + pick(A2_F[1], 0.0) * axis + pick(A2_F[2], 1.0 / 36.0) * diag
    )
    own = pick(1.4 / 18.0 - 3.0 / 540.0, 1.0 / 18.0)
    away = pick(-1.4 / 36.0 + 3.0 / 540.0, -1.0 / 36.0)
    a2 = [own * m["e"][a] + away * m["across"][a] + common for a in range(3)]
    cross_own = pick(1.25 / 36.0, 1.0 / 36.0)
    axy, axz, ayz = [cross_own * c for c in m["cross"]]
    o_own = pick(1.0 / 30.0, 1.0 / 36.0)
    j_own = pick(0.96 / 36.0, 1.0 / 36.0)
    a1 = [o_own * m["o"][a] + j_own * m["j"][a] for a in range(3)]
    me = [mu[a] + mu[a + 1] for a in (1, 3, 5)]
    mo = [mu[a] - mu[a + 1] for a in (1, 3, 5)]
    me_sum = me[0] + me[1] + me[2]
    mean_h = (RATE_E / 7.0) * (mu[0] + me_sum)
    b0 = pick(RATE_E, 1.0) * (0.25 * mu[0] + 0.125 * me_sum) - pick(mean_h, 0.0)
    b1_own = pick(0.125 * RATE_H, 0.125)
    b1 = [b1_own * c for c in mo]

    ab = [
        a2[0] * b[0] + axy * b[1] + axz * b[2],
        axy * b[0] + a2[1] * b[1] + ayz * b[2],
        axz * b[0] + ayz * b[1] + a2[2] * b[2],
    ]
    curved = [9.0 * ab[a] - 3.0 * a0 * b[a] for a in range(3)]
    b1b = dot3(b1, b)
    total = [3.0 * a1[a] + curved[a] + ratio4 * b1[a] for a in range(3)]
    to_r = a0 - 0.5 * dot3(b, curved) - ratio4 * b1b
    to_s = b0 + 4.0 * b1b
    sens = jnp.where(fluid, BRINKMAN * d * d * dot3(ms["j"], total), 0.0)

    active = jnp.logical_or(fluid, outlet)
    d_on = jnp.where(active, d, 0.0)
    to_r = jnp.where(active, to_r, 0.0)
    to_s = jnp.where(active, to_s, 0.0)
    to_j = [d_on * c for c in total]

    def on(value):
        return jnp.where(fluid, value, 0.0)

    mean = on(K_MEAN) * (f0 + axis + diag)
    ef = on(K_E) * (-30.0 * f0 - 11.0 * axis + 8.0 * diag)
    base = to_r + mean
    n_own = on(K_N)
    n = [n_own * c for c in second_order(m)]
    d_own = on(K_D)
    jj_own = on(K_J)
    q_own = on(-K_Q)
    odd = [to_j[a] + jj_own * m["j"][a] for a in range(3)]
    rest_own = jnp.where(fluid, -0.4, jnp.where(solid, 1.0, 0.0))
    base_axis = base - 11.0 * ef
    base_diag = base + 8.0 * ef
    out_f = assemble(
        rest_own * f0 + base - 30.0 * ef,
        [base_axis + n[a] for a in range(3)],
        [base_diag - n[a] for a in range(3)],
        [d_own * c for c in m["cross"]],
        odd,
        odd,
        [q_own * c for c in m["q"]],
        pe,
        po,
        m,
    )
    to_s = to_s + on(mean_h)
    out_h = [jnp.where(fluid, 1.0 - RATE_E, jnp.where(solid, 1.0, 0.0)) * mu[0] + to_s]
    for a in range(3):
        even = he * me[a] + to_s
        odd = ho * mo[a]
        out_h += [even + odd, even - odd]
    return out_f + out_h, sens


class Stream:
    def __init__(self, heading, fields):
        self.heading = heading
        self.fields = fields
        self.vel = [tuple(heading * c for c in v) for v in VEL]
        plus = [i for i in range(CH) if self.vel[i][0] == 1]
        minus = [i for i in range(CH) if self.vel[i][0] == -1]
        still = [i for i in range(CH) if self.vel[i][0] == 0]
        order = [(k, i) for group in (plus, minus, still) for k in range(fields) for i in group]
        self.place = {key: at for at, key in enumerate(order)}
        self.face = len(plus) * fields
        self.z_place = {}
        self.edge = {}
        for sign in (1, -1):
            group = [i for i in range(CH) if self.vel[i][2] == sign]
            group.sort(key=lambda i: -abs(self.vel[i][0]))
            keys = [(k, i) for i in group for k in range(fields)]
            self.z_count = len(keys)
            self.rows_over_z = 2 * self.z_count * PLANES
            self.rows_over_x = 2 * self.face * ROWS + 4 * fields
            for at, key in enumerate(keys):
                self.z_place[key] = (0 if sign == 1 else 1, at)
            for at, i in enumerate(group[:2]):
                self.edge[(self.vel[i][0], sign)] = at * fields

    def scratch(self):
        return [
            pltpu.VMEM((CH * self.fields, PLANES + 2, ROWS, LANES), F32),
            pltpu.VMEM((2, self.z_count, PLANES, 1, LANES), F32),
            pltpu.VMEM((2, self.z_count, PLANES + 2, 1, LANES), F32),
            pltpu.SemaphoreType.DMA((1,)),
            pltpu.SemaphoreType.DMA((2,)),
        ]

    def put(self, refs, x, field, values):
        padded, rows = refs[0], refs[1]
        for i, value in enumerate(values):
            _, vy, vz = self.vel[i]
            if vy:
                value = pltpu.roll(value, vy % LANES, 1)
            padded[self.place[(field, i)], x + 1] = value
            if vz:
                side, at = self.z_place[(field, i)]
                row = ROWS - 1 if vz == 1 else 0
                rows[side, at, x] = value[row : row + 1, :]

    def copies(self, refs, gx, gz, n_gx, n_gz):
        padded, rows, halo, send, recv = refs
        found = []
        for dx, dz in NEIGHBOURS:
            target = (lax.rem(gx + dx + n_gx, n_gx), lax.rem(gz + dz + n_gz, n_gz))
            side = 0 if dz == 1 else 1
            if dz == 0:
                start = 0 if dx == 1 else self.face
                source = padded.at[pl.ds(start, self.face), PLANES if dx == 1 else 1]
                landing = padded.at[pl.ds(start, self.face), 0 if dx == 1 else PLANES + 1]
            elif dx == 0:
                source = rows.at[side]
                landing = halo.at[side, :, pl.ds(1, PLANES)]
            else:
                start = self.edge[(dx, dz)]
                source = rows.at[side, pl.ds(start, self.fields), PLANES - 1 if dx == 1 else 0]
                landing = halo.at[side, pl.ds(start, self.fields), 0 if dx == 1 else PLANES + 1]
            found.append(
                pltpu.make_async_remote_copy(
                    src_ref=source,
                    dst_ref=landing,
                    send_sem=send.at[0],
                    recv_sem=recv.at[0 if dx == 0 else 1],
                    device_id=target,
                    device_id_type=MESH,
                )
            )
        return found

    def get(self, refs, x, field):
        padded, halo = refs[0], refs[2]
        row = lax.broadcasted_iota(jnp.int32, (ROWS, LANES), 0)
        values = []
        for i in range(CH):
            vx, _, vz = self.vel[i]
            value = padded[self.place[(field, i)], x + 1 - vx]
            if vz:
                side, at = self.z_place[(field, i)]
                edge = 0 if vz == 1 else ROWS - 1
                value = jnp.where(
                    row == edge, halo[side, at, x + 1 - vx], pltpu.roll(value, vz % ROWS, 0)
                )
            values.append(value)
        return values


OPPOSITE = [VEL.index(tuple(-c for c in v)) for v in VEL[:19]]
OPPOSITE += [19 + k for k in OPPOSITE[:7]]
FORWARD = Stream(1, 3)
BACKWARD = Stream(-1, 1)


def kernel(n_gx, n_gz, *refs):
    (checkpoint, adjoint_end, porosity, node_type, inlet_index, inlet_conc) = refs[:6]
    (out_ref, grad_ref, sum_ref) = refs[6:9]
    (cp, ae, por, kind, feed, conc, sens, in_sem) = refs[9:17]
    forward, back = refs[17:22], refs[22:27]
    (mine_a, got_a, mine_b, got_b, total_row, got_c, got_r, red_send, red_recv) = refs[27:]
    gx, gz = lax.axis_index("gx"), lax.axis_index("gz")
    n_column, n_sheet = n_gx // 2, 2 * n_gz
    x_lo, column_at = gx // n_column, lax.rem(gx, n_column)
    z, core = column_at // 2, lax.rem(column_at, 2)
    x_hi, y = gz // (n_gz // 2), lax.rem(gz, n_gz // 2)

    n_z = n_column // 2
    lower = z < n_z // 2
    upper = jnp.logical_not(lower)
    hub = jnp.logical_and(lower, core == HUB_CORE)
    lower_only = jnp.logical_and(lower, core != HUB_CORE)
    last_hub = jnp.logical_and(hub, z == n_z // 2 - 1)
    next_hub = jnp.logical_and(hub, z == n_z // 2 - 2)

    root = jnp.logical_and(gx == HUB_CORE, gz == 0)
    not_root = jnp.logical_not(root)
    root_at = (HUB_CORE, 0)

    def column(at_z, at_core):
        return (x_lo * n_column + 2 * at_z + at_core, gz)

    n_y = n_gz // 2

    sheet_at = x_lo * n_gz + gz

    def sheet(lo, hi, at_y, at_core):
        return (lo * n_column + 2 * z + at_core, hi * n_y + at_y)

    around = [
        (lo, hi, k, c)
        for half in range(2)
        for lo, hi in ((0, 0), (1, 0), (1, 1), (0, 1))
        for k in reversed(range(half * n_y // 2, (half + 1) * n_y // 2))
        for c in (1 - HUB_CORE, HUB_CORE)
    ]

    def each_of(offsets, act):
        for lo, hi, k, c in offsets:
            if c != HUB_CORE:
                act(sheet(lo, hi, k, c))
            else:

                @pl.when(sheet_at != lo * n_gz + hi * n_y + k)
                def _():
                    act(sheet(lo, hi, k, c))

    to_hubs = [o for o in around if o[3] == HUB_CORE]
    column_hubs = [(k, HUB_CORE) for k in range(n_z // 2)]
    fourth = [(k, c) for k in range(3 * n_z // 4, n_z) for c in range(2)]
    third = [(k, c) for k in range(n_z // 2, 3 * n_z // 4) for c in range(2)]

    barrier = pltpu.get_barrier_semaphore()

    def greet(target):
        pl.semaphore_signal(barrier, inc=1, device_id=target, device_id_type=MESH)

    def neighbour(dx, dz):
        return (lax.rem(gx + dx + n_gx, n_gx), lax.rem(gz + dz + n_gz, n_gz))

    for dx, dz in NEIGHBOURS:
        greet(neighbour(dx, dz))

    loads = [
        pltpu.make_async_copy(source, target, in_sem.at[k])
        for source, target, k in (
            (checkpoint, cp, 0),
            (porosity, por, 0),
            (node_type, kind, 0),
            (inlet_index, feed, 0),
            (inlet_conc, conc, 1),
            (adjoint_end, ae, 2),
        )
    ]
    for load in loads:
        load.start()

    @pl.when(upper)
    def _():
        greet(column(n_z // 2 - jnp.where(z < 3 * n_z // 4, 1, 2), HUB_CORE))

    @pl.when(lower_only)
    def _():
        for offset in to_hubs:
            greet(sheet(*offset))

    @pl.when(jnp.logical_and(hub, not_root))
    def _():
        each_of(to_hubs, greet)

    @pl.when(hub)
    def _():
        greet(column(z, 1 - HUB_CORE))
        for k in range(1, n_z):
            for c in range(2):
                greet(column(lax.rem(z + k, n_z), c))

    @pl.when(root)
    def _():
        @pl.loop(0, n_gx)
        def _(k):
            to_gx = lax.rem(k, 2) * n_column + n_column - 1 - k // 2
            for to_gz in range(n_gz):
                if to_gz:
                    greet((to_gx, to_gz))
                else:

                    @pl.when(to_gx != HUB_CORE)
                    def _():
                        greet((to_gx, to_gz))

    loaded = forward[0].at[pl.ds(0, CH + 3), pl.ds(0, PLANES)]
    pltpu.make_async_copy(loaded, loaded, in_sem.at[0]).wait()
    loads[4].wait()

    def start_plane(x, carry):
        level = jnp.where(feed[x] == 0, conc[0], jnp.where(feed[x] == 1, conc[1], 0.0))
        post, slope = collide([cp[i, x] for i in range(CH)], por[x], kind[x], level)
        FORWARD.put(forward, x, 0, post)
        FORWARD.put(forward, x, 1, slope)
        return carry

    lax.fori_loop(0, PLANES, start_plane, 0, unroll=True)
    loads[5].wait()

    def end_plane(x, carry):
        FORWARD.put(forward, x, 2, [ae[i, x] for i in OPPOSITE])
        return carry

    lax.fori_loop(0, PLANES, end_plane, 0, unroll=True)

    hub_sends = len(column_hubs) - 1 + len(around) - 1
    awaited = len(NEIGHBOURS) + jnp.where(hub, hub_sends, len(column_hubs))
    awaited += jnp.where(root, 0, 1) - jnp.where(jnp.logical_and(jnp.logical_and(hub, z == 0), not_root), 1, 0)
    awaited += jnp.where(next_hub, len(fourth), 0) + jnp.where(last_hub, len(third), 0)
    pl.semaphore_wait(barrier, awaited)
    for copy in FORWARD.copies(forward, gx, gz, n_gx, n_gz):
        copy.start()
    def mid_plane(x, total):
        state = FORWARD.get(forward, x, 0)
        slope = FORWARD.get(forward, x, 1)
        mirrored = FORWARD.get(forward, x, 2)
        carried = [mirrored[i] for i in OPPOSITE]
        adjoint, sens_mid = transposed(state, carried, por[x], kind[x])
        sens[x] = sens_mid
        BACKWARD.put(back, x, 0, adjoint)
        sums = [a * b for a, b in zip(adjoint, slope)] + [sens_mid, total]
        while len(sums) > 1:
            sums = [a + b for a, b in zip(sums[::2], sums[1::2])] + sums[len(sums) & ~1 :]
        return sums[0]

    def wait_for(semaphore, got, count):
        pltpu.make_async_copy(got.at[pl.ds(0, count)], got.at[pl.ds(0, count)], semaphore).wait()

    wait_for(forward[4].at[0], got_r, FORWARD.rows_over_z)
    total = jnp.zeros((ROWS, LANES), F32)
    total = lax.fori_loop(0, PLANES - 2, lambda k, t: mid_plane(k + 1, t), total, unroll=True)
    wait_for(forward[4].at[1], got_r, FORWARD.rows_over_x)
    total = lax.fori_loop(0, 2, lambda k, t: mid_plane(k * (PLANES - 1), t), total, unroll=True)

    def reduce_copy(stage, mine, got, slot, target):
        return pltpu.make_async_remote_copy(
            src_ref=mine,
            dst_ref=got.at[slot],
            send_sem=red_send.at[0],
            recv_sem=red_recv.at[min(stage, 1)],
            device_id=target,
            device_id_type=MESH,
        )

    def in_order(terms):
        sum_of = terms[0]
        for term in terms[1:]:
            sum_of = sum_of + term
        return sum_of

    mine_a[...] = jnp.sum(total, axis=0, keepdims=True)

    @pl.when(not_root)
    def _():
        reduce_copy(3, mine_a, got_r, pl.ds(column_at * n_sheet + sheet_at, 1), root_at).start()

    for k, c in column_hubs:

        @pl.when(jnp.logical_not(jnp.logical_and(hub, z == k)))
        def _():
            reduce_copy(0, mine_a, got_a, column_at, column(k, c)).start()

    for copy in BACKWARD.copies(back, gx, gz, n_gx, n_gz):
        copy.start()

    def send_sheet(target):
        reduce_copy(1, mine_b, got_b, pl.ds(sheet_at, 1), target).start()

    def send_unless_root(target):
        @pl.when(jnp.logical_or(target[0] != HUB_CORE, target[1] != 0))
        def _():
            send_sheet(target)

    @pl.when(hub)
    def _():
        wait_for(red_recv.at[0], got_a, n_column - 1)
        got_a[column_at] = mine_a[...]
        mine_b[...] = in_order([got_a[k] for k in range(n_column)])
        may_be_root = [(0, 0, 0, HUB_CORE)]
        each_of([o for o in around if o not in may_be_root], send_sheet)
        each_of(may_be_root, send_unless_root)
        got_b[pl.ds(sheet_at, 1), :] = mine_b[...]

    wait_for(back[4].at[0], got_r, BACKWARD.rows_over_z)
    wait_for(back[4].at[1], got_r, BACKWARD.rows_over_x)

    def last_plane(x, carry):
        state = [cp[i, x] for i in range(CH)]
        carried = BACKWARD.get(back, x, 0)
        adjoint, sens_start = transposed(state, carried, por[x], kind[x])
        for i in range(CH):
            out_ref[i, x] = adjoint[i]
        grad_ref[x] = sens_start + sens[x]
        return carry

    lax.fori_loop(0, PLANES, last_plane, 0, unroll=True)

    wait_for(forward[3].at[0], got_r, FORWARD.rows_over_z + FORWARD.rows_over_x)
    wait_for(back[3].at[0], got_r, BACKWARD.rows_over_z + BACKWARD.rows_over_x)

    @pl.when(jnp.logical_and(hub, not_root))
    def _():
        wait_for(red_recv.at[1], got_b, n_sheet - 1)

    @pl.when(lower_only)
    def _():
        wait_for(red_recv.at[1], got_b, n_sheet)

    @pl.when(jnp.logical_and(lower, not_root))
    def _():
        total_row[...] = jnp.sum(got_b[...], axis=0, keepdims=True)
        sum_ref[...] = total_row[...]

    @pl.when(root)
    def _():
        wait_for(red_recv.at[1], got_r, n_column * n_sheet - 1)
        got_r[pl.ds(HUB_CORE * n_sheet, 1), :] = mine_a[...]
        sheet_sums = in_order([got_r[pl.ds(k * n_sheet, n_sheet), :] for k in range(n_column)])
        total_row[...] = jnp.sum(sheet_sums, axis=0, keepdims=True)
        sum_ref[...] = total_row[...]

    for is_hub, targets in ((next_hub, fourth), (last_hub, third)):

        @pl.when(is_hub)
        def _():
            for k, c in targets:
                reduce_copy(2, total_row, got_c, 0, column(k, c)).start()

    @pl.when(upper)
    def _():
        wait_for(red_recv.at[1], got_c, 1)
        sum_ref[...] = got_c[0]

    hub_rows = len(column_hubs) - 1 + len(around) - 1
    for kind_of, rows_sent in (
        (jnp.logical_not(hub), len(column_hubs) + 1),
        (jnp.logical_and(hub, z == 0), hub_rows),
        (next_hub, hub_rows + 1 + len(fourth)),
        (last_hub, hub_rows + 1 + len(third)),
        (jnp.logical_and(hub, jnp.logical_and(z > 0, z < n_z // 2 - 2)), hub_rows + 1),
    ):

        @pl.when(kind_of)
        def _():
            wait_for(red_send.at[0], got_r, rows_sent)


def finish(adjoint, grad, row, out_ref, grad_ref, total_ref, held, sems):
    copies = [
        pltpu.make_async_copy(adjoint, out_ref, sems.at[0]),
        pltpu.make_async_copy(grad, grad_ref, sems.at[1]),
        pltpu.make_async_copy(held, total_ref, sems.at[2]),
    ]
    copies[0].start()
    copies[1].start()
    held[...] = jnp.sum(row[...], axis=1, keepdims=True)
    copies[2].start()
    for copy in copies:
        copy.wait()


def solution(mesh):
    n_gx, n_gz = mesh.shape["gx"], mesh.shape["gz"]
    block = (PLANES, ROWS, LANES)
    any_space = pl.BlockSpec(memory_space=pl.ANY)
    in_vmem = pl.BlockSpec(memory_space=pltpu.VMEM)

    def on_device(*args):
        args = [pltpu.with_memory_space_constraint(a, pltpu.HBM) for a in args]
        held = pl.pallas_call(
            lambda *refs: kernel(n_gx, n_gz, *refs),
            out_shape=(
                pltpu.VMEM((CH,) + block, F32),
                pltpu.VMEM(block, F32),
                pltpu.VMEM((1, LANES), F32),
            ),
            in_specs=[any_space] * 6,
            out_specs=(in_vmem, in_vmem, in_vmem),
            scratch_shapes=[
                pltpu.VMEM((CH,) + block, F32),
                pltpu.VMEM((CH,) + block, F32),
                pltpu.VMEM(block, F32),
                pltpu.VMEM(block, jnp.int32),
                pltpu.VMEM(block, jnp.int32),
                pltpu.SMEM((2,), F32),
                pltpu.VMEM(block, F32),
                pltpu.SemaphoreType.DMA((3,)),
            ]
            + FORWARD.scratch()
            + BACKWARD.scratch()
            + [
                pltpu.VMEM((1, LANES), F32),
                pltpu.VMEM((n_gx // 2, 1, LANES), F32),
                pltpu.VMEM((1, LANES), F32),
                pltpu.VMEM((2 * n_gz, LANES), F32),
                pltpu.VMEM((1, LANES), F32),
                pltpu.VMEM((1, 1, LANES), F32),
                pltpu.VMEM((n_gx * n_gz, LANES), F32),
                pltpu.SemaphoreType.DMA((1,)),
                pltpu.SemaphoreType.DMA((2,)),
            ],
            compiler_params=pltpu.CompilerParams(
                collective_id=0, has_side_effects=True, vmem_limit_bytes=32 * 1024 * 1024
            ),
        )(*args)
        held = [pltpu.with_memory_space_constraint(a, pltpu.VMEM) for a in held]
        adjoint, grad, total = pl.pallas_call(
            finish,
            out_shape=(
                jax.ShapeDtypeStruct((CH,) + block, F32),
                jax.ShapeDtypeStruct(block, F32),
                jax.ShapeDtypeStruct((1, 1), F32),
            ),
            in_specs=[in_vmem, in_vmem, in_vmem],
            out_specs=(any_space, any_space, any_space),
            scratch_shapes=[pltpu.VMEM((1, 1), F32), pltpu.SemaphoreType.DMA((3,))],
        )(*held)
        return adjoint, grad, total.reshape(())

    return jax.shard_map(
        on_device,
        mesh=mesh,
        in_specs=(
            P(None, "gx", "gz", None),
            P(None, "gx", "gz", None),
            P("gx", "gz", None),
            P("gx", "gz", None),
            P("gx", "gz", None),
            P(),
        ),
        out_specs=(P(None, "gx", "gz", None), P("gx", "gz", None), P()),
        check_vma=False,
    )
```

```python
import jax
import jax.numpy as jnp
from jax import lax
from jax.experimental import pallas as pl
from jax.experimental.pallas import tpu as pltpu
from jax.sharding import PartitionSpec as P

MESH = pl.DeviceIdType.MESH
F32 = jnp.float32

VEL = [
    (0, 0, 0),
    (1, 0, 0),
    (-1, 0, 0),
    (0, 1, 0),
    (0, -1, 0),
    (0, 0, 1),
    (0, 0, -1),
    (1, 1, 0),
    (-1, -1, 0),
    (1, -1, 0),
    (-1, 1, 0),
    (1, 0, 1),
    (-1, 0, -1),
    (1, 0, -1),
    (-1, 0, 1),
    (0, 1, 1),
    (0, -1, -1),
    (0, 1, -1),
    (0, -1, 1),
]
VEL = VEL + VEL[:7]
CH = 26
PLANES = 4
ROWS = 8
LANES = 128

NEIGHBOURS = ((1, 0), (-1, 0), (1, 1), (1, -1), (-1, 1), (-1, -1), (0, 1), (0, -1))

HUB_CORE = 1

BRINKMAN = 4.0
SPEED = 0.05
RATE_H = 1.0 / 0.7
RATE_E = 1.5

E_NORM = 2394.0
FLUID_P, FLUID_Q = -0.2, -0.1
K_MEAN = 1.4 / 19.0
K_E = (1.4 - 1.19) / E_NORM
K_N = 0.15 / 18.0
K_D = 0.15 / 4.0
K_J = 0.2 / 10.0
K_Q = 0.78 / 8.0


def moments(f):
    e = [f[a] + f[a + 1] for a in range(1, 19, 2)]
    o = [f[a] - f[a + 1] for a in range(1, 19, 2)]
    sxy, txy = o[3] + o[4], o[3] - o[4]
    sxz, txz = o[5] + o[6], o[5] - o[6]
    syz, tyz = o[7] + o[8], o[7] - o[8]
    exy, dxy = e[3] + e[4], e[3] - e[4]
    exz, dxz = e[5] + e[6], e[5] - e[6]
    eyz, dyz = e[7] + e[8], e[7] - e[8]
    axis_sum = e[0] + e[1] + e[2]
    diag_sum = exy + exz + eyz
    return dict(
        e=e,
        o=o,
        f0=f[0],
        axis=axis_sum,
        diag=diag_sum,
        across=(eyz, exz, exy),
        cross=(dxy, dxz, dyz),
        j=(o[0] + sxy + sxz, o[1] + txy + syz, o[2] + txz + tyz),
        q=(sxy - sxz, syz - txy, txz - tyz),
    )


def density_velocity(m):
    r = m["f0"] + m["axis"] + m["diag"]
    inverse = 1.0 / r
    return r, inverse, [j * inverse for j in m["j"]]


def second_order(m):
    shift = m["axis"] - m["diag"]
    return [3.0 * (m["e"][a] - m["across"][a]) - shift for a in range(3)]


def assemble(even_rest, even_axis, even_diag, cross, odd_axis, odd_diag, third, pe, po, m):
    out = [even_rest]
    for a in range(3):
        even = pe * m["e"][a] + even_axis[a]
        odd = po * m["o"][a] + odd_axis[a]
        out += [even + odd, even - odd]
    x, y, z = odd_diag
    qx, qy, qz = third
    xy_x, xy_y = x + qx, y - qy
    xz_x, xz_z = x - qx, z + qz
    yz_y, yz_z = y + qy, z - qz
    odds = [xy_x + xy_y, xy_x - xy_y, xz_x + xz_z, xz_x - xz_z, yz_y + yz_z, yz_y - yz_z]
    for k in range(6):
        base = even_diag[2 - k // 2]
        base = base + cross[k // 2] if k % 2 == 0 else base - cross[k // 2]
        even = pe * m["e"][3 + k] + base
        odd = po * m["o"][3 + k] + odds[k]
        out += [even + odd, even - odd]
    return out


def cell_kinds(kind):
    return kind == 0, kind == 1, kind == 2, kind == 3


def relax_factors(kind):
    fluid, solid, _, _ = cell_kinds(kind)
    pe = jnp.where(fluid, FLUID_P, jnp.where(solid, 0.5, 0.0))
    po = jnp.where(fluid, FLUID_Q, jnp.where(solid, -0.5, 0.0))
    he = jnp.where(fluid, 0.5 - RATE_E / 2, jnp.where(solid, 0.5, 0.0))
    ho = jnp.where(fluid, 0.5 - RATE_H / 2, jnp.where(solid, -0.5, 0.0))
    return pe, po, he, ho


def damping_of(porosity):
    return 1.0 / (1.0 + BRINKMAN * (1.0 - porosity))


def dot3(a, b):
    return a[0] * b[0] + a[1] * b[1] + a[2] * b[2]


def collide(pops, porosity, kind, level):
    fluid, solid, inlet, outlet = cell_kinds(kind)
    pe, po, he, ho = relax_factors(kind)
    f, h = pops[:19], pops[19:]
    m = moments(f)
    r, _, u = density_velocity(m)
    d = damping_of(porosity)
    d_eff = jnp.where(outlet, 1.0, d)
    b = [c * d_eff for c in u]
    zero = jnp.zeros_like(r)

    def on(value):
        return jnp.where(fluid, value, 0.0)

    def pick(at_fluid, elsewhere):
        return jnp.where(fluid, at_fluid, jnp.where(solid, 0.0, elsewhere))

    re = jnp.where(inlet, 1.0, r)
    be = [
        jnp.where(inlet, SPEED, b[0]),
        jnp.where(inlet, 0.0, b[1]),
        jnp.where(inlet, 0.0, b[2]),
    ]
    rb = [re * c for c in be]
    bb = [p * c for p, c in zip(rb, be)]
    b2 = bb[0] + bb[1] + bb[2]
    crossed = (rb[0] * be[1], rb[0] * be[2], rb[1] * be[2])
    quad_rest = pick(-0.65, -0.5) * b2
    axis_all = pick(-0.09, -1.0 / 12.0) * b2
    axis_own = pick(0.325, 0.25)
    quad_axis = [axis_all + axis_own * c for c in bb]
    diag_all = pick(0.095, 1.0 / 12.0) * b2
    diag_own = pick(-0.15, -0.125)
    quad_diag = [diag_all + diag_own * c for c in bb]
    cross_own = pick(0.3125, 0.25)
    quad_cross = [cross_own * c for c in crossed]
    lin_axis_own = pick(0.18, 1.0 / 6.0)
    lin_diag_own = pick(0.08, 1.0 / 12.0)
    lin_axis = [lin_axis_own * c for c in rb]
    lin_diag = [lin_diag_own * c for c in rb]
    n = second_order(m)
    e_f = -30.0 * m["f0"] - 11.0 * m["axis"] + 8.0 * m["diag"]
    de = K_E * (e_f + 11.0 * r)
    even_rest = jnp.where(fluid, 1.4 / 3.0 * r - 30.0 * de, pick(0.0, 1.0 / 3.0) * re)
    even_axis = jnp.where(fluid, 1.4 / 18.0 * r - 11.0 * de, pick(0.0, 1.0 / 18.0) * re)
    even_diag = jnp.where(fluid, 1.4 / 36.0 * r + 8.0 * de, pick(0.0, 1.0 / 36.0) * re)
    rest_own = jnp.where(fluid, -0.4, jnp.where(solid, 1.0, 0.0))
    n_own = on(K_N)
    n = [n_own * c for c in n]
    d_own = on(K_D)
    j_own = on(K_J)
    q_own = on(-K_Q)
    jj = [j_own * c for c in m["j"]]
    new_f = assemble(
        rest_own * m["f0"] + even_rest + quad_rest,
        [even_axis + quad_axis[a] + n[a] for a in range(3)],
        [even_diag + quad_diag[a] - n[a] for a in range(3)],
        [quad_cross[k] + d_own * m["cross"][k] for k in range(3)],
        [lin_axis[a] + jj[a] for a in range(3)],
        [lin_diag[a] + jj[a] for a in range(3)],
        [q_own * c for c in m["q"]],
        pe,
        po,
        m,
    )
    kappa = on(BRINKMAN * d)
    kappa2 = kappa + kappa
    g_rest = kappa2 * quad_rest
    g_axis = [kappa2 * c for c in quad_axis]
    g_diag = [kappa2 * c for c in quad_diag]
    g_cross = [kappa2 * c for c in quad_cross]
    g_la = [kappa * c for c in lin_axis]
    g_ld = [kappa * c for c in lin_diag]
    g_f = [g_rest]
    for a in range(3):
        g_f += [g_axis[a] + g_la[a], g_axis[a] - g_la[a]]
    x, y, z = g_ld
    odds = [x + y, x - y, x + z, x - z, y + z, y - z]
    for k in range(6):
        even = g_diag[2 - k // 2]
        even = even + g_cross[k // 2] if k % 2 == 0 else even - g_cross[k // 2]
        g_f += [even + odds[k], even - odds[k]]
    he_pairs = [h[a] + h[a + 1] for a in (1, 3, 5)]
    ho_pairs = [h[a] - h[a + 1] for a in (1, 3, 5)]
    s = h[0] + he_pairs[0] + he_pairs[1] + he_pairs[2]
    se = jnp.where(inlet, level, s)
    s_even = pick(RATE_E, 1.0) * se
    s_odd = pick(0.5 * RATE_H, 0.5) * se
    new_h = [jnp.where(fluid, 1.0 - RATE_E, jnp.where(solid, 1.0, 0.0)) * h[0] + 0.25 * s_even]
    g_h = [zero]
    for a in range(3):
        even = he * he_pairs[a] + 0.125 * s_even
        push = s_odd * be[a]
        odd = ho * ho_pairs[a] + push
        new_h += [even + odd, even - odd]
        push = kappa * push
        g_h += [push, -push]
    return new_f + new_h, g_f + g_h


def weighted_factors(a, b, own):
    return (
        own[0] - a * K_MEAN + 30.0 * b * K_E,
        own[1] - a * K_MEAN + 11.0 * b * K_E,
        own[2] - a * K_MEAN - 8.0 * b * K_E,
    )


A0_F = weighted_factors(1.0, -11.0, (1.4 / 3.0, 1.4 / 18.0, 1.4 / 36.0))
A2_F = weighted_factors(1.0 / 3.0, 5.0 / 9.0, (0.0, 1.0 / 540.0, 1.4 / 36.0 - 1.0 / 540.0))


def transposed(pops, carried, porosity, kind):
    fluid, solid, inlet, outlet = cell_kinds(kind)
    pe, po, he, ho = relax_factors(kind)
    f, h = pops[:19], pops[19:]
    ms = moments(f)
    r, inverse, u = density_velocity(ms)
    s = h[0] + (h[1] + h[2]) + (h[3] + h[4]) + (h[5] + h[6])
    d = jnp.where(outlet, 1.0, damping_of(porosity))
    b = [c * d for c in u]
    ratio4 = 4.0 * s * inverse

    m = moments(carried[:19])
    mu = carried[19:]
    f0, axis, diag = m["f0"], m["axis"], m["diag"]

    def pick(at_fluid, at_outlet):
        return jnp.where(fluid, at_fluid, at_outlet)

    a0 = (
        pick(A0_F[0], 1.0 / 3.0) * f0
        + pick(A0_F[1], 1.0 / 18.0) * axis
        + pick(A0_F[2], 1.0 / 36.0) * diag
    )
    common = (
        pick(A2_F[0], 0.0) * f0 + pick(A2_F[1], 0.0) * axis + pick(A2_F[2], 1.0 / 36.0) * diag
    )
    own = pick(1.4 / 18.0 - 3.0 / 540.0, 1.0 / 18.0)
    away = pick(-1.4 / 36.0 + 3.0 / 540.0, -1.0 / 36.0)
    a2 = [own * m["e"][a] + away * m["across"][a] + common for a in range(3)]
    cross_own = pick(1.25 / 36.0, 1.0 / 36.0)
    axy, axz, ayz = [cross_own * c for c in m["cross"]]
    o_own = pick(1.0 / 30.0, 1.0 / 36.0)
    j_own = pick(0.96 / 36.0, 1.0 / 36.0)
    a1 = [o_own * m["o"][a] + j_own * m["j"][a] for a in range(3)]
    me = [mu[a] + mu[a + 1] for a in (1, 3, 5)]
    mo = [mu[a] - mu[a + 1] for a in (1, 3, 5)]
    me_sum = me[0] + me[1] + me[2]
    mean_h = (RATE_E / 7.0) * (mu[0] + me_sum)
    b0 = pick(RATE_E, 1.0) * (0.25 * mu[0] + 0.125 * me_sum) - pick(mean_h, 0.0)
    b1_own = pick(0.125 * RATE_H, 0.125)
    b1 = [b1_own * c for c in mo]

    ab = [
        a2[0] * b[0] + axy * b[1] + axz * b[2],
        axy * b[0] + a2[1] * b[1] + ayz * b[2],
        axz * b[0] + ayz * b[1] + a2[2] * b[2],
    ]
    curved = [9.0 * ab[a] - 3.0 * a0 * b[a] for a in range(3)]
    b1b = dot3(b1, b)
    total = [3.0 * a1[a] + curved[a] + ratio4 * b1[a] for a in range(3)]
    to_r = a0 - 0.5 * dot3(b, curved) - ratio4 * b1b
    to_s = b0 + 4.0 * b1b
    sens = jnp.where(fluid, BRINKMAN * d * d * dot3(ms["j"], total), 0.0)

    active = jnp.logical_or(fluid, outlet)
    d_on = jnp.where(active, d, 0.0)
    to_r = jnp.where(active, to_r, 0.0)
    to_s = jnp.where(active, to_s, 0.0)
    to_j = [d_on * c for c in total]

    def on(value):
        return jnp.where(fluid, value, 0.0)

    mean = on(K_MEAN) * (f0 + axis + diag)
    ef = on(K_E) * (-30.0 * f0 - 11.0 * axis + 8.0 * diag)
    base = to_r + mean
    n_own = on(K_N)
    n = [n_own * c for c in second_order(m)]
    d_own = on(K_D)
    jj_own = on(K_J)
    q_own = on(-K_Q)
    odd = [to_j[a] + jj_own * m["j"][a] for a in range(3)]
    rest_own = jnp.where(fluid, -0.4, jnp.where(solid, 1.0, 0.0))
    base_axis = base - 11.0 * ef
    base_diag = base + 8.0 * ef
    out_f = assemble(
        rest_own * f0 + base - 30.0 * ef,
        [base_axis + n[a] for a in range(3)],
        [base_diag - n[a] for a in range(3)],
        [d_own * c for c in m["cross"]],
        odd,
        odd,
        [q_own * c for c in m["q"]],
        pe,
        po,
        m,
    )
    to_s = to_s + on(mean_h)
    out_h = [jnp.where(fluid, 1.0 - RATE_E, jnp.where(solid, 1.0, 0.0)) * mu[0] + to_s]
    for a in range(3):
        even = he * me[a] + to_s
        odd = ho * mo[a]
        out_h += [even + odd, even - odd]
    return out_f + out_h, sens


class Stream:
    def __init__(self, heading, fields):
        self.heading = heading
        self.fields = fields
        self.vel = [tuple(heading * c for c in v) for v in VEL]
        plus = [i for i in range(CH) if self.vel[i][0] == 1]
        minus = [i for i in range(CH) if self.vel[i][0] == -1]
        still = [i for i in range(CH) if self.vel[i][0] == 0]
        order = [(k, i) for group in (plus, minus, still) for k in range(fields) for i in group]
        self.place = {key: at for at, key in enumerate(order)}
        self.face = len(plus) * fields
        self.z_place = {}
        self.edge = {}
        for sign in (1, -1):
            group = [i for i in range(CH) if self.vel[i][2] == sign]
            group.sort(key=lambda i: -abs(self.vel[i][0]))
            keys = [(k, i) for i in group for k in range(fields)]
            self.z_count = len(keys)
            self.rows_over_z = 2 * self.z_count * PLANES
            self.rows_over_x = 2 * self.face * ROWS + 4 * fields
            for at, key in enumerate(keys):
                self.z_place[key] = (0 if sign == 1 else 1, at)
            for at, i in enumerate(group[:2]):
                self.edge[(self.vel[i][0], sign)] = at * fields

    def scratch(self):
        return [
            pltpu.VMEM((CH * self.fields, PLANES + 2, ROWS, LANES), F32),
            pltpu.VMEM((2, self.z_count, PLANES, 1, LANES), F32),
            pltpu.VMEM((2, self.z_count, PLANES + 2, 1, LANES), F32),
            pltpu.SemaphoreType.DMA((1,)),
            pltpu.SemaphoreType.DMA((2,)),
        ]

    def put(self, refs, x, field, values):
        padded, rows = refs[0], refs[1]
        for i, value in enumerate(values):
            _, vy, vz = self.vel[i]
            if vy:
                value = pltpu.roll(value, vy % LANES, 1)
            padded[self.place[(field, i)], x + 1] = value
            if vz:
                side, at = self.z_place[(field, i)]
                row = ROWS - 1 if vz == 1 else 0
                rows[side, at, x] = value[row : row + 1, :]

    def copies(self, refs, gx, gz, n_gx, n_gz):
        padded, rows, halo, send, recv = refs
        found = []
        for dx, dz in NEIGHBOURS:
            target = (lax.rem(gx + dx + n_gx, n_gx), lax.rem(gz + dz + n_gz, n_gz))
            side = 0 if dz == 1 else 1
            if dz == 0:
                start = 0 if dx == 1 else self.face
                source = padded.at[pl.ds(start, self.face), PLANES if dx == 1 else 1]
                landing = padded.at[pl.ds(start, self.face), 0 if dx == 1 else PLANES + 1]
            elif dx == 0:
                source = rows.at[side]
                landing = halo.at[side, :, pl.ds(1, PLANES)]
            else:
                start = self.edge[(dx, dz)]
                source = rows.at[side, pl.ds(start, self.fields), PLANES - 1 if dx == 1 else 0]
                landing = halo.at[side, pl.ds(start, self.fields), 0 if dx == 1 else PLANES + 1]
            found.append(
                pltpu.make_async_remote_copy(
                    src_ref=source,
                    dst_ref=landing,
                    send_sem=send.at[0],
                    recv_sem=recv.at[0 if dx == 0 else 1],
                    device_id=target,
                    device_id_type=MESH,
                )
            )
        return found

    def get(self, refs, x, field):
        padded, halo = refs[0], refs[2]
        row = lax.broadcasted_iota(jnp.int32, (ROWS, LANES), 0)
        values = []
        for i in range(CH):
            vx, _, vz = self.vel[i]
            value = padded[self.place[(field, i)], x + 1 - vx]
            if vz:
                side, at = self.z_place[(field, i)]
                edge = 0 if vz == 1 else ROWS - 1
                value = jnp.where(
                    row == edge, halo[side, at, x + 1 - vx], pltpu.roll(value, vz % ROWS, 0)
                )
            values.append(value)
        return values


OPPOSITE = [VEL.index(tuple(-c for c in v)) for v in VEL[:19]]
OPPOSITE += [19 + k for k in OPPOSITE[:7]]
FORWARD = Stream(1, 3)
BACKWARD = Stream(-1, 1)


def kernel(n_gx, n_gz, *refs):
    (checkpoint, adjoint_end, porosity, node_type, inlet_index, inlet_conc) = refs[:6]
    (out_ref, grad_ref, sum_ref) = refs[6:9]
    (cp, ae, por, kind, feed, conc, sens, in_sem) = refs[9:17]
    forward, back = refs[17:22], refs[22:27]
    (mine_a, got_a, mine_b, got_b, total_row, got_c, got_r, red_send, red_recv) = refs[27:]
    gx, gz = lax.axis_index("gx"), lax.axis_index("gz")
    n_column, n_sheet = n_gx // 2, 2 * n_gz
    x_lo, column_at = gx // n_column, lax.rem(gx, n_column)
    z, core = column_at // 2, lax.rem(column_at, 2)
    x_hi, y = gz // (n_gz // 2), lax.rem(gz, n_gz // 2)

    n_z = n_column // 2
    lower = z < n_z // 2
    upper = jnp.logical_not(lower)
    hub = jnp.logical_and(lower, core == HUB_CORE)
    lower_only = jnp.logical_and(lower, core != HUB_CORE)
    last_hub = jnp.logical_and(hub, z == n_z // 2 - 1)
    next_hub = jnp.logical_and(hub, z == n_z // 2 - 2)

    root = jnp.logical_and(gx == HUB_CORE, gz == 0)
    not_root = jnp.logical_not(root)
    root_at = (HUB_CORE, 0)

    def column(at_z, at_core):
        return (x_lo * n_column + 2 * at_z + at_core, gz)

    n_y = n_gz // 2

    sheet_at = x_lo * n_gz + gz

    def sheet(lo, hi, at_y, at_core):
        return (lo * n_column + 2 * z + at_core, hi * n_y + at_y)

    around = [
        (lo, hi, k, c)
        for half in range(2)
        for lo, hi in ((0, 0), (1, 0), (1, 1), (0, 1))
        for k in reversed(range(half * n_y // 2, (half + 1) * n_y // 2))
        for c in (1 - HUB_CORE, HUB_CORE)
    ]

    def each_of(offsets, act):
        for lo, hi, k, c in offsets:
            if c != HUB_CORE:
                act(sheet(lo, hi, k, c))
            else:

                @pl.when(sheet_at != lo * n_gz + hi * n_y + k)
                def _():
                    act(sheet(lo, hi, k, c))

    to_hubs = [o for o in around if o[3] == HUB_CORE]
    column_hubs = [(k, HUB_CORE) for k in range(n_z // 2)]
    fourth = [(k, c) for k in range(3 * n_z // 4, n_z) for c in range(2)]
    third = [(k, c) for k in range(n_z // 2, 3 * n_z // 4) for c in range(2)]

    barrier = pltpu.get_barrier_semaphore()

    def greet(target):
        pl.semaphore_signal(barrier, inc=1, device_id=target, device_id_type=MESH)

    def neighbour(dx, dz):
        return (lax.rem(gx + dx + n_gx, n_gx), lax.rem(gz + dz + n_gz, n_gz))

    for dx, dz in NEIGHBOURS:
        greet(neighbour(dx, dz))

    loads = [
        pltpu.make_async_copy(source, target, in_sem.at[k])
        for source, target, k in (
            (checkpoint, cp, 0),
            (porosity, por, 0),
            (node_type, kind, 0),
            (inlet_index, feed, 0),
            (inlet_conc, conc, 1),
            (adjoint_end, ae, 2),
        )
    ]
    for load in loads:
        load.start()

    @pl.when(upper)
    def _():
        greet(column(n_z // 2 - jnp.where(z < 3 * n_z // 4, 1, 2), HUB_CORE))

    @pl.when(lower_only)
    def _():
        for offset in to_hubs:
            greet(sheet(*offset))

    @pl.when(jnp.logical_and(hub, not_root))
    def _():
        each_of(to_hubs, greet)

    @pl.when(hub)
    def _():
        greet(column(z, 1 - HUB_CORE))
        for k in range(1, n_z):
            for c in range(2):
                greet(column(lax.rem(z + k, n_z), c))

    @pl.when(root)
    def _():
        @pl.loop(0, n_gx)
        def _(k):
            to_gx = lax.rem(k, 2) * n_column + n_column - 1 - k // 2
            for to_gz in range(n_gz):
                if to_gz:
                    greet((to_gx, to_gz))
                else:

                    @pl.when(to_gx != HUB_CORE)
                    def _():
                        greet((to_gx, to_gz))

    loaded = forward[0].at[pl.ds(0, CH + 3), pl.ds(0, PLANES)]
    pltpu.make_async_copy(loaded, loaded, in_sem.at[0]).wait()
    loads[4].wait()

    def start_plane(x, carry):
        level = jnp.where(feed[x] == 0, conc[0], jnp.where(feed[x] == 1, conc[1], 0.0))
        post, slope = collide([cp[i, x] for i in range(CH)], por[x], kind[x], level)
        FORWARD.put(forward, x, 0, post)
        FORWARD.put(forward, x, 1, slope)
        return carry

    lax.fori_loop(0, PLANES, start_plane, 0, unroll=True)
    loads[5].wait()

    def end_plane(x, carry):
        FORWARD.put(forward, x, 2, [ae[i, x] for i in OPPOSITE])
        return carry

    lax.fori_loop(0, PLANES, end_plane, 0, unroll=True)

    hub_sends = len(column_hubs) - 1 + len(around) - 1
    awaited = len(NEIGHBOURS) + jnp.where(hub, hub_sends, len(column_hubs))
    awaited += jnp.where(root, 0, 1) - jnp.where(jnp.logical_and(jnp.logical_and(hub, z == 0), not_root), 1, 0)
    awaited += jnp.where(next_hub, len(fourth), 0) + jnp.where(last_hub, len(third), 0)
    pl.semaphore_wait(barrier, awaited)
    for copy in FORWARD.copies(forward, gx, gz, n_gx, n_gz):
        copy.start()
    def mid_plane(x, total):
        state = FORWARD.get(forward, x, 0)
        slope = FORWARD.get(forward, x, 1)
        mirrored = FORWARD.get(forward, x, 2)
        carried = [mirrored[i] for i in OPPOSITE]
        adjoint, sens_mid = transposed(state, carried, por[x], kind[x])
        sens[x] = sens_mid
        for i in range(CH):
            ae[i, x] = adjoint[i]
        sums = [a * b for a, b in zip(adjoint, slope)] + [sens_mid, total]
        while len(sums) > 1:
            sums = [a + b for a, b in zip(sums[::2], sums[1::2])] + sums[len(sums) & ~1 :]
        return sums[0]

    def wait_for(semaphore, got, count):
        pltpu.make_async_copy(got.at[pl.ds(0, count)], got.at[pl.ds(0, count)], semaphore).wait()

    wait_for(forward[4].at[0], got_r, FORWARD.rows_over_z)
    total = jnp.zeros((ROWS, LANES), F32)
    total = lax.fori_loop(0, PLANES - 2, lambda k, t: mid_plane(k + 1, t), total, unroll=True)
    wait_for(forward[4].at[1], got_r, FORWARD.rows_over_x)
    total = lax.fori_loop(0, 2, lambda k, t: mid_plane(k * (PLANES - 1), t), total, unroll=True)

    def reduce_copy(stage, mine, got, slot, target):
        return pltpu.make_async_remote_copy(
            src_ref=mine,
            dst_ref=got.at[slot],
            send_sem=red_send.at[0],
            recv_sem=red_recv.at[min(stage, 1)],
            device_id=target,
            device_id_type=MESH,
        )

    def in_order(terms):
        sum_of = terms[0]
        for term in terms[1:]:
            sum_of = sum_of + term
        return sum_of

    mine_a[...] = jnp.sum(total, axis=0, keepdims=True)

    @pl.when(not_root)
    def _():
        reduce_copy(3, mine_a, got_r, pl.ds(column_at * n_sheet + sheet_at, 1), root_at).start()

    for k, c in column_hubs:

        @pl.when(jnp.logical_not(jnp.logical_and(hub, z == k)))
        def _():
            reduce_copy(0, mine_a, got_a, column_at, column(k, c)).start()

    def back_plane(x, carry):
        BACKWARD.put(back, x, 0, [ae[i, x] for i in range(CH)])
        return carry

    lax.fori_loop(0, PLANES, back_plane, 0, unroll=True)
    for copy in BACKWARD.copies(back, gx, gz, n_gx, n_gz):
        copy.start()

    def send_sheet(target):
        reduce_copy(1, mine_b, got_b, pl.ds(sheet_at, 1), target).start()

    def send_unless_root(target):
        @pl.when(jnp.logical_or(target[0] != HUB_CORE, target[1] != 0))
        def _():
            send_sheet(target)

    @pl.when(hub)
    def _():
        wait_for(red_recv.at[0], got_a, n_column - 1)
        got_a[column_at] = mine_a[...]
        mine_b[...] = in_order([got_a[k] for k in range(n_column)])
        may_be_root = [(0, 0, 0, HUB_CORE)]
        each_of([o for o in around if o not in may_be_root], send_sheet)
        each_of(may_be_root, send_unless_root)
        got_b[pl.ds(sheet_at, 1), :] = mine_b[...]

    wait_for(back[4].at[0], got_r, BACKWARD.rows_over_z)
    wait_for(back[4].at[1], got_r, BACKWARD.rows_over_x)

    def last_plane(x, carry):
        state = [cp[i, x] for i in range(CH)]
        carried = BACKWARD.get(back, x, 0)
        adjoint, sens_start = transposed(state, carried, por[x], kind[x])
        for i in range(CH):
            out_ref[i, x] = adjoint[i]
        grad_ref[x] = sens_start + sens[x]
        return carry

    lax.fori_loop(0, PLANES, last_plane, 0, unroll=True)

    wait_for(forward[3].at[0], got_r, FORWARD.rows_over_z + FORWARD.rows_over_x)
    wait_for(back[3].at[0], got_r, BACKWARD.rows_over_z + BACKWARD.rows_over_x)

    @pl.when(jnp.logical_and(hub, not_root))
    def _():
        wait_for(red_recv.at[1], got_b, n_sheet - 1)

    @pl.when(lower_only)
    def _():
        wait_for(red_recv.at[1], got_b, n_sheet)

    @pl.when(jnp.logical_and(lower, not_root))
    def _():
        total_row[...] = jnp.sum(got_b[...], axis=0, keepdims=True)
        sum_ref[...] = total_row[...]

    @pl.when(root)
    def _():
        wait_for(red_recv.at[1], got_r, n_column * n_sheet - 1)
        got_r[pl.ds(HUB_CORE * n_sheet, 1), :] = mine_a[...]
        sheet_sums = in_order([got_r[pl.ds(k * n_sheet, n_sheet), :] for k in range(n_column)])
        total_row[...] = jnp.sum(sheet_sums, axis=0, keepdims=True)
        sum_ref[...] = total_row[...]

    for is_hub, targets in ((next_hub, fourth), (last_hub, third)):

        @pl.when(is_hub)
        def _():
            for k, c in targets:
                reduce_copy(2, total_row, got_c, 0, column(k, c)).start()

    @pl.when(upper)
    def _():
        wait_for(red_recv.at[1], got_c, 1)
        sum_ref[...] = got_c[0]

    hub_rows = len(column_hubs) - 1 + len(around) - 1
    for kind_of, rows_sent in (
        (jnp.logical_not(hub), len(column_hubs) + 1),
        (jnp.logical_and(hub, z == 0), hub_rows),
        (next_hub, hub_rows + 1 + len(fourth)),
        (last_hub, hub_rows + 1 + len(third)),
        (jnp.logical_and(hub, jnp.logical_and(z > 0, z < n_z // 2 - 2)), hub_rows + 1),
    ):

        @pl.when(kind_of)
        def _():
            wait_for(red_send.at[0], got_r, rows_sent)


def finish(adjoint, grad, row, out_ref, grad_ref, total_ref, held, sems):
    copies = [
        pltpu.make_async_copy(adjoint, out_ref, sems.at[0]),
        pltpu.make_async_copy(grad, grad_ref, sems.at[1]),
        pltpu.make_async_copy(held, total_ref, sems.at[2]),
    ]
    copies[0].start()
    copies[1].start()
    held[...] = jnp.sum(row[...], axis=1, keepdims=True)
    copies[2].start()
    for copy in copies:
        copy.wait()


def solution(mesh):
    n_gx, n_gz = mesh.shape["gx"], mesh.shape["gz"]
    block = (PLANES, ROWS, LANES)
    any_space = pl.BlockSpec(memory_space=pl.ANY)
    in_vmem = pl.BlockSpec(memory_space=pltpu.VMEM)

    def on_device(*args):
        args = [pltpu.with_memory_space_constraint(a, pltpu.HBM) for a in args]
        held = pl.pallas_call(
            lambda *refs: kernel(n_gx, n_gz, *refs),
            out_shape=(
                pltpu.VMEM((CH,) + block, F32),
                pltpu.VMEM(block, F32),
                pltpu.VMEM((1, LANES), F32),
            ),
            in_specs=[any_space] * 6,
            out_specs=(in_vmem, in_vmem, in_vmem),
            scratch_shapes=[
                pltpu.VMEM((CH,) + block, F32),
                pltpu.VMEM((CH,) + block, F32),
                pltpu.VMEM(block, F32),
                pltpu.VMEM(block, jnp.int32),
                pltpu.VMEM(block, jnp.int32),
                pltpu.SMEM((2,), F32),
                pltpu.VMEM(block, F32),
                pltpu.SemaphoreType.DMA((3,)),
            ]
            + FORWARD.scratch()
            + BACKWARD.scratch()
            + [
                pltpu.VMEM((1, LANES), F32),
                pltpu.VMEM((n_gx // 2, 1, LANES), F32),
                pltpu.VMEM((1, LANES), F32),
                pltpu.VMEM((2 * n_gz, LANES), F32),
                pltpu.VMEM((1, LANES), F32),
                pltpu.VMEM((1, 1, LANES), F32),
                pltpu.VMEM((n_gx * n_gz, LANES), F32),
                pltpu.SemaphoreType.DMA((1,)),
                pltpu.SemaphoreType.DMA((2,)),
            ],
            compiler_params=pltpu.CompilerParams(
                collective_id=0, has_side_effects=True, vmem_limit_bytes=32 * 1024 * 1024
            ),
        )(*args)
        held = [pltpu.with_memory_space_constraint(a, pltpu.VMEM) for a in held]
        adjoint, grad, total = pl.pallas_call(
            finish,
            out_shape=(
                jax.ShapeDtypeStruct((CH,) + block, F32),
                jax.ShapeDtypeStruct(block, F32),
                jax.ShapeDtypeStruct((1, 1), F32),
            ),
            in_specs=[in_vmem, in_vmem, in_vmem],
            out_specs=(any_space, any_space, any_space),
            scratch_shapes=[pltpu.VMEM((1, 1), F32), pltpu.SemaphoreType.DMA((3,))],
        )(*held)
        return adjoint, grad, total.reshape(())

    return jax.shard_map(
        on_device,
        mesh=mesh,
        in_specs=(
            P(None, "gx", "gz", None),
            P(None, "gx", "gz", None),
            P("gx", "gz", None),
            P("gx", "gz", None),
            P("gx", "gz", None),
            P(),
        ),
        out_specs=(P(None, "gx", "gz", None), P("gx", "gz", None), P()),
        check_vma=False,
    )
```
